32 devices in a mesh: row: 8 (over z, x), col: 4 (over y, core).
Axes of the slice: x: 2, y: 2, z: 4, core: 2. Of those that a mesh axis runs over, the one named last changes fastest.
Arguments:
- tokens: bfloat16 [256, 128, 384], P('row', 'col'), may hold values from -6 to 6
- first_gain: float32 [384], replicated, may hold values from 0.1 to 1.9
- second_gain: float32 [384], replicated, may hold values from 0.1 to 1.9
- joint_weight: bfloat16 [384, 1152], replicated, may hold values from -0.3125 to 0.3125
- merge_weight: bfloat16 [384, 384], replicated, may hold values from -0.3125 to 0.3125
- expand_weight: bfloat16 [384, 1536], replicated, may hold values from -0.3125 to 0.3125
- shrink_weight: bfloat16 [1536, 384], replicated, may hold values from -0.15625 to 0.15625
- relative_bias: float32 [12, 64, 64], replicated, may hold values from -4 to 270
- lateral_weight: bfloat16 [384, 256], replicated, may hold values from -0.3125 to 0.3125
- conv_weight: bfloat16 [4, 2304, 256], replicated, may hold values from -0.125 to 0.125
- mask_weight: bfloat16 [256], replicated, may hold values from -0.375 to 0.375
- box_geometry: int32 [8, 4, 16, 4], P('row', 'col'), may hold values from 0 to 18, as said below
- box_counts: int32 [8, 4], P('row', 'col'), may hold values from 0 to 16, as said below
- box_owner: int32 [8, 4, 16], P('row', 'col'), may hold values from -1 to 7, as said below
- soft_target: bfloat16 [8, 4, 16, 196], P('row', 'col'), may hold values from 0 to 1
Outputs:
- features: bfloat16 [256, 128, 256], P('row', 'col')
- feature_grad: float32 [256, 128, 256], P('row', 'col')
- mask_logits: float32 [8, 4, 8, 196], P('row', 'col')
The draws below stay inside these ranges and needn't reach their ends.
Inputs may be any that keep to these rules, and one draw needn't show every extreme that they name: `box_geometry`: components are top from 0 to 18, left from 0 to 18, height and width from 4 to 14; every slot, used or not, holds such a box. `box_counts`: the counts of one tile column sum to 8 times the tiles along the column; some tile of every column holds exactly 16 boxes. `box_owner`: A slot at or beyond its tile's count holds -1, a used slot an owner in its tile column; every owner is named by exactly 8 boxes of its column, and a tile names one owner at most 2 times, a bound reached by every tile holding 16 boxes.
All inputs are finite; a program needn't handle non-finite values.
Results may differ from the reference program's by a relative error of at most 0.02.
Values may be sent and summed in bfloat16 or wider, within the bound.
No kernel may reach another device: no remote copies, remote signals or barrier semaphores. Data moves between devices by JAX's collectives and lax.ppermute only.
A program may use at most 128 MiB of HBM per device.

```python
import jax
import jax.numpy as jnp
from jax import lax

C = 384
HEADS = 12
FF = 1536
F = 256
HEAD_DIM = 32
WIN = 8
SHIFT = 4
TILE_R = 32
TILE_C = 32
CROP = 14
MIN_SIDE = 4
CONV_LAYERS = 4
BOX_OWN = 8
CAP = 16
TILES_DOWN = 8
TILES_ACROSS = 4
GRID_ROWS = 256
GRID_COLS = 128


def box_plan(key):
    base = jax.random.fold_in(key, 11)
    order_keys = jax.random.split(jax.random.fold_in(base, 1), TILES_ACROSS)
    owner_keys = jax.random.split(jax.random.fold_in(base, 2), TILES_ACROSS)
    tile_order = jax.vmap(lambda single_key: jax.random.permutation(single_key, TILES_DOWN))(order_keys).astype(jnp.int32)
    owner_order = jax.vmap(lambda single_key: jax.random.permutation(single_key, TILES_DOWN))(owner_keys).astype(jnp.int32)
    moved = jax.random.randint(jax.random.fold_in(base, 3), (TILES_ACROSS, TILES_DOWN // 2), 0, BOX_OWN + 1)
    moved = moved.at[:, 0].set(BOX_OWN)
    signs = 2 * jax.random.randint(jax.random.fold_in(base, 4), (TILES_ACROSS, TILES_DOWN // 2), 0, 2) - 1
    paired = jnp.stack([BOX_OWN + signs * moved, BOX_OWN - signs * moved], axis=2).reshape(TILES_ACROSS, TILES_DOWN)
    column_index = jnp.broadcast_to(jnp.arange(TILES_ACROSS, dtype=jnp.int32)[:, None], (TILES_ACROSS, TILES_DOWN))
    counts = jnp.zeros((TILES_ACROSS, TILES_DOWN), jnp.int32).at[column_index, tile_order].set(paired.astype(jnp.int32))
    counts = counts.T
    starts = jnp.cumsum(counts, axis=0) - counts
    slot_range = jnp.arange(CAP, dtype=jnp.int32)
    sequence = (starts[:, :, None] + slot_range[None, None, :]) % TILES_DOWN
    column_grid = jnp.broadcast_to(jnp.arange(TILES_ACROSS, dtype=jnp.int32)[None, :, None], sequence.shape)
    owner = owner_order[column_grid, sequence]
    owner = jnp.where(slot_range[None, None, :] < counts[:, :, None], owner, -1)
    return (counts.astype(jnp.int32), owner.astype(jnp.int32))


def draw_box_counts(key, part):
    return box_plan(key)[0]


def draw_box_owner(key, part):
    return box_plan(key)[1]


def draw_box_geometry(key, part):
    base = jax.random.fold_in(key, 23)
    shape = (TILES_DOWN, TILES_ACROSS, CAP)
    upper = jax.random.randint(jax.random.fold_in(base, 1), shape, 0, TILE_R - CROP + 1)
    leftmost = jax.random.randint(jax.random.fold_in(base, 2), shape, 0, TILE_C - CROP + 1)
    tall = jax.random.randint(jax.random.fold_in(base, 3), shape, MIN_SIDE, CROP + 1)
    broad = jax.random.randint(jax.random.fold_in(base, 4), shape, MIN_SIDE, CROP + 1)
    return jnp.stack([upper, leftmost, tall, broad], axis=-1).astype(jnp.int32)


def draw_relative_bias(key, part):
    base = jax.random.fold_in(key, 37)
    positions = WIN * WIN
    return jnp.clip(jax.random.normal(jax.random.fold_in(base, 6), (HEADS, positions, positions), jnp.float32), -4.0, 4.0)


def block_levels(own_key, dims, cuts, low, largest):
    level = 1.0
    for dim, blocks in cuts:
        heights = jax.random.uniform(jax.random.fold_in(jax.random.fold_in(own_key, 6), dim), (blocks,), jnp.float32, low / len(cuts), largest / len(cuts))
        level = level * jnp.repeat(jnp.exp(heights), dims[dim] // blocks).reshape((-1,) + (1,) * (len(dims) - 1 - dim))
    return level


def scatter_about(stream_key, dims, scale, limit, cuts=(), kind=jnp.bfloat16):
    result = scale * jax.random.normal(stream_key, dims, jnp.float32)
    if cuts:
        result = result * block_levels(stream_key, dims, cuts, -0.22, 0.18)
    return jnp.clip(result, -limit, limit).astype(kind)


def setup_inputs(seed: int = 0) -> dict:
    key_of = jax.random.split(jax.random.key(seed), 16)
    tokens = scatter_about(key_of[0], (GRID_ROWS, GRID_COLS, C), 1.0, 6.0, ((0, 8), (1, 4)))
    first_gain = jnp.clip(1.0 + 0.18 * jax.random.normal(key_of[1], (C,), jnp.float32), 0.1, 1.9)
    second_gain = jnp.clip(1.0 + 0.18 * jax.random.normal(key_of[2], (C,), jnp.float32), 0.1, 1.9)
    joint_weight = scatter_about(key_of[3], (C, 3 * C), C ** -0.5, 0.3125)
    merge_weight = scatter_about(key_of[4], (C, C), C ** -0.5, 0.3125)
    expand_weight = scatter_about(key_of[5], (C, FF), C ** -0.5, 0.3125)
    shrink_weight = scatter_about(key_of[6], (FF, C), FF ** -0.5, 0.15625)
    relative_bias = draw_relative_bias(jax.random.fold_in(key_of[15], 71), 0)
    lateral_weight = scatter_about(key_of[8], (C, F), C ** -0.5, 0.3125)
    conv_weight = scatter_about(key_of[9], (CONV_LAYERS, 9 * F, F), (9 * F) ** -0.5, 0.125)
    mask_weight = scatter_about(key_of[10], (F,), F ** -0.5, 0.375)
    box_geometry = draw_box_geometry(jax.random.fold_in(key_of[15], 71), 0)
    box_counts = draw_box_counts(jax.random.fold_in(key_of[15], 71), 0)
    box_owner = draw_box_owner(jax.random.fold_in(key_of[15], 71), 0)
    soft_target = jnp.clip(1.0 * jax.random.uniform(key_of[14], (TILES_DOWN, TILES_ACROSS, CAP, CROP * CROP), jnp.float32) ** block_levels(key_of[14], (TILES_DOWN, TILES_ACROSS, CAP, CROP * CROP), ((0, 8), (1, 4)), -0.2, 0.2), 0.0, 1.0).astype(jnp.bfloat16)
    return {"tokens": tokens, "first_gain": first_gain, "second_gain": second_gain, "joint_weight": joint_weight, "merge_weight": merge_weight, "expand_weight": expand_weight, "shrink_weight": shrink_weight, "relative_bias": relative_bias, "lateral_weight": lateral_weight, "conv_weight": conv_weight, "mask_weight": mask_weight, "box_geometry": box_geometry, "box_counts": box_counts, "box_owner": box_owner, "soft_target": soft_target}


EPSILON = 1e-05
loss_scale = 128.0

def layer_norm(values, gain):
    values = values.astype(jnp.float32)
    centered = values - lax.optimization_barrier(jnp.mean(values, axis=-1, keepdims=True))
    variance = lax.optimization_barrier(jnp.mean(centered * centered, axis=-1, keepdims=True))
    return centered * lax.rsqrt(variance + EPSILON) * gain

def swin_strip(strip_rows, labels, first_gain, second_gain, joint_weight, merge_weight, expand_weight, shrink_weight, relative_bias):
    width_model = strip_rows.shape[-1]
    windows = strip_rows.shape[1] // WIN
    normed = layer_norm(strip_rows, first_gain).astype(jnp.bfloat16)
    joint = jnp.dot(normed.reshape(-1, width_model), joint_weight, preferred_element_type=jnp.float32).astype(jnp.bfloat16)
    joint = joint.reshape(WIN, windows, WIN, 3, HEADS, HEAD_DIM).transpose(1, 0, 2, 3, 4, 5)
    joint = joint.reshape(windows, WIN * WIN, 3, HEADS, HEAD_DIM)
    window_labels = labels.reshape(WIN, windows, WIN).transpose(1, 0, 2).reshape(windows, WIN * WIN)
    queries = joint[:, :, 0].astype(jnp.float32)
    key_rows = joint[:, :, 1].astype(jnp.float32)
    value_rows = joint[:, :, 2].astype(jnp.float32)
    scores = jnp.einsum('wqhd,wkhd->whqk', queries, key_rows) * HEAD_DIM ** (-0.5) + relative_bias[None]
    allowed = window_labels[:, None, :, None] == window_labels[:, None, None, :]
    scores = jnp.where(allowed, scores, -1000000000.0)
    highest = lax.optimization_barrier(jnp.max(scores, axis=-1, keepdims=True))
    weights = jnp.exp(scores - highest)
    probabilities = (weights / lax.optimization_barrier(jnp.sum(weights, axis=-1, keepdims=True))).astype(jnp.bfloat16)
    mixed = jnp.einsum('whqk,wkhd->wqhd', probabilities.astype(jnp.float32), value_rows).astype(jnp.bfloat16)
    mixed = mixed.reshape(windows, WIN, WIN, width_model).transpose(1, 0, 2, 3).reshape(-1, width_model)
    residual = strip_rows.reshape(-1, width_model).astype(jnp.float32) + jnp.dot(mixed, merge_weight, preferred_element_type=jnp.float32)
    normed_second = layer_norm(residual, second_gain).astype(jnp.bfloat16)
    hidden = jax.nn.gelu(jnp.dot(normed_second, expand_weight, preferred_element_type=jnp.float32)).astype(jnp.bfloat16)
    block_out = (residual + jnp.dot(hidden, shrink_weight, preferred_element_type=jnp.float32)).astype(jnp.bfloat16)
    return block_out.reshape(WIN, -1, width_model)

def conv_forward(activation, kernel):
    padded = jnp.pad(activation, ((0, 0), (1, 1), (1, 1), (0, 0)))
    columns = jnp.concatenate([padded[:, row_off:row_off + CROP, col_off:col_off + CROP, :] for row_off in range(3) for col_off in range(3)], axis=-1)
    product = jnp.dot(columns.reshape(-1, columns.shape[-1]), kernel, preferred_element_type=jnp.float32)
    return product.reshape(activation.shape[0], CROP, CROP, -1)

def conv_backward(grad_before, kernel):
    channels = kernel.shape[-1]
    spread = jnp.dot(grad_before.reshape(-1, channels), kernel.T, preferred_element_type=jnp.float32)
    spread = spread.reshape(grad_before.shape[0], CROP, CROP, 9, channels)
    padded = jnp.pad(spread, ((0, 0), (1, 1), (1, 1), (0, 0), (0, 0)))
    summed = jnp.zeros((grad_before.shape[0], CROP, CROP, channels), jnp.float32)
    for row_off in range(3):
        for col_off in range(3):
            summed = summed + padded[:, 2 - row_off:2 - row_off + CROP, 2 - col_off:2 - col_off + CROP, row_off * 3 + col_off]
    return summed

def mask_head(crops, box_maps, conv_weight, mask_weight):
    activation = crops
    pre_stack = []
    for layer_index in range(conv_weight.shape[0]):
        before = conv_forward(activation, conv_weight[layer_index])
        pre_stack.append(before)
        activation = jax.nn.gelu(before).astype(jnp.bfloat16)
    channels = activation.shape[-1]
    logits = jnp.dot(activation.reshape(-1, channels), mask_weight, preferred_element_type=jnp.float32).reshape(activation.shape[0], -1)
    target = box_maps[:, 0]
    inside = box_maps[:, 1]
    grad_logits = loss_scale * (jax.nn.sigmoid(logits) - target) * inside
    grad_activation = grad_logits.reshape(activation.shape[:3])[..., None] * mask_weight.astype(jnp.float32)
    for layer_index in reversed(range(conv_weight.shape[0])):
        grad_before = jax.vjp(jax.nn.gelu, pre_stack[layer_index])[1](grad_activation)[0].astype(jnp.bfloat16)
        grad_activation = conv_backward(grad_before, conv_weight[layer_index])
    crop_grad = grad_activation * inside.reshape(-1, CROP, CROP)[..., None]
    return (logits, crop_grad)

def reference(tokens, first_gain, second_gain, joint_weight, merge_weight, expand_weight, shrink_weight, relative_bias, lateral_weight, conv_weight, mask_weight, box_geometry, box_counts, box_owner, soft_target):
    grid_rows = tokens.shape[0]
    grid_cols = tokens.shape[1]
    rolled = jnp.roll(tokens, (-SHIFT, -SHIFT), axis=(0, 1))
    col_wrap = (jnp.arange(grid_cols, dtype=jnp.int32) >= grid_cols - SHIFT).astype(jnp.int32)

    def one_strip(strip_index):
        strip_rows = lax.dynamic_slice_in_dim(rolled, strip_index * WIN, WIN, 0)
        row_wrap = (strip_index * WIN + jnp.arange(WIN, dtype=jnp.int32) >= grid_rows - SHIFT).astype(jnp.int32)
        labels = 2 * row_wrap[:, None] + col_wrap[None, :]
        return swin_strip(strip_rows, labels, first_gain, second_gain, joint_weight, merge_weight, expand_weight, shrink_weight, relative_bias)
    strips = lax.map(one_strip, jnp.arange(grid_rows // WIN, dtype=jnp.int32))
    block_out = jnp.roll(strips.reshape(grid_rows, grid_cols, -1), (SHIFT, SHIFT), axis=(0, 1))
    features = jnp.dot(block_out.reshape(-1, block_out.shape[-1]), lateral_weight, preferred_element_type=jnp.float32)
    features = features.astype(jnp.bfloat16).reshape(grid_rows, grid_cols, -1)
    channels = features.shape[-1]
    slot_range = jnp.arange(CAP, dtype=jnp.int32)
    is_valid = slot_range[None, None, :] < box_counts[:, :, None]
    owner_list = jnp.where(is_valid, box_owner, -1)
    column_major = owner_list.transpose(1, 0, 2).reshape(TILES_ACROSS, TILES_DOWN * CAP)
    hits = (column_major[:, :, None] == jnp.arange(TILES_DOWN, dtype=jnp.int32)[None, None, :]).astype(jnp.int32)
    earlier = jnp.cumsum(hits, axis=1) - hits
    position = lax.optimization_barrier(jnp.sum(earlier * hits, axis=2)).astype(jnp.int32)
    flat_ids = (jnp.arange(TILES_DOWN, dtype=jnp.int32)[None, :, None] * TILES_ACROSS + jnp.arange(TILES_ACROSS, dtype=jnp.int32)[:, None, None]) * CAP + slot_range[None, None, :]
    flat_ids = flat_ids.reshape(TILES_ACROSS, TILES_DOWN * CAP).astype(jnp.int32)
    owner_row = jnp.where(column_major >= 0, column_major, TILES_DOWN).astype(jnp.int32)
    column_index = jnp.broadcast_to(jnp.arange(TILES_ACROSS, dtype=jnp.int32)[:, None], owner_row.shape)
    table = jnp.zeros((TILES_DOWN, TILES_ACROSS, BOX_OWN), jnp.int32).at[owner_row, column_index, position].set(flat_ids, mode='drop')
    geometry_flat = box_geometry.reshape(-1, 4)
    targets_flat = soft_target.reshape(-1, CROP * CROP)
    offsets = jnp.arange(CROP, dtype=jnp.int32)

    def box_anchor(box_ids):
        tile_row = box_ids // (TILES_ACROSS * CAP)
        tile_col = box_ids // CAP % TILES_ACROSS
        geometry = geometry_flat[box_ids]
        return ((tile_row * TILE_R + geometry[:, 0]).astype(jnp.int32), (tile_col * TILE_C + geometry[:, 1]).astype(jnp.int32), geometry)

    def one_group(box_ids):
        row_start, col_start, geometry = box_anchor(box_ids)

        def cut(start_row, start_col):
            return lax.dynamic_slice(features, (start_row, start_col, jnp.int32(0)), (CROP, CROP, channels))
        crops = jax.vmap(cut)(row_start, col_start)
        inside = (offsets[None, :, None] < geometry[:, 2, None, None]) & (offsets[None, None, :] < geometry[:, 3, None, None])
        crops = jnp.where(inside[..., None], crops, jnp.zeros((), crops.dtype))
        box_maps = jnp.stack([targets_flat[box_ids].astype(jnp.float32), inside.reshape(-1, CROP * CROP).astype(jnp.float32)], axis=1)
        return mask_head(crops, box_maps, conv_weight, mask_weight)
    logits, crop_grad = lax.map(one_group, table.reshape(TILES_DOWN * TILES_ACROSS, BOX_OWN))
    mask_logits = logits.reshape(TILES_DOWN, TILES_ACROSS, BOX_OWN, CROP * CROP)
    all_ids = table.reshape(-1)
    row_start, col_start, geometry = box_anchor(all_ids)
    row_index = jnp.broadcast_to(row_start[:, None, None] + offsets[None, :, None], (all_ids.shape[0], CROP, CROP))
    col_index = jnp.broadcast_to(col_start[:, None, None] + offsets[None, None, :], (all_ids.shape[0], CROP, CROP))
    feature_grad = jnp.zeros((grid_rows, grid_cols, channels), jnp.float32).at[row_index, col_index].add(crop_grad.reshape(-1, CROP, CROP, channels))
    return (features, feature_grad, mask_logits)
```

```python
import functools
import jax
import jax.numpy as jnp
from jax import lax
from jax.experimental import pallas as pl
from jax.experimental.pallas import tpu as pltpu
from jax.sharding import PartitionSpec as P

CROP = 14
PAD = CROP + 2
GELU_A = 0.7978845608028654
GELU_B = 0.044715
loss_scale = 128.0
NT = (((1,), (1,)), ((), ()))
TN = (((0,), (0,)), ((), ()))


def gelu_parts(x):
    square = x * x
    inner = x * (GELU_A + (GELU_A * GELU_B) * square)
    half = 0.5 + 0.5 * jnp.tanh(inner)
    value = x * half
    slope = half + value * (1.0 - half) * (2.0 * GELU_A + (6.0 * GELU_A * GELU_B) * square)
    return value, slope


def gelu_value(x):
    inner = x * (GELU_A + (GELU_A * GELU_B) * (x * x))
    return x * (0.5 + 0.5 * jnp.tanh(inner))


def clear_border(ref):
    blank = jnp.zeros((PAD,) + ref.shape[2:], ref.dtype)
    ref[0] = blank
    ref[PAD - 1] = blank

    def body(row, carry):
        ref[row, 0] = jnp.zeros(ref.shape[2:], ref.dtype)
        ref[row, PAD - 1] = jnp.zeros(ref.shape[2:], ref.dtype)
        return carry

    lax.fori_loop(1, PAD - 1, body, 0)


def taps_of(ref, row, rows, flip):
    boxes, channels = ref.shape[2:]
    pieces = []
    for s in range(3):
        for t in range(3):
            s0, t0 = (2 - s, 2 - t) if flip else (s, t)
            part = ref[pl.ds(row + s0, rows), t0 : t0 + CROP]
            pieces.append(part.reshape(rows * CROP * boxes, channels))
    return pieces


def mask_forward_kernel(
    rows, geom_ref, count_ref, geomv_ref, features_ref, weight_ref, mask_ref,
    logits_ref, slope_ref, a_ref, b_ref, strip_ref, pick_ref,
):
    boxes, tile_cols, channels = strip_ref.shape
    layers = weight_ref.shape[0]
    clear_border(a_ref)
    clear_border(b_ref)
    lane = lax.broadcasted_iota(jnp.int32, (boxes, boxes * tile_cols), 1)
    sub = lax.broadcasted_iota(jnp.int32, (boxes, boxes * tile_cols), 0)
    mine = (lane // tile_cols == sub) & (sub < count_ref[0])
    away = jnp.where(mine, lane % tile_cols - geomv_ref[:, 1:2], -1)
    away = jnp.where(away < geomv_ref[:, 3:4], away, -1)
    for v in range(CROP):
        pick_ref[v * boxes : (v + 1) * boxes, :] = (away == v).astype(jnp.bfloat16)

    def cut(u, carry):
        for n in range(boxes):
            row = features_ref[geom_ref[n, 0] + u]
            strip_ref[n] = jnp.where(u < geom_ref[n, 2], row, jnp.zeros_like(row))
        crop = jnp.dot(
            pick_ref[...], strip_ref[...].reshape(-1, channels), preferred_element_type=jnp.float32
        )
        a_ref[u + 1, 1 : 1 + CROP] = crop.astype(jnp.bfloat16).reshape(CROP, boxes, channels)
        return carry

    lax.fori_loop(0, CROP, cut, 0)
    steps = CROP // rows
    source, target = a_ref, b_ref
    for layer in range(layers):
        last = layer == layers - 1

        def product(step):
            return jnp.dot(
                jnp.concatenate(taps_of(source, step * rows, rows, False), axis=1),
                weight_ref[layer],
                preferred_element_type=jnp.float32,
            )

        def finish(before, step):
            value, slope = gelu_parts(before)
            value = value.astype(jnp.bfloat16)
            slope_ref[layer, pl.ds(step * rows, rows)] = slope.astype(jnp.bfloat16).reshape(
                rows, CROP * boxes, channels
            )
            if last:
                for r in range(rows):
                    line = value[r * CROP * boxes : (r + 1) * CROP * boxes]
                    logits_ref[pl.ds(step * rows + r, 1), :] = lax.dot_general(
                        mask_ref[...], line, NT, preferred_element_type=jnp.float32
                    )[0:1]
            else:
                target[pl.ds(step * rows + 1, rows), 1 : 1 + CROP] = value.reshape(
                    rows, CROP, boxes, channels
                )

        def body(step, before):
            after = product(step)
            finish(before, step - 1)
            return after

        before = lax.fori_loop(1, steps, body, product(0))
        finish(before, steps - 1)
        source, target = target, source


def mask_backward_kernel(
    rows, geom_ref, count_ref, logits_ref, soft_ref, slope_ref, weight_ref, mask_ref,
    grad_ref, a_ref, b_ref, spread_ref, pick_ref, lead_ref,
):
    boxes, channels = a_ref.shape[2:]
    tile_cols = grad_ref.shape[1]
    layers = weight_ref.shape[0]
    lanes = CROP * boxes
    clear_border(a_ref)
    clear_border(b_ref)
    grad_ref[...] = jnp.zeros_like(grad_ref)
    lane = lax.broadcasted_iota(jnp.int32, (1, lanes), 1)
    box, col = lane % boxes, lane // boxes
    height = jnp.zeros((1, lanes), jnp.int32)
    offset = jnp.zeros((1, lanes), jnp.int32)
    kept = jnp.zeros((1, lanes), jnp.bool_)
    for n in range(boxes):
        here = box == n
        valid = n < count_ref[0]
        height = jnp.where(here, jnp.where(valid, geom_ref[n, 2], 0), height)
        offset = jnp.where(here, jnp.where(valid, geom_ref[n, 1], -tile_cols), offset)
        offset = jnp.where(here & (col >= geom_ref[n, 3]), -tile_cols, offset)
    inside = (lax.broadcasted_iota(jnp.int32, (CROP, lanes), 0) < height) & (offset >= 0)
    for n in range(boxes):
        cell = lax.broadcasted_iota(jnp.int32, (tile_cols, lanes), 0)
        pick_ref[n * tile_cols : (n + 1) * tile_cols, :] = (
            (cell == col + offset) & (box == n)
        ).astype(jnp.bfloat16)
    grad_logits = jnp.where(
        inside, loss_scale * (jax.nn.sigmoid(logits_ref[...]) - soft_ref[...]), 0.0
    )
    high = grad_logits.astype(jnp.bfloat16).astype(jnp.float32)
    lead_ref[0] = high
    lead_ref[1] = grad_logits - high

    def top(u, carry):
        pair = jnp.concatenate(
            [lead_ref[0, pl.ds(u, 1)], lead_ref[1, pl.ds(u, 1)], jnp.zeros((6, lanes), jnp.float32)],
            axis=0,
        ).astype(jnp.bfloat16)
        grad = lax.dot_general(pair, mask_ref[...], TN, preferred_element_type=jnp.float32)
        grad = grad * slope_ref[layers - 1, u].astype(jnp.float32)
        a_ref[u + 1, 1 : 1 + CROP] = grad.astype(jnp.bfloat16).reshape(CROP, boxes, channels)
        return carry

    lax.fori_loop(0, CROP, top, 0)
    steps = CROP // rows
    source, target = a_ref, b_ref
    for layer in reversed(range(layers)):

        def product(step):
            total = None
            for tap, piece in enumerate(taps_of(source, step * rows, rows, True)):
                part = lax.dot_general(
                    piece,
                    weight_ref[layer, tap * channels : (tap + 1) * channels, :],
                    NT,
                    preferred_element_type=jnp.float32,
                )
                total = part if total is None else total + part
            return total

        def finish(grad, step):
            if layer > 0:
                slope = slope_ref[layer - 1, pl.ds(step * rows, rows)].astype(jnp.float32)
                grad = (grad * slope.reshape(-1, channels)).astype(jnp.bfloat16)
                target[pl.ds(step * rows + 1, rows), 1 : 1 + CROP] = grad.reshape(
                    rows, CROP, boxes, channels
                )
                return
            grad = grad.astype(jnp.bfloat16)
            for r in range(rows):
                u = step * rows + r
                spread_ref[...] = jnp.dot(
                    pick_ref[...], grad[r * lanes : (r + 1) * lanes], preferred_element_type=jnp.float32
                )
                for n in range(boxes):
                    row = geom_ref[n, 0] + u
                    part = spread_ref[n * tile_cols : (n + 1) * tile_cols]
                    grad_ref[row] = grad_ref[row] + jnp.where(u < geom_ref[n, 2], part, 0.0)

        def body(step, before):
            after = product(step)
            finish(before, step - 1)
            return after

        before = lax.fori_loop(1, steps, body, product(0))
        finish(before, steps - 1)
        source, target = target, source


VMEM = pl.BlockSpec(memory_space=pltpu.VMEM)
SMEM = pl.BlockSpec(memory_space=pltpu.SMEM)


def mask_forward(features, geometry, count, weight, mask_pad, rows=1):
    tile_rows, tile_cols, channels = features.shape
    boxes = geometry.shape[0]
    layers = weight.shape[0]
    lanes = CROP * boxes
    return pl.pallas_call(
        functools.partial(mask_forward_kernel, rows),
        out_shape=(
            jax.ShapeDtypeStruct((CROP, lanes), jnp.float32),
            jax.ShapeDtypeStruct((layers, CROP, lanes, channels), jnp.bfloat16),
        ),
        in_specs=[SMEM, SMEM, VMEM, VMEM, VMEM, VMEM],
        out_specs=(VMEM, VMEM),
        scratch_shapes=[
            pltpu.VMEM((PAD, PAD, boxes, channels), jnp.bfloat16),
            pltpu.VMEM((PAD, PAD, boxes, channels), jnp.bfloat16),
            pltpu.VMEM((boxes, tile_cols, channels), jnp.bfloat16),
            pltpu.VMEM((lanes, boxes * tile_cols), jnp.bfloat16),
        ],
        compiler_params=pltpu.CompilerParams(vmem_limit_bytes=40 * 2**20),
        name="mask_forward",
    )(geometry, count, geometry, features, weight, mask_pad)


def mask_backward(logits, soft, slope, geometry, count, weight, mask_pad, tile, rows=1):
    layers, _, lanes, channels = slope.shape
    boxes = geometry.shape[0]
    tile_rows, tile_cols = tile
    return pl.pallas_call(
        functools.partial(mask_backward_kernel, rows),
        out_shape=jax.ShapeDtypeStruct((tile_rows, tile_cols, channels), jnp.float32),
        in_specs=[SMEM, SMEM, VMEM, VMEM, VMEM, VMEM, VMEM],
        out_specs=VMEM,
        scratch_shapes=[
            pltpu.VMEM((PAD, PAD, boxes, channels), jnp.bfloat16),
            pltpu.VMEM((PAD, PAD, boxes, channels), jnp.bfloat16),
            pltpu.VMEM((boxes * tile_cols, channels), jnp.float32),
            pltpu.VMEM((boxes * tile_cols, lanes), jnp.bfloat16),
            pltpu.VMEM((2, CROP, lanes), jnp.float32),
        ],
        compiler_params=pltpu.CompilerParams(vmem_limit_bytes=40 * 2**20),
        name="mask_backward",
    )(geometry, count, logits, soft, slope, weight, mask_pad)


HEADS = 12
WIN = 8
SUB = WIN // 2
CELL = SUB * SUB
AREA = WIN * WIN
GROUP = 4
EPSILON = 1e-05
BLOCKED = -1000000000.0
HIGHEST = lax.Precision.HIGHEST


def norm_rows(values, gain):
    centered = values - jnp.mean(values, axis=-1, keepdims=True)
    variance = jnp.mean(centered * centered, axis=-1, keepdims=True)
    return (centered * lax.rsqrt(variance + EPSILON) * gain).astype(jnp.bfloat16)


def one_hot(equal, dtype=jnp.bfloat16):
    return equal.astype(jnp.float32).astype(dtype)


def strip_order(width):
    size = SUB * width
    cell_pos = lax.broadcasted_iota(jnp.int32, (size, size), 0)
    token = lax.broadcasted_iota(jnp.int32, (size, size), 1)
    cell, row, col = cell_pos // CELL, cell_pos // SUB % SUB, cell_pos % SUB
    return one_hot(token == row * width + cell * SUB + col)


def window_order():
    place = lax.broadcasted_iota(jnp.int32, (AREA, AREA), 0)
    token = lax.broadcasted_iota(jnp.int32, (AREA, AREA), 1)
    cell, row, col = place // CELL, place // SUB % SUB, place % SUB
    return one_hot(token == (cell // 2 * SUB + row) * WIN + cell % 2 * SUB + col, jnp.float32)


def head_blocks(lanes):
    row = lax.broadcasted_iota(jnp.int32, (GROUP * AREA, lanes), 0)
    col = lax.broadcasted_iota(jnp.int32, (GROUP * AREA, lanes), 1)
    return one_hot(row // AREA == col // (lanes // GROUP))


def attend(queries, key_rows, value_rows, bias, blocks, key_mask):
    lanes = blocks.shape[1]
    scale = (lanes // GROUP) ** (-0.5)
    first = lax.broadcasted_iota(jnp.int32, (1, 2 * AREA), 1) < AREA
    mixed = []
    for group in range(len(bias)):
        cut = slice(group * lanes, (group + 1) * lanes)
        keys = jnp.concatenate([key_rows[:, cut]] * GROUP, axis=0) * blocks
        values = jnp.concatenate([value_rows[:, cut]] * GROUP, axis=0) * blocks
        scores = lax.dot_general(queries[:, cut], keys, NT, preferred_element_type=jnp.float32)
        scores = scores * scale + bias[group]
        if key_mask is not None:
            scores = scores + key_mask
        weights = []
        for pair in range(GROUP // 2):
            part = scores[:, pair * 2 * AREA : (pair + 1) * 2 * AREA]
            low = jnp.max(jnp.where(first, part, -jnp.inf), axis=-1, keepdims=True)
            high = jnp.max(jnp.where(first, -jnp.inf, part), axis=-1, keepdims=True)
            weights.append(jnp.exp(part - jnp.where(first, low, high)))
        weights = jnp.concatenate(weights, axis=1).astype(jnp.bfloat16)
        both = jnp.dot(
            weights, jnp.concatenate([values, blocks], axis=1), preferred_element_type=jnp.float32
        )
        mixed.append((both[:, :lanes] / both[:, lanes:]).astype(jnp.bfloat16))
    return jnp.concatenate(mixed, axis=1)


def joint_kernel(tokens_ref, gain_ref, joint_ref, relative_ref, out_ref, bias_ref, order_ref):
    width = order_ref.shape[0] // SUB
    strip = SUB * width
    order_ref[...] = strip_order(width)
    place = window_order()
    turned = lax.dot_general(
        relative_ref[...], place, NT, precision=HIGHEST, preferred_element_type=jnp.float32
    )
    for group in range(HEADS // GROUP):
        rows = [
            turned[(group * GROUP + h) * AREA : (group * GROUP + h + 1) * AREA]
            for h in range(GROUP)
        ]
        bias_ref[group] = jnp.dot(
            place,
            jnp.concatenate(rows, axis=1),
            precision=HIGHEST,
            preferred_element_type=jnp.float32,
        )

    def body(step, carry):
        normed = []
        for part in range(2):
            begin = pl.multiple_of((2 * step + part) * strip, strip)
            ordered = jnp.dot(
                order_ref[...], tokens_ref[pl.ds(begin, strip)], preferred_element_type=jnp.float32
            )
            normed.append(norm_rows(ordered, gain_ref[...]))
        normed = jnp.concatenate(normed, axis=0)
        begin = pl.multiple_of(2 * step * strip, 2 * strip)
        out_ref[pl.ds(begin, 2 * strip)] = jnp.dot(
            normed, joint_ref[...], preferred_element_type=jnp.float32
        ).astype(jnp.bfloat16)
        return carry

    lax.fori_loop(0, tokens_ref.shape[0] // (2 * strip), body, 0)


def inner_kernel(joint_ref, bias_ref, out_ref):
    cells_down, cells_across, _, triple = joint_ref.shape
    model = triple // 3
    blocks = head_blocks(GROUP * model // HEADS)
    bias = [bias_ref[group] for group in range(bias_ref.shape[0])]

    def body(i, carry):
        for j in range(cells_across // 2 - 1):
            rows = joint_ref[pl.ds(2 * i + 1, 2), 2 * j + 1 : 2 * j + 3].reshape(AREA, triple)
            mixed = attend(
                rows[:, :model], rows[:, model : 2 * model], rows[:, 2 * model :], bias, blocks, None
            )
            out_ref[pl.ds(2 * i + 1, 2), 2 * j + 1 : 2 * j + 3] = mixed.reshape(2, 2, CELL, model)
        return carry

    lax.fori_loop(0, cells_down // 2 - 1, body, 0)


def outer_kernel(
    edge_ref, tokens_ref, joint_out_ref, inner_ref, up_ref, down_ref, left_ref, right_ref,
    bias_ref, first_ref, second_ref, joint_ref, merge_ref, expand_ref, shrink_ref, lateral_ref,
    features_ref, pairs_ref, mixed_ref, order_ref,
):
    cells_down, cells_across, _, triple = joint_out_ref.shape
    model = triple // 3
    width = cells_across * SUB
    strip = SUB * width
    order_ref[...] = strip_order(width)
    blocks = head_blocks(GROUP * model // HEADS)
    groups = bias_ref.shape[0]
    ends = [
        jnp.dot(order_ref[...], ref[...], preferred_element_type=jnp.float32)
        for ref in (up_ref, down_ref)
    ]
    ends += [ref[...].astype(jnp.float32) for ref in (left_ref, right_ref)]
    halo = norm_rows(jnp.concatenate(ends, axis=0), first_ref[...])
    halo = jnp.dot(halo, joint_ref[:, model:], preferred_element_type=jnp.float32)
    halo = halo.astype(jnp.bfloat16)
    tall = left_ref.shape[0]
    pairs_ref[0, 1:-1] = halo[:strip].reshape(cells_across, CELL, 2 * model)
    pairs_ref[cells_down + 1, 1:-1] = halo[strip : 2 * strip].reshape(cells_across, CELL, 2 * model)
    pairs_ref[:, 0] = halo[2 * strip : 2 * strip + tall].reshape(-1, CELL, 2 * model)
    pairs_ref[:, cells_across + 1] = halo[2 * strip + tall :].reshape(-1, CELL, 2 * model)
    for c in (0, 1, cells_across - 2, cells_across - 1):
        pairs_ref[1:-1, c + 1] = joint_out_ref[:, c, :, model:]
    for r in (0, 1, cells_down - 2, cells_down - 1):
        pairs_ref[r + 1, 1:-1] = joint_out_ref[r, :, :, model:]
    mixed_ref[1:-1, 1:-1] = inner_ref[1:-1, 1:-1]
    key_cell = lax.broadcasted_iota(jnp.int32, (1, GROUP * AREA), 1) // CELL % (2 * 2)
    key_down, key_across = key_cell // 2, key_cell % 2

    def window(i, j, side_down, side_across):
        pairs = pairs_ref[pl.ds(2 * i, 2), pl.ds(2 * j, 2)].reshape(AREA, 2 * model)
        hidden = jnp.zeros((1, GROUP * AREA), jnp.bool_)
        down = [0, 1] if side_down is None else [1 - side_down]
        across = [0, 1] if side_across is None else [1 - side_across]
        if side_down is not None:
            hidden = hidden | ((key_down == side_down) & (edge_ref[side_down] > 0))
        if side_across is not None:
            hidden = hidden | ((key_across == side_across) & (edge_ref[2 + side_across] > 0))
        key_mask = jnp.where(hidden, BLOCKED, 0.0)
        queries, bias_rows = [], []
        for d in down:
            for a in across:
                queries.append(joint_out_ref[2 * i + d - 1, 2 * j + a - 1, :, :model])
                bias_rows.append((2 * d + a) * CELL)
        bias = [
            jnp.concatenate([bias_ref[g, b : b + CELL] for b in bias_rows], axis=0)
            for g in range(groups)
        ]
        mixed = attend(
            jnp.concatenate(queries, axis=0), pairs[:, :model], pairs[:, model:], bias, blocks, key_mask
        )
        place = 0
        for d in down:
            for a in across:
                mixed_ref[2 * i + d - 1, 2 * j + a - 1] = mixed[place : place + CELL]
                place += CELL

    last_down, last_across = cells_down // 2, cells_across // 2
    for side, i in enumerate((0, last_down)):
        for other, j in enumerate((0, last_across)):
            window(i, j, side, other)

    def along(j, carry):
        window(0, j, 0, None)
        window(last_down, j, 1, None)
        return carry

    def beside(i, carry):
        window(i, 0, None, 0)
        window(i, last_across, None, 1)
        return carry

    lax.fori_loop(1, last_across, along, 0)
    lax.fori_loop(1, last_down, beside, 0)

    def body(step, carry):
        tokens = []
        for part in range(2):
            begin = pl.multiple_of((2 * step + part) * strip, strip)
            tokens.append(
                jnp.dot(
                    order_ref[...],
                    tokens_ref[pl.ds(begin, strip)],
                    preferred_element_type=jnp.float32,
                )
            )
        mixed = mixed_ref[pl.ds(2 * step, 2)].reshape(2 * strip, model)
        residual = jnp.concatenate(tokens, axis=0) + jnp.dot(
            mixed, merge_ref[...], preferred_element_type=jnp.float32
        )
        normed = norm_rows(residual, second_ref[...])
        hidden = gelu_value(jnp.dot(normed, expand_ref[...], preferred_element_type=jnp.float32))
        block_out = (
            residual
            + jnp.dot(
                hidden.astype(jnp.bfloat16), shrink_ref[...], preferred_element_type=jnp.float32
            )
        ).astype(jnp.bfloat16)
        features = jnp.dot(block_out, lateral_ref[...], preferred_element_type=jnp.float32)
        features = features.astype(jnp.bfloat16)
        for part in range(2):
            begin = pl.multiple_of((2 * step + part) * strip, strip)
            features_ref[pl.ds(begin, strip)] = lax.dot_general(
                order_ref[...],
                features[part * strip : (part + 1) * strip],
                TN,
                preferred_element_type=jnp.float32,
            ).astype(jnp.bfloat16)
        return carry

    lax.fori_loop(0, cells_down // 2, body, 0)


def params(mebibytes):
    return pltpu.CompilerParams(vmem_limit_bytes=mebibytes * 2**20)


def joint_rows(tokens, gain, weight, relative, width):
    strip = SUB * width
    return pl.pallas_call(
        joint_kernel,
        out_shape=(
            jax.ShapeDtypeStruct((tokens.shape[0], weight.shape[1]), jnp.bfloat16),
            jax.ShapeDtypeStruct((HEADS // GROUP, AREA, GROUP * AREA), jnp.float32),
        ),
        in_specs=[VMEM] * 4,
        out_specs=(VMEM, VMEM),
        scratch_shapes=[pltpu.VMEM((strip, strip), jnp.bfloat16)],
        compiler_params=params(24),
        name="joint_rows",
    )(tokens, gain, weight, relative)


def inner_windows(joint, bias):
    return pl.pallas_call(
        inner_kernel,
        out_shape=jax.ShapeDtypeStruct(joint.shape[:3] + (joint.shape[3] // 3,), jnp.bfloat16),
        in_specs=[VMEM] * 2,
        out_specs=VMEM,
        compiler_params=params(24),
        name="inner_windows",
    )(joint, bias)


def outer_windows(edges, tokens, joint, inner, halos, bias, gains, weights):
    cells_down, cells_across, _, triple = joint.shape
    strip = SUB * SUB * cells_across
    return pl.pallas_call(
        outer_kernel,
        out_shape=jax.ShapeDtypeStruct((tokens.shape[0], weights[-1].shape[1]), jnp.bfloat16),
        in_specs=[SMEM] + [VMEM] * 15,
        out_specs=VMEM,
        scratch_shapes=[
            pltpu.VMEM((cells_down + 2, cells_across + 2, CELL, triple * 2 // 3), jnp.bfloat16),
            pltpu.VMEM((cells_down, cells_across, CELL, triple // 3), jnp.bfloat16),
            pltpu.VMEM((strip, strip), jnp.bfloat16),
        ],
        compiler_params=params(40),
        name="outer_windows",
    )(edges, tokens, joint, inner, *halos, bias, *gains, *weights)


BOX_OWN = 8


def shift(x, axis, step):
    size = lax.axis_size(axis)
    pairs = [(i, i + step) for i in range(size) if 0 <= i + step < size]
    return lax.ppermute(x, axis, pairs)


def shards(
    tokens, first_gain, second_gain, joint_weight, merge_weight, expand_weight, shrink_weight,
    relative_bias, lateral_weight, conv_weight, mask_weight, box_geometry, box_counts, box_owner,
    soft_target,
):
    tile_rows, tile_cols, model = tokens.shape
    cells_down, cells_across = tile_rows // SUB, tile_cols // SUB
    rows_size, cols_size = lax.axis_size("row"), lax.axis_size("col")
    row_index, col_index = lax.axis_index("row"), lax.axis_index("col")
    up = shift(tokens[-SUB:], "row", 1)
    down = shift(tokens[:SUB], "row", -1)
    flat = tokens.reshape(-1, model)
    joint, bias = joint_rows(
        flat, first_gain[None], joint_weight, relative_bias.reshape(-1, AREA), tile_cols
    )
    joint = joint.reshape(cells_down, cells_across, CELL, -1)
    east = jnp.concatenate([up[:, -SUB:], tokens[:, -SUB:], down[:, -SUB:]], axis=0)
    west = jnp.concatenate([up[:, :SUB], tokens[:, :SUB], down[:, :SUB]], axis=0)
    left = shift(east.reshape(-1, model), "col", 1)
    right = shift(west.reshape(-1, model), "col", -1)
    inner = inner_windows(joint, bias)
    edges = jnp.stack(
        [row_index == 0, row_index == rows_size - 1, col_index == 0, col_index == cols_size - 1]
    ).astype(jnp.int32)
    features = outer_windows(
        edges, flat, joint, inner, (up.reshape(-1, model), down.reshape(-1, model), left, right),
        bias, (first_gain[None], second_gain[None]),
        (joint_weight, merge_weight, expand_weight, shrink_weight, lateral_weight),
    )
    features = features.reshape(tile_rows, tile_cols, -1)
    geometry = box_geometry.reshape(-1, 4)
    capacity = geometry.shape[0]
    count = box_counts.reshape(1)
    row8 = lambda *rows: jnp.concatenate(
        [jnp.stack(rows), jnp.zeros((8 - len(rows),) + rows[0].shape, rows[0].dtype)], axis=0
    )
    logits, slope = mask_forward(
        features, geometry, count, conv_weight, row8(mask_weight), rows=2
    )
    soft = soft_target.reshape(capacity, CROP, CROP).transpose(1, 2, 0).astype(jnp.float32)
    feature_grad = mask_backward(
        logits, soft.reshape(CROP, -1), slope, geometry, count, conv_weight,
        row8(mask_weight, mask_weight), (tile_rows, tile_cols), rows=2,
    )
    local = logits.reshape(CROP * CROP, capacity)
    slots = jnp.arange(capacity, dtype=jnp.int32)
    valid = slots < count
    owner = box_owner.reshape(-1)
    rank = jnp.sum((owner[:, None] == owner[None, :]) & (slots[None, :] < slots[:, None]), axis=1)
    each = max(1, capacity // rows_size)
    send = rows_size * each
    routing = (
        (owner * each + rank)[None, :] == jnp.arange(send, dtype=jnp.int32)[:, None]
    ) & valid[None, :]
    packed = jnp.concatenate(
        [local, jnp.ones((1, capacity), jnp.float32)], axis=0
    )
    outgoing = lax.dot_general(
        routing.astype(jnp.float32), packed, NT, precision=HIGHEST
    ).reshape(rows_size, each, -1)
    arriving = lax.all_to_all(outgoing, "row", split_axis=0, concat_axis=0, tiled=True)
    arriving = arriving.reshape(send, -1)
    present = arriving[:, -1] > 0.5
    position = jnp.cumsum(present.astype(jnp.int32)) - 1
    picker = (
        position[None, :] == jnp.arange(BOX_OWN, dtype=jnp.int32)[:, None]
    ) & present[None, :]
    mask_logits = jnp.dot(picker.astype(jnp.float32), arriving[:, :-1], precision=HIGHEST)
    return features, feature_grad, mask_logits.reshape(1, 1, BOX_OWN, -1)


def solution(mesh):
    tile = P("row", "col", None)
    placed = (tile,) + (P(),) * 10 + (
        P("row", "col", None, None), P("row", "col"), tile, P("row", "col", None, None),
    )
    return jax.shard_map(
        shards,
        mesh=mesh,
        in_specs=placed,
        out_specs=(tile, tile, P("row", "col", None, None)),
        check_vma=False,
    )
```

```python
import functools
import jax
import jax.numpy as jnp
from jax import lax
from jax.experimental import pallas as pl
from jax.experimental.pallas import tpu as pltpu
from jax.sharding import PartitionSpec as P

CROP = 14
ROWS = 2
PAD = CROP + 2
GELU_A = 0.7978845608028654
GELU_B = 0.044715
loss_scale = 128.0
NT = (((1,), (1,)), ((), ()))
TN = (((0,), (0,)), ((), ()))
VMEM = pl.BlockSpec(memory_space=pltpu.VMEM)
SMEM = pl.BlockSpec(memory_space=pltpu.SMEM)


def gelu_value(x):
    inner = x * (GELU_A + (GELU_A * GELU_B) * (x * x))
    return x * (0.5 + 0.5 * jnp.tanh(inner))


def gelu_parts(x):
    square = x * x
    inner = x * (GELU_A + (GELU_A * GELU_B) * square)
    half = 0.5 + 0.5 * jnp.tanh(inner)
    value = x * half
    slope = half + value * (1.0 - half) * (2.0 * GELU_A + (6.0 * GELU_A * GELU_B) * square)
    return value, slope


def clear_border(ref):
    blank = jnp.zeros((PAD,) + ref.shape[2:], ref.dtype)
    ref[0] = blank
    ref[PAD - 1] = blank
    for row in range(1, PAD - 1):
        ref[row, 0] = blank[0]
        ref[row, PAD - 1] = blank[0]


def taps_of(ref, begin, end, flip):
    boxes, channels = ref.shape[2:]
    pieces = []
    for s in range(3):
        for t in range(3):
            s0, t0 = (2 - s, 2 - t) if flip else (s, t)
            part = ref[begin + s0 : end + s0, t0 : t0 + CROP]
            pieces.append(part.reshape((end - begin) * CROP * boxes, channels))
    return pieces


def mask_kernel(
    geom_ref, count_ref, features_ref, weight_ref, mask_ref, soft_ref,
    logits_ref, grad_ref,
    a_ref, b_ref, slope_ref, strip_ref, spread_ref, pick_ref, place_ref, before_ref,
):
    _, boxes, tile_cols, channels = strip_ref.shape
    layers = weight_ref.shape[0]
    lanes = CROP * boxes
    count = count_ref[0, 0]
    top = [geom_ref[0, 0, n, 0] for n in range(boxes)]
    left = [geom_ref[0, 0, n, 1] for n in range(boxes)]
    tall = [jnp.where(n < count, geom_ref[0, 0, n, 2], 0) for n in range(boxes)]
    broad = [geom_ref[0, 0, n, 3] for n in range(boxes)]
    clear_border(a_ref)
    clear_border(b_ref)
    lane = lax.broadcasted_iota(jnp.int32, (boxes, boxes * tile_cols), 1)
    sub = lax.broadcasted_iota(jnp.int32, (boxes, boxes * tile_cols), 0)
    start = jnp.zeros((boxes, boxes * tile_cols), jnp.int32)
    width = jnp.zeros((boxes, boxes * tile_cols), jnp.int32)
    for n in range(boxes):
        start = jnp.where(sub == n, left[n], start)
        width = jnp.where(sub == n, broad[n], width)
    away = jnp.where(lane // tile_cols == sub, lane % tile_cols - start, -1)
    away = jnp.where(away < width, away, -1)
    for v in range(CROP):
        pick_ref[v * boxes : (v + 1) * boxes, :] = (away == v).astype(jnp.bfloat16)
    for n in range(boxes):
        rows = features_ref[pl.ds(top[n], CROP)]
        for u in range(CROP):
            strip_ref[u, n] = jnp.where(u < tall[n], rows[u], jnp.zeros_like(rows[u]))
    for u in range(CROP):
        crop = jnp.dot(
            pick_ref[...], strip_ref[u].reshape(-1, channels), preferred_element_type=jnp.float32
        )
        a_ref[u + 1, 1 : 1 + CROP] = crop.astype(jnp.bfloat16).reshape(CROP, boxes, channels)

    lane = lax.broadcasted_iota(jnp.int32, (1, lanes), 1)
    box, col = lane % boxes, lane // boxes
    height = jnp.zeros((1, lanes), jnp.int32)
    for n in range(boxes):
        height = jnp.where((box == n) & (col < broad[n]), tall[n], height)
    cell = lax.broadcasted_iota(jnp.int32, (tile_cols, lanes), 0)
    for n in range(boxes):
        place_ref[n * tile_cols : (n + 1) * tile_cols, :] = (
            (cell == col + left[n]) & (box == n) & (col < broad[n])
        ).astype(jnp.bfloat16)
    vector = jnp.broadcast_to(
        mask_ref[...].astype(jnp.float32).reshape(1, channels), (8, channels)
    ).astype(jnp.bfloat16)

    def forward(layer, source, begin, end):
        return jnp.dot(
            jnp.concatenate(taps_of(source, begin, end, False), axis=1),
            weight_ref[layer],
            preferred_element_type=jnp.float32,
        )

    def activate(layer, before, target, begin, end):
        for u in range(begin, end):
            for v in range(CROP):
                piece = slice(v * boxes, (v + 1) * boxes)
                value, slope = gelu_parts(before[u, piece])
                slope_ref[layer + 1, u, piece] = slope.astype(jnp.bfloat16)
                target[u + 1, 1 + v] = value.astype(jnp.bfloat16)

    def backward(layer, source, begin, end):
        total = None
        for tap, piece in enumerate(taps_of(source, begin, end, True)):
            part = lax.dot_general(
                piece,
                weight_ref[layer, tap * channels : (tap + 1) * channels, :],
                NT,
                preferred_element_type=jnp.float32,
            )
            total = part if total is None else total + part
        return total

    def descend(layer, before, target, begin, end):
        for u in range(begin, end):
            for v in range(CROP):
                piece = slice(v * boxes, (v + 1) * boxes)
                slope = slope_ref[layer, u, piece].astype(jnp.float32)
                target[u + 1, 1 + v] = (before[u, piece] * slope).astype(jnp.bfloat16)

    def chain(product, finish, stages):
        late = None
        for number, (layer, source, target) in enumerate(stages):
            before = before_ref.at[number % 2]
            for begin in range(0, CROP, ROWS):
                end = min(begin + ROWS, CROP)
                before[begin:end] = product(layer, source, begin, end).reshape(
                    end - begin, lanes, channels
                )
                if late is not None:
                    late()
                late = functools.partial(finish, layer, before, target, begin, end)
        late()

    def up(pair, carry):
        chain(forward, activate, [(2 * pair, a_ref, b_ref), (2 * pair + 1, b_ref, a_ref)])
        return carry

    def down(pair, carry):
        layer = layers - 1 - 2 * pair
        chain(backward, descend, [(layer, b_ref, a_ref), (layer - 1, a_ref, b_ref)])
        return carry

    slope_ref[0] = jnp.ones(slope_ref.shape[1:], slope_ref.dtype)
    lax.fori_loop(0, layers // 2, up, 0)
    for u in range(CROP):
        line = lax.dot_general(
            vector, a_ref[u + 1, 1 : 1 + CROP].reshape(lanes, channels), NT,
            preferred_element_type=jnp.float32,
        )[0:1]
        logits_ref[u : u + 1, :] = line
    grad = loss_scale * (jax.nn.sigmoid(logits_ref[...]) - soft_ref[...])
    grad = jnp.where(lax.broadcasted_iota(jnp.int32, (CROP, lanes), 0) < height, grad, 0.0)
    high = grad.astype(jnp.bfloat16).astype(jnp.float32)
    for u in range(CROP):
        pair = jnp.concatenate(
            [high[u : u + 1], (grad - high)[u : u + 1], jnp.zeros((6, lanes), jnp.float32)], axis=0
        )
        lead = lax.dot_general(
            pair.astype(jnp.bfloat16), vector, TN, preferred_element_type=jnp.float32
        )
        b_ref[u + 1, 1 : 1 + CROP] = (
            (lead * slope_ref[layers, u].astype(jnp.float32))
            .astype(jnp.bfloat16)
            .reshape(CROP, boxes, channels)
        )
    lax.fori_loop(0, layers // 2, down, 0)
    for u in range(CROP):
        spread_ref[u] = jnp.dot(
            place_ref[...],
            b_ref[u + 1, 1 : 1 + CROP].reshape(lanes, channels),
            preferred_element_type=jnp.float32,
        ).reshape(boxes, tile_cols, channels)
    grad_ref[...] = jnp.zeros_like(grad_ref)
    for n in range(boxes):
        kept = lax.broadcasted_iota(jnp.int32, (CROP, 1, 1), 0) < tall[n]
        rows = pl.ds(top[n], CROP)
        grad_ref[rows] = grad_ref[rows] + jnp.where(kept, spread_ref[:, n], 0.0)


def mask_head(features, geometry, count, weight, mask, soft):
    tile_rows, tile_cols, channels = features.shape
    boxes = geometry.shape[2]
    layers = weight.shape[0]
    lanes = CROP * boxes
    return pl.pallas_call(
        mask_kernel,
        out_shape=(
            jax.ShapeDtypeStruct((CROP, lanes), jnp.float32),
            jax.ShapeDtypeStruct((tile_rows, tile_cols, channels), jnp.float32),
        ),
        in_specs=[SMEM, SMEM, VMEM, VMEM, VMEM, VMEM],
        out_specs=(VMEM, VMEM),
        scratch_shapes=[
            pltpu.VMEM((PAD, PAD, boxes, channels), jnp.bfloat16),
            pltpu.VMEM((PAD, PAD, boxes, channels), jnp.bfloat16),
            pltpu.VMEM((layers + 1, CROP, lanes, channels), jnp.bfloat16),
            pltpu.VMEM((CROP, boxes, tile_cols, channels), jnp.bfloat16),
            pltpu.VMEM((CROP, boxes, tile_cols, channels), jnp.float32),
            pltpu.VMEM((lanes, boxes * tile_cols), jnp.bfloat16),
            pltpu.VMEM((boxes * tile_cols, lanes), jnp.bfloat16),
            pltpu.VMEM((2, CROP, lanes, channels), jnp.float32),
        ],
        compiler_params=pltpu.CompilerParams(vmem_limit_bytes=48 * 2**20),
        name="mask_head",
    )(geometry, count, features, weight, mask, soft)


HEADS = 12
WIN = 8
SUB = WIN // 2
CELL = SUB * SUB
AREA = WIN * WIN
GROUP = 4
EPSILON = 1e-05
BLOCKED = -1000000000.0
HIGHEST = lax.Precision.HIGHEST


def norm_rows(values, gain):
    centered = values - jnp.mean(values, axis=-1, keepdims=True)
    variance = jnp.mean(centered * centered, axis=-1, keepdims=True)
    return (centered * lax.rsqrt(variance + EPSILON) * gain).astype(jnp.bfloat16)


def one_hot(equal, dtype=jnp.bfloat16):
    return equal.astype(jnp.float32).astype(dtype)


def strip_order(width):
    size = SUB * width
    cell_pos = lax.broadcasted_iota(jnp.int32, (size, size), 0)
    token = lax.broadcasted_iota(jnp.int32, (size, size), 1)
    cell, row, col = cell_pos // CELL, cell_pos // SUB % SUB, cell_pos % SUB
    return one_hot(token == row * width + cell * SUB + col)


def window_order():
    place = lax.broadcasted_iota(jnp.int32, (AREA, AREA), 0)
    token = lax.broadcasted_iota(jnp.int32, (AREA, AREA), 1)
    cell, row, col = place // CELL, place // SUB % SUB, place % SUB
    return one_hot(token == (cell // 2 * SUB + row) * WIN + cell % 2 * SUB + col, jnp.float32)


def head_blocks(lanes):
    row = lax.broadcasted_iota(jnp.int32, (GROUP * AREA, lanes), 0)
    col = lax.broadcasted_iota(jnp.int32, (GROUP * AREA, lanes), 1)
    return one_hot(row // AREA == col // (lanes // GROUP))


def attend(queries, key_rows, value_rows, bias, blocks, key_mask):
    lanes = blocks.shape[1]
    scale = (lanes // GROUP) ** (-0.5)
    first = lax.broadcasted_iota(jnp.int32, (1, 2 * AREA), 1) < AREA
    mixed = []
    for group in range(len(bias)):
        cut = slice(group * lanes, (group + 1) * lanes)
        keys = jnp.concatenate([key_rows[:, cut]] * GROUP, axis=0) * blocks
        values = jnp.concatenate([value_rows[:, cut]] * GROUP, axis=0) * blocks
        scores = lax.dot_general(queries[:, cut], keys, NT, preferred_element_type=jnp.float32)
        scores = scores * scale + bias[group]
        if key_mask is not None:
            scores = scores + key_mask
        weights = []
        for pair in range(GROUP // 2):
            part = scores[:, pair * 2 * AREA : (pair + 1) * 2 * AREA]
            low = jnp.max(jnp.where(first, part, -jnp.inf), axis=-1, keepdims=True)
            high = jnp.max(jnp.where(first, -jnp.inf, part), axis=-1, keepdims=True)
            weights.append(jnp.exp(part - jnp.where(first, low, high)))
        weights = jnp.concatenate(weights, axis=1).astype(jnp.bfloat16)
        both = jnp.dot(
            weights, jnp.concatenate([values, blocks], axis=1), preferred_element_type=jnp.float32
        )
        mixed.append((both[:, :lanes] / both[:, lanes:]).astype(jnp.bfloat16))
    return jnp.concatenate(mixed, axis=1)


def joint_kernel(
    tokens_ref, gain_ref, joint_ref, relative_ref,
    out_ref, bias_ref, ordered_ref, north_ref, south_ref, west_ref, east_ref, order_ref,
):
    cells_down, cells_across, _, model = ordered_ref.shape
    strip = order_ref.shape[0]
    order_ref[...] = strip_order(strip // SUB)
    place = window_order()
    turned = lax.dot_general(
        relative_ref[...].reshape(-1, AREA), place, NT,
        precision=HIGHEST, preferred_element_type=jnp.float32,
    )
    for group in range(HEADS // GROUP):
        rows = [
            turned[(group * GROUP + h) * AREA : (group * GROUP + h + 1) * AREA]
            for h in range(GROUP)
        ]
        bias_ref[group] = jnp.dot(
            place,
            jnp.concatenate(rows, axis=1),
            precision=HIGHEST,
            preferred_element_type=jnp.float32,
        )
    gain = gain_ref[...].reshape(1, model)

    def body(step, carry):
        normed = []
        for part in range(2):
            down = 2 * step + part
            ordered = jnp.dot(
                order_ref[...],
                tokens_ref[pl.ds(down * SUB, SUB)].reshape(strip, model),
                preferred_element_type=jnp.float32,
            )
            ordered_ref[down] = ordered.astype(jnp.bfloat16).reshape(cells_across, CELL, model)
            normed.append(norm_rows(ordered, gain))
        out_ref[pl.ds(2 * step, 2)] = (
            jnp.dot(
                jnp.concatenate(normed, axis=0), joint_ref[...], preferred_element_type=jnp.float32
            )
            .astype(jnp.bfloat16)
            .reshape(2, cells_across, CELL, 3 * model)
        )
        return carry

    lax.fori_loop(0, cells_down // 2, body, 0)
    north_ref[...] = ordered_ref[0]
    south_ref[...] = ordered_ref[cells_down - 1]
    west_ref[...] = ordered_ref[:, 0]
    east_ref[...] = ordered_ref[:, cells_across - 1]


def inner_kernel(joint_ref, bias_ref, out_ref):
    cells_down, cells_across, _, triple = joint_ref.shape
    model = triple // 3
    blocks = head_blocks(GROUP * model // HEADS)
    bias = [bias_ref[group] for group in range(bias_ref.shape[0])]

    def body(i, carry):
        for j in range(cells_across // 2 - 1):
            rows = joint_ref[pl.ds(2 * i + 1, 2), 2 * j + 1 : 2 * j + 3].reshape(AREA, triple)
            mixed = attend(
                rows[:, :model], rows[:, model : 2 * model], rows[:, 2 * model :], bias, blocks, None
            )
            out_ref[pl.ds(2 * i + 1, 2), 2 * j + 1 : 2 * j + 3] = mixed.reshape(2, 2, CELL, model)
        return carry

    lax.fori_loop(0, cells_down // 2 - 1, body, 0)


def hidden_keys(down_side, down_edge, across_side, across_edge):
    cell = lax.broadcasted_iota(jnp.int32, (1, GROUP * AREA), 1) // CELL % 4
    hidden = jnp.zeros((1, GROUP * AREA), jnp.bool_)
    if down_side is not None:
        hidden = hidden | ((cell // 2 == down_side) & down_edge)
    if across_side is not None:
        hidden = hidden | ((cell % 2 == across_side) & across_edge)
    return jnp.where(hidden, BLOCKED, 0.0)


def at_end(axis, side):
    return lax.axis_index(axis) == (lax.axis_size(axis) - 1 if side else 0)


def window_bias(bias_ref, cells):
    return [
        jnp.concatenate([bias_ref[g, c * CELL : (c + 1) * CELL] for c in cells], axis=0)
        for g in range(bias_ref.shape[0])
    ]


def halo_pairs(halo, gain, joint_ref):
    model = halo.shape[-1]
    normed = norm_rows(halo.astype(jnp.float32), gain)
    return jnp.dot(normed, joint_ref[:, model:], preferred_element_type=jnp.float32).astype(
        jnp.bfloat16
    )


def ends_kernel(joint_out_ref, up_ref, down_ref, bias_ref, gain_ref, joint_ref, pairs_ref, out_ref):
    cells_down, cells_across, _, triple = joint_out_ref.shape
    model = triple // 3
    blocks = head_blocks(GROUP * model // HEADS)
    gain = gain_ref[...].reshape(1, model)
    halo = jnp.concatenate([ref[...].reshape(-1, model) for ref in (up_ref, down_ref)], axis=0)
    pairs_ref[...] = halo_pairs(halo, gain, joint_ref).reshape(2, cells_across, CELL, 2 * model)
    for side in range(2):
        row = side * (cells_down - 1)
        bias = window_bias(bias_ref, [2 - 2 * side, 3 - 2 * side])
        key_mask = hidden_keys(side, at_end("row", side), None, None)
        for j in range(1, cells_across // 2):
            cut = slice(2 * j - 1, 2 * j + 1)
            own = joint_out_ref[row, cut].reshape(2 * CELL, triple)
            other = pairs_ref[side, cut].reshape(2 * CELL, 2 * model)
            both = [own[:, model:], other] if side else [other, own[:, model:]]
            both = jnp.concatenate(both, axis=0)
            mixed = attend(own[:, :model], both[:, :model], both[:, model:], bias, blocks, key_mask)
            out_ref[side, cut] = mixed.reshape(2, CELL, model)


def sides_kernel(
    ordered_ref, joint_out_ref, inner_ref, pairs_ref, ends_ref, left_ref, right_ref,
    bias_ref, first_ref, second_ref, joint_ref, merge_ref, expand_ref, shrink_ref, lateral_ref,
    features_ref, mixed_ref, halo_ref, order_ref, residual_ref, normed_ref, wide_ref, hidden_ref,
):
    cells_down, cells_across, _, triple = joint_out_ref.shape
    model = triple // 3
    strip = cells_across * CELL
    order_ref[...] = strip_order(cells_across * SUB)
    blocks = head_blocks(GROUP * model // HEADS)
    halo = jnp.concatenate([ref[...].reshape(-1, model) for ref in (left_ref, right_ref)], axis=0)
    halo = halo_pairs(halo, first_ref[...].reshape(1, model), joint_ref)
    halo_ref[...] = halo.reshape(2, cells_down + 2, CELL, 2 * model)
    mixed_ref[1:-1, 1:-1] = inner_ref[1:-1, 1:-1]
    mixed_ref[0, 1:-1] = ends_ref[0, 1:-1]
    mixed_ref[cells_down - 1, 1:-1] = ends_ref[1, 1:-1]

    for across in range(2):
        col = across * (cells_across - 1)
        bias = window_bias(bias_ref, [1 - across, 3 - across])
        key_mask = hidden_keys(None, None, across, at_end("col", across))

        def keys(pieces):
            rows = []
            for own, other in pieces:
                rows += [own, other] if across else [other, own]
            return jnp.concatenate(rows, axis=0)

        for i in range(1, cells_down // 2):
            cells = [2 * i - 1, 2 * i]
            both = keys(
                [(joint_out_ref[c, col, :, model:], halo_ref[across, c + 1]) for c in cells]
            )
            queries = jnp.concatenate([joint_out_ref[c, col, :, :model] for c in cells], axis=0)
            mixed = attend(queries, both[:, :model], both[:, model:], bias, blocks, key_mask)
            for place, c in enumerate(cells):
                mixed_ref[c, col] = mixed[place * CELL : (place + 1) * CELL]
        for down in range(2):
            row = down * (cells_down - 1)
            near = (joint_out_ref[row, col, :, model:], halo_ref[across, row + 1])
            far = (pairs_ref[down, col], halo_ref[across, down * (cells_down + 1)])
            both = keys([near, far] if down else [far, near])
            mixed_ref[row, col] = attend(
                joint_out_ref[row, col, :, :model], both[:, :model], both[:, model:],
                window_bias(bias_ref, [3 - 2 * down - across]), blocks,
                hidden_keys(down, at_end("row", down), across, at_end("col", across)),
            )

    second = second_ref[...].reshape(1, model)
    rows = hidden_ref.shape[1]
    group = rows // strip
    steps = cells_down // group

    def merge(step):
        residual = residual_ref.at[step % 2]
        cells = slice(step * group, (step + 1) * group)
        residual[...] = jnp.dot(
            mixed_ref[cells].reshape(rows, model), merge_ref[...], preferred_element_type=jnp.float32
        )
        for part in range(0, rows, PART):
            cut = slice(part, part + PART)
            c, a = divmod(part // CELL, cells_across)
            own = ordered_ref[step * group + c, a : a + PART // CELL].reshape(PART, model)
            total = residual[cut] + own.astype(jnp.float32)
            residual[cut] = total
            normed_ref[step % 2, cut] = norm_rows(total, second)

    def expand(step):
        wide_ref[step % 2] = jnp.dot(
            normed_ref[step % 2], expand_ref[...], preferred_element_type=jnp.float32
        )

    def activate(step):
        for part in range(0, rows, CELL):
            cut = slice(part, part + CELL)
            for lane in range(0, wide_ref.shape[2], 512):
                hidden_ref[step % 2, cut, lane : lane + 512] = gelu_value(
                    wide_ref[step % 2, cut, lane : lane + 512]
                ).astype(jnp.bfloat16)

    def shrink(step):
        block_out = residual_ref[step % 2] + jnp.dot(
            hidden_ref[step % 2], shrink_ref[...], preferred_element_type=jnp.float32
        )
        features = jnp.dot(
            block_out.astype(jnp.bfloat16), lateral_ref[...], preferred_element_type=jnp.float32
        ).astype(jnp.bfloat16)
        for part in range(group):
            natural = lax.dot_general(
                order_ref[...], features[part * strip : (part + 1) * strip], TN,
                preferred_element_type=jnp.float32,
            ).astype(jnp.bfloat16)
            first = (step * group + part) * SUB
            features_ref[first : first + SUB] = natural.reshape((SUB,) + features_ref.shape[1:])

    merge(0)
    expand(0)
    for step in range(steps):
        if step + 1 < steps:
            merge(step + 1)
        activate(step)
        if step + 1 < steps:
            expand(step + 1)
        shrink(step)


PART = 64


def params(mebibytes):
    return pltpu.CompilerParams(vmem_limit_bytes=mebibytes * 2**20)


def cells_of(count_down, count_across, channels, dtype=jnp.bfloat16):
    return jax.ShapeDtypeStruct((count_down, count_across, CELL, channels), dtype)


def joint_rows(tokens, gain, weight, relative):
    tile_rows, tile_cols, model = tokens.shape
    down, across = tile_rows // SUB, tile_cols // SUB
    lone = lambda n: jax.ShapeDtypeStruct((n, CELL, model), jnp.bfloat16)
    return pl.pallas_call(
        joint_kernel,
        out_shape=(
            cells_of(down, across, weight.shape[1]),
            jax.ShapeDtypeStruct((HEADS // GROUP, AREA, GROUP * AREA), jnp.float32),
            cells_of(down, across, model),
            lone(across), lone(across), lone(down), lone(down),
        ),
        in_specs=[VMEM] * 4,
        out_specs=(VMEM,) * 7,
        scratch_shapes=[pltpu.VMEM((SUB * tile_cols, SUB * tile_cols), jnp.bfloat16)],
        compiler_params=params(20),
        cost_estimate=cost(tokens.shape[0] * tile_cols, model * weight.shape[1]),
        name="joint_rows",
    )(tokens, gain, weight, relative)


def cost(rows, weights):
    return pl.CostEstimate(flops=4 * rows * weights, bytes_accessed=4 * 2**20, transcendentals=0)


def inner_windows(joint, bias):
    return pl.pallas_call(
        inner_kernel,
        out_shape=jax.ShapeDtypeStruct(joint.shape[:3] + (joint.shape[3] // 3,), jnp.bfloat16),
        in_specs=[VMEM] * 2,
        out_specs=VMEM,
        compiler_params=params(20),
        cost_estimate=cost(joint.shape[0] * joint.shape[1] * CELL, 2**19),
        name="inner_windows",
    )(joint, bias)


def end_windows(joint, up, down, bias, gain, weight):
    _, across, _, triple = joint.shape
    return pl.pallas_call(
        ends_kernel,
        out_shape=(cells_of(2, across, triple * 2 // 3), cells_of(2, across, triple // 3)),
        in_specs=[VMEM] * 6,
        out_specs=(VMEM, VMEM),
        compiler_params=params(20),
        cost_estimate=cost(joint.shape[0] * joint.shape[1] * CELL, 2**19),
        name="end_windows",
    )(joint, up, down, bias, gain, weight)


def side_windows(ordered, joint, inner, pairs, ends, left, right, bias, gains, weights):
    down, across, _, triple = joint.shape
    model = triple // 3
    strip = CELL * across
    rows = 2 * strip
    wide = weights[2].shape[1]
    return pl.pallas_call(
        sides_kernel,
        out_shape=jax.ShapeDtypeStruct((down * SUB, across * SUB, weights[-1].shape[1]), jnp.bfloat16),
        in_specs=[VMEM] * 15,
        out_specs=VMEM,
        scratch_shapes=[
            pltpu.VMEM((down, across, CELL, model), jnp.bfloat16),
            pltpu.VMEM((2, down + 2, CELL, 2 * model), jnp.bfloat16),
            pltpu.VMEM((strip, strip), jnp.bfloat16),
            pltpu.VMEM((2, rows, model), jnp.float32),
            pltpu.VMEM((2, rows, model), jnp.bfloat16),
            pltpu.VMEM((2, rows, wide), jnp.float32),
            pltpu.VMEM((2, rows, wide), jnp.bfloat16),
        ],
        compiler_params=params(28),
        name="side_windows",
    )(ordered, joint, inner, pairs, ends, left, right, bias, *gains, *weights)


BOX_OWN = 8


def shift(x, axis, step):
    size = lax.axis_size(axis)
    pairs = [(i, i + step) for i in range(size) if 0 <= i + step < size]
    return lax.ppermute(x, axis, pairs)


def shards(
    tokens, first_gain, second_gain, joint_weight, merge_weight, expand_weight, shrink_weight,
    relative_bias, lateral_weight, conv_weight, mask_weight, box_geometry, box_counts, box_owner,
    soft_target,
):
    tile_rows, tile_cols, model = tokens.shape
    rows_size = lax.axis_size("row")
    joint, bias, ordered, north, south, west, east = joint_rows(
        tokens, first_gain, joint_weight, relative_bias
    )
    up = shift(south, "row", 1)
    down = shift(north, "row", -1)
    inner = inner_windows(joint, bias)
    left = shift(jnp.concatenate([up[-1:], east, down[-1:]], axis=0), "col", 1)
    right = shift(jnp.concatenate([up[:1], west, down[:1]], axis=0), "col", -1)
    pairs, ends = end_windows(joint, up, down, bias, first_gain, joint_weight)
    features = side_windows(
        ordered, joint, inner, pairs, ends, left, right, bias, (first_gain, second_gain),
        (joint_weight, merge_weight, expand_weight, shrink_weight, lateral_weight),
    )
    capacity = box_geometry.shape[2]
    count = box_counts.reshape(1)
    soft = soft_target.reshape(capacity, CROP, CROP).transpose(1, 2, 0).astype(jnp.float32)
    logits, feature_grad = mask_head(
        features, box_geometry, box_counts, conv_weight, mask_weight, soft.reshape(CROP, -1)
    )
    local = logits.reshape(CROP * CROP, capacity)
    slots = jnp.arange(capacity, dtype=jnp.int32)
    valid = slots < count
    owner = box_owner.reshape(-1)
    rank = jnp.sum((owner[:, None] == owner[None, :]) & (slots[None, :] < slots[:, None]), axis=1)
    each = max(1, capacity // rows_size)
    send = rows_size * each
    routing = (
        (owner * each + rank)[None, :] == jnp.arange(send, dtype=jnp.int32)[:, None]
    ) & valid[None, :]
    packed = jnp.concatenate(
        [local, jnp.ones((1, capacity), jnp.float32)], axis=0
    )
    outgoing = lax.dot_general(
        routing.astype(jnp.float32), packed, NT, precision=HIGHEST
    ).reshape(rows_size, each, -1)
    arriving = lax.all_to_all(outgoing, "row", split_axis=0, concat_axis=0, tiled=True)
    arriving = arriving.reshape(send, -1)
    present = arriving[:, -1] > 0.5
    position = jnp.cumsum(present.astype(jnp.int32)) - 1
    picker = (
        position[None, :] == jnp.arange(BOX_OWN, dtype=jnp.int32)[:, None]
    ) & present[None, :]
    mask_logits = jnp.dot(picker.astype(jnp.float32), arriving[:, :-1], precision=HIGHEST)
    return features, feature_grad, mask_logits.reshape(1, 1, BOX_OWN, -1)


def solution(mesh):
    tile = P("row", "col", None)
    placed = (tile,) + (P(),) * 10 + (
        P("row", "col", None, None), P("row", "col"), tile, P("row", "col", None, None),
    )
    return jax.shard_map(
        shards,
        mesh=mesh,
        in_specs=placed,
        out_specs=(tile, tile, P("row", "col", None, None)),
        check_vma=False,
    )
```

```python
import functools
import jax
import jax.numpy as jnp
from jax import lax
from jax.experimental import pallas as pl
from jax.experimental.pallas import tpu as pltpu
from jax.sharding import PartitionSpec as P

CROP = 14
ROWS = 2
PAD = CROP + 2
GELU_A = 0.7978845608028654
GELU_B = 0.044715
loss_scale = 128.0
NT = (((1,), (1,)), ((), ()))
HIGHEST = lax.Precision.HIGHEST
TN = (((0,), (0,)), ((), ()))
VMEM = pl.BlockSpec(memory_space=pltpu.VMEM)
SMEM = pl.BlockSpec(memory_space=pltpu.SMEM)


def gelu_value(x):
    inner = x * (GELU_A + (GELU_A * GELU_B) * (x * x))
    return x * (0.5 + 0.5 * jnp.tanh(inner))


def gelu_parts(x):
    square = x * x
    inner = x * (GELU_A + (GELU_A * GELU_B) * square)
    half = 0.5 + 0.5 * jnp.tanh(inner)
    value = x * half
    slope = half + value * (1.0 - half) * (2.0 * GELU_A + (6.0 * GELU_A * GELU_B) * square)
    return value, slope


def clear_border(ref):
    blank = jnp.zeros((PAD,) + ref.shape[2:], ref.dtype)
    ref[0] = blank
    ref[PAD - 1] = blank
    for row in range(1, PAD - 1):
        ref[row, 0] = blank[0]
        ref[row, PAD - 1] = blank[0]


def taps_of(ref, begin, end, flip):
    boxes, channels = ref.shape[2:]
    pieces = []
    for s in range(3):
        for t in range(3):
            s0, t0 = (2 - s, 2 - t) if flip else (s, t)
            part = ref[begin + s0 : end + s0, t0 : t0 + CROP]
            pieces.append(part.reshape((end - begin) * CROP * boxes, channels))
    return pieces


def box_columns(values, shape, axis):
    index = lax.broadcasted_iota(jnp.int32, shape, axis)
    spread = jnp.zeros(shape, jnp.int32)
    for n, value in enumerate(values):
        spread = jnp.where(index == n, value, spread)
    return spread


def chain(product, finish, before_ref, stages):
    late = None
    for number, (layer, source, target) in enumerate(stages):
        before = before_ref.at[number % 2]
        for begin in range(0, CROP, ROWS):
            end = min(begin + ROWS, CROP)
            before[begin:end] = product(layer, source, begin, end).reshape(
                (end - begin,) + before.shape[1:]
            )
            if late is not None:
                late()
            late = functools.partial(finish, layer, before, target, begin, end)
    late()


def forward_kernel(
    geom_ref, count_ref, owner_ref, features_ref, weight_ref, mask_ref,
    send_ref, slope_ref,
    a_ref, b_ref, strip_ref, pick_ref, before_ref,
):
    _, boxes, tile_cols, channels = strip_ref.shape
    layers = weight_ref.shape[0]
    lanes = CROP * boxes
    count = count_ref[0, 0]
    clear_border(a_ref)
    clear_border(b_ref)
    shape = (boxes, boxes * tile_cols)
    lane = lax.broadcasted_iota(jnp.int32, shape, 1)
    start = box_columns([geom_ref[0, 0, n, 1] for n in range(boxes)], shape, 0)
    width = box_columns([geom_ref[0, 0, n, 3] for n in range(boxes)], shape, 0)
    mine = lane // tile_cols == lax.broadcasted_iota(jnp.int32, shape, 0)
    away = jnp.where(mine, lane % tile_cols - start, -1)
    away = jnp.where(away < width, away, -1)
    for v in range(CROP):
        pick_ref[v * boxes : (v + 1) * boxes, :] = (away == v).astype(jnp.bfloat16)
    for n in range(boxes):
        rows = features_ref[pl.ds(geom_ref[0, 0, n, 0], CROP)]
        tall = jnp.where(n < count, geom_ref[0, 0, n, 2], 0)
        for u in range(CROP):
            strip_ref[u, n] = jnp.where(u < tall, rows[u], jnp.zeros_like(rows[u]))
    for u in range(CROP):
        crop = jnp.dot(
            pick_ref[...], strip_ref[u].reshape(-1, channels), preferred_element_type=jnp.float32
        )
        a_ref[u + 1, 1 : 1 + CROP] = crop.astype(jnp.bfloat16).reshape(CROP, boxes, channels)

    def forward(layer, source, begin, end):
        return jnp.dot(
            jnp.concatenate(taps_of(source, begin, end, False), axis=1),
            weight_ref[layer],
            preferred_element_type=jnp.float32,
        )

    def activate(layer, before, target, begin, end):
        for u in range(begin, end):
            for v in range(CROP):
                piece = slice(v * boxes, (v + 1) * boxes)
                value, slope = gelu_parts(before[u, piece])
                slope_ref[layer, u, piece] = slope.astype(jnp.bfloat16)
                target[u + 1, 1 + v] = value.astype(jnp.bfloat16)

    def up(pair, carry):
        stages = [(2 * pair, a_ref, b_ref), (2 * pair + 1, b_ref, a_ref)]
        chain(forward, activate, before_ref, stages)
        return carry

    lax.fori_loop(0, layers // 2, up, 0)
    vector = mask_ref[...].astype(jnp.float32).reshape(1, channels)
    place = lax.broadcasted_iota(jnp.int32, send_ref.shape, 1)
    sums = [jnp.zeros(send_ref.shape, jnp.float32) for _ in range(2)]
    for cell in range(CROP * CROP):
        u, v = divmod(cell, CROP)
        line = jnp.sum(a_ref[u + 1, v + 1].astype(jnp.float32) * vector, axis=-1, keepdims=True)
        sums[cell % 2] = jnp.where(place == cell, line, sums[cell % 2])
    owner = box_columns(
        [jnp.where(n < count, owner_ref[0, 0, n], -1) for n in range(boxes)], send_ref.shape, 0
    )
    send_ref[...] = jnp.where(
        place == CROP * CROP, owner.astype(jnp.float32), sums[0] + sums[1]
    )


def backward_kernel(
    geom_ref, count_ref, send_ref, soft_ref, slope_ref, weight_ref, mask_ref,
    grad_ref,
    a_ref, b_ref, spread_ref, place_ref, before_ref,
):
    boxes, channels = a_ref.shape[2:]
    tile_cols = grad_ref.shape[1]
    layers = weight_ref.shape[0]
    lanes = CROP * boxes
    cells = CROP * CROP
    count = count_ref[0, 0]
    clear_border(a_ref)
    clear_border(b_ref)
    broad = [geom_ref[0, 0, n, 3] for n in range(boxes)]
    tall = [jnp.where(n < count, geom_ref[0, 0, n, 2], 0) for n in range(boxes)]
    lane = lax.broadcasted_iota(jnp.int32, (tile_cols, lanes), 1)
    cell = lax.broadcasted_iota(jnp.int32, (tile_cols, lanes), 0)
    box, col = lane % boxes, lane // boxes
    for n in range(boxes):
        place_ref[n * tile_cols : (n + 1) * tile_cols, :] = (
            (cell == col + geom_ref[0, 0, n, 1]) & (box == n) & (col < broad[n])
        ).astype(jnp.bfloat16)
    shape = (boxes, cells)
    where = lax.broadcasted_iota(jnp.int32, shape, 1)
    inside = (where // CROP < box_columns(tall, shape, 0)) & (
        where % CROP < box_columns(broad, shape, 0)
    )
    soft = soft_ref[0, 0].astype(jnp.float32)
    lead = loss_scale * (jax.nn.sigmoid(send_ref[:, :cells]) - soft)
    lead = jnp.where(inside, lead, 0.0)
    vector = mask_ref[...].astype(jnp.float32).reshape(1, channels)
    for u in range(CROP):
        for v in range(CROP):
            piece = slice(v * boxes, (v + 1) * boxes)
            grad = lead[:, u * CROP + v : u * CROP + v + 1] * vector
            slope = slope_ref[layers - 1, u, piece].astype(jnp.float32)
            b_ref[u + 1, 1 + v] = (grad * slope).astype(jnp.bfloat16)

    def backward(layer, source, begin, end):
        total = None
        for tap, piece in enumerate(taps_of(source, begin, end, True)):
            part = lax.dot_general(
                piece,
                weight_ref[layer, tap * channels : (tap + 1) * channels, :],
                NT,
                preferred_element_type=jnp.float32,
            )
            total = part if total is None else total + part
        return total

    def descend(layer, before, target, begin, end):
        first = layer == 0
        for u in range(begin, end):
            for v in range(CROP):
                piece = slice(v * boxes, (v + 1) * boxes)
                slope = slope_ref[jnp.maximum(layer - 1, 0), u, piece].astype(jnp.float32)
                slope = jnp.where(first, 1.0, slope)
                target[u + 1, 1 + v] = (before[u, piece] * slope).astype(jnp.bfloat16)

    def down(pair, carry):
        layer = layers - 1 - 2 * pair
        stages = [(layer, b_ref, a_ref), (layer - 1, a_ref, b_ref)]
        chain(backward, descend, before_ref, stages)
        return carry

    lax.fori_loop(0, layers // 2, down, 0)
    for u in range(CROP):
        spread_ref[u] = jnp.dot(
            place_ref[...],
            b_ref[u + 1, 1 : 1 + CROP].reshape(lanes, channels),
            preferred_element_type=jnp.float32,
        ).reshape(boxes, tile_cols, channels)
    grad_ref[...] = jnp.zeros_like(grad_ref)
    for n in range(boxes):
        kept = lax.broadcasted_iota(jnp.int32, (CROP, 1, 1), 0) < tall[n]
        rows = pl.ds(geom_ref[0, 0, n, 0], CROP)
        grad_ref[rows] = grad_ref[rows] + jnp.where(kept, spread_ref[:, n], 0.0)


def collect_kernel(sent_ref, out_ref):
    boxes = sent_ref.shape[0]
    keep, cells = out_ref.shape[2:]
    owner = sent_ref[:, cells : cells + 1]
    mine = (owner == lax.axis_index("row").astype(jnp.float32)).astype(jnp.float32)
    row = lax.broadcasted_iota(jnp.int32, (boxes, boxes), 0)
    col = lax.broadcasted_iota(jnp.int32, (boxes, boxes), 1)
    earlier = (col < row).astype(jnp.float32).astype(jnp.bfloat16)
    many = jnp.broadcast_to(mine, (boxes, 128)).astype(jnp.bfloat16)
    position = jnp.dot(earlier, many, preferred_element_type=jnp.float32)[:, :keep]
    slot = lax.broadcasted_iota(jnp.int32, (boxes, keep), 1).astype(jnp.float32)
    picker = jnp.where(position == slot, mine, 0.0)
    out_ref[0, 0] = lax.dot_general(
        picker, sent_ref[:, :cells], TN, precision=HIGHEST, preferred_element_type=jnp.float32
    )


def mask_cost(weight):
    return pl.CostEstimate(flops=25 * 10**9, bytes_accessed=2 * weight.size, transcendentals=0)


def mask_forward(features, geometry, count, owner, weight, mask):
    tile_rows, tile_cols, channels = features.shape
    boxes = geometry.shape[2]
    layers = weight.shape[0]
    lanes = CROP * boxes
    padded = pltpu.VMEM((PAD, PAD, boxes, channels), jnp.bfloat16)
    return pl.pallas_call(
        forward_kernel,
        out_shape=(
            jax.ShapeDtypeStruct((boxes, 256), jnp.float32),
            jax.ShapeDtypeStruct((layers, CROP, lanes, channels), jnp.bfloat16),
        ),
        in_specs=[SMEM, SMEM, SMEM, VMEM, VMEM, VMEM],
        out_specs=(VMEM, VMEM),
        scratch_shapes=[
            padded,
            padded,
            pltpu.VMEM((CROP, boxes, tile_cols, channels), jnp.bfloat16),
            pltpu.VMEM((lanes, boxes * tile_cols), jnp.bfloat16),
            pltpu.VMEM((2, CROP, lanes, channels), jnp.float32),
        ],
        compiler_params=pltpu.CompilerParams(vmem_limit_bytes=32 * 2**20),
        cost_estimate=mask_cost(weight),
        name="mask_forward",
    )(geometry, count, owner, features, weight, mask)


def mask_backward(send, soft, slope, geometry, count, weight, mask, tile):
    layers, _, lanes, channels = slope.shape
    boxes = geometry.shape[2]
    padded = pltpu.VMEM((PAD, PAD, boxes, channels), jnp.bfloat16)
    return pl.pallas_call(
        backward_kernel,
        out_shape=jax.ShapeDtypeStruct(tile + (channels,), jnp.float32),
        in_specs=[SMEM, SMEM, VMEM, VMEM, VMEM, VMEM, VMEM],
        out_specs=VMEM,
        scratch_shapes=[
            padded,
            padded,
            pltpu.VMEM((CROP, boxes, tile[1], channels), jnp.float32),
            pltpu.VMEM((boxes * tile[1], lanes), jnp.bfloat16),
            pltpu.VMEM((2, CROP, lanes, channels), jnp.float32),
        ],
        compiler_params=pltpu.CompilerParams(vmem_limit_bytes=38 * 2**20),
        cost_estimate=mask_cost(weight),
        name="mask_backward",
    )(geometry, count, send, soft, slope, weight, mask)


def collect(sent, keep, cells):
    return pl.pallas_call(
        collect_kernel,
        out_shape=jax.ShapeDtypeStruct((1, 1, keep, cells), jnp.float32),
        in_specs=[VMEM],
        out_specs=VMEM,
        compiler_params=pltpu.CompilerParams(vmem_limit_bytes=8 * 2**20),
        name="collect",
    )(sent)


HEADS = 12
WIN = 8
SUB = WIN // 2
CELL = SUB * SUB
AREA = WIN * WIN
GROUP = 4
EPSILON = 1e-05
BLOCKED = -1000000000.0


def norm_rows(values, gain):
    centered = values - jnp.mean(values, axis=-1, keepdims=True)
    variance = jnp.mean(centered * centered, axis=-1, keepdims=True)
    return (centered * lax.rsqrt(variance + EPSILON) * gain).astype(jnp.bfloat16)


def one_hot(equal, dtype=jnp.bfloat16):
    return equal.astype(jnp.float32).astype(dtype)


def strip_order(width):
    size = SUB * width
    cell_pos = lax.broadcasted_iota(jnp.int32, (size, size), 0)
    token = lax.broadcasted_iota(jnp.int32, (size, size), 1)
    cell, row, col = cell_pos // CELL, cell_pos // SUB % SUB, cell_pos % SUB
    return one_hot(token == row * width + cell * SUB + col)


def window_order():
    place = lax.broadcasted_iota(jnp.int32, (AREA, AREA), 0)
    token = lax.broadcasted_iota(jnp.int32, (AREA, AREA), 1)
    cell, row, col = place // CELL, place // SUB % SUB, place % SUB
    return one_hot(token == (cell // 2 * SUB + row) * WIN + cell % 2 * SUB + col, jnp.float32)


def head_blocks(lanes):
    row = lax.broadcasted_iota(jnp.int32, (GROUP * AREA, lanes), 0)
    col = lax.broadcasted_iota(jnp.int32, (GROUP * AREA, lanes), 1)
    return one_hot(row // AREA == col // (lanes // GROUP))


def attend(queries, key_rows, value_rows, bias, blocks, key_mask):
    lanes = blocks.shape[1]
    scale = (lanes // GROUP) ** (-0.5)
    first = lax.broadcasted_iota(jnp.int32, (1, 2 * AREA), 1) < AREA
    mixed = []
    for group in range(len(bias)):
        cut = slice(group * lanes, (group + 1) * lanes)
        keys = jnp.concatenate([key_rows[:, cut]] * GROUP, axis=0) * blocks
        values = jnp.concatenate([value_rows[:, cut]] * GROUP, axis=0) * blocks
        scores = lax.dot_general(queries[:, cut], keys, NT, preferred_element_type=jnp.float32)
        scores = scores * scale + bias[group]
        if key_mask is not None:
            scores = scores + key_mask
        weights = []
        for pair in range(GROUP // 2):
            part = scores[:, pair * 2 * AREA : (pair + 1) * 2 * AREA]
            low = jnp.max(jnp.where(first, part, -jnp.inf), axis=-1, keepdims=True)
            high = jnp.max(jnp.where(first, -jnp.inf, part), axis=-1, keepdims=True)
            weights.append(jnp.exp(part - jnp.where(first, low, high)))
        weights = jnp.concatenate(weights, axis=1).astype(jnp.bfloat16)
        both = jnp.dot(
            weights, jnp.concatenate([values, blocks], axis=1), preferred_element_type=jnp.float32
        )
        mixed.append((both[:, :lanes] / both[:, lanes:]).astype(jnp.bfloat16))
    return jnp.concatenate(mixed, axis=1)


def joint_kernel(
    tokens_ref, gain_ref, joint_ref, relative_ref,
    out_ref, bias_ref, ordered_ref, north_ref, south_ref, west_ref, east_ref, order_ref,
):
    cells_down, cells_across, _, model = ordered_ref.shape
    strip = order_ref.shape[0]
    order_ref[...] = strip_order(strip // SUB)
    place = window_order()
    turned = lax.dot_general(
        relative_ref[...].reshape(-1, AREA), place, NT,
        precision=HIGHEST, preferred_element_type=jnp.float32,
    )
    for group in range(HEADS // GROUP):
        rows = [
            turned[(group * GROUP + h) * AREA : (group * GROUP + h + 1) * AREA]
            for h in range(GROUP)
        ]
        bias_ref[group] = jnp.dot(
            place,
            jnp.concatenate(rows, axis=1),
            precision=HIGHEST,
            preferred_element_type=jnp.float32,
        )
    gain = gain_ref[...].reshape(1, model)

    def body(step, carry):
        normed = []
        for part in range(2):
            down = 2 * step + part
            ordered = jnp.dot(
                order_ref[...],
                tokens_ref[pl.ds(down * SUB, SUB)].reshape(strip, model),
                preferred_element_type=jnp.float32,
            )
            ordered_ref[down] = ordered.astype(jnp.bfloat16).reshape(cells_across, CELL, model)
            normed.append(norm_rows(ordered, gain))
        out_ref[pl.ds(2 * step, 2)] = (
            jnp.dot(
                jnp.concatenate(normed, axis=0), joint_ref[...], preferred_element_type=jnp.float32
            )
            .astype(jnp.bfloat16)
            .reshape(2, cells_across, CELL, 3 * model)
        )
        return carry

    lax.fori_loop(0, cells_down // 2, body, 0)
    north_ref[...] = ordered_ref[0]
    south_ref[...] = ordered_ref[cells_down - 1]
    west_ref[...] = ordered_ref[:, 0]
    east_ref[...] = ordered_ref[:, cells_across - 1]


def inner_kernel(joint_ref, bias_ref, out_ref):
    cells_down, cells_across, _, triple = joint_ref.shape
    model = triple // 3
    blocks = head_blocks(GROUP * model // HEADS)
    bias = [bias_ref[group] for group in range(bias_ref.shape[0])]

    def body(i, carry):
        for j in range(cells_across // 2 - 1):
            rows = joint_ref[pl.ds(2 * i + 1, 2), 2 * j + 1 : 2 * j + 3].reshape(AREA, triple)
            mixed = attend(
                rows[:, :model], rows[:, model : 2 * model], rows[:, 2 * model :], bias, blocks, None
            )
            out_ref[pl.ds(2 * i + 1, 2), 2 * j + 1 : 2 * j + 3] = mixed.reshape(2, 2, CELL, model)
        return carry

    lax.fori_loop(0, cells_down // 2 - 1, body, 0)


def hidden_keys(down_side, down_edge, across_side, across_edge):
    cell = lax.broadcasted_iota(jnp.int32, (1, GROUP * AREA), 1) // CELL % 4
    hidden = jnp.zeros((1, GROUP * AREA), jnp.bool_)
    if down_side is not None:
        hidden = hidden | ((cell // 2 == down_side) & down_edge)
    if across_side is not None:
        hidden = hidden | ((cell % 2 == across_side) & across_edge)
    return jnp.where(hidden, BLOCKED, 0.0)


def at_end(axis, side):
    return lax.axis_index(axis) == (lax.axis_size(axis) - 1 if side else 0)


def window_bias(bias_ref, cells):
    return [
        jnp.concatenate([bias_ref[g, c * CELL : (c + 1) * CELL] for c in cells], axis=0)
        for g in range(bias_ref.shape[0])
    ]


def halo_pairs(halo, gain, joint_ref):
    model = halo.shape[-1]
    normed = norm_rows(halo.astype(jnp.float32), gain)
    return jnp.dot(normed, joint_ref[:, model:], preferred_element_type=jnp.float32).astype(
        jnp.bfloat16
    )


def ends_kernel(joint_out_ref, up_ref, down_ref, bias_ref, gain_ref, joint_ref, pairs_ref, out_ref):
    cells_down, cells_across, _, triple = joint_out_ref.shape
    model = triple // 3
    blocks = head_blocks(GROUP * model // HEADS)
    gain = gain_ref[...].reshape(1, model)
    halo = jnp.concatenate([ref[...].reshape(-1, model) for ref in (up_ref, down_ref)], axis=0)
    pairs_ref[...] = halo_pairs(halo, gain, joint_ref).reshape(2, cells_across, CELL, 2 * model)
    for side in range(2):
        row = side * (cells_down - 1)
        bias = window_bias(bias_ref, [2 - 2 * side, 3 - 2 * side])
        key_mask = hidden_keys(side, at_end("row", side), None, None)
        for j in range(1, cells_across // 2):
            cut = slice(2 * j - 1, 2 * j + 1)
            own = joint_out_ref[row, cut].reshape(2 * CELL, triple)
            other = pairs_ref[side, cut].reshape(2 * CELL, 2 * model)
            both = [own[:, model:], other] if side else [other, own[:, model:]]
            both = jnp.concatenate(both, axis=0)
            mixed = attend(own[:, :model], both[:, :model], both[:, model:], bias, blocks, key_mask)
            out_ref[side, cut] = mixed.reshape(2, CELL, model)


def sides_kernel(
    ordered_ref, joint_out_ref, inner_ref, pairs_ref, ends_ref, left_ref, right_ref,
    bias_ref, first_ref, second_ref, joint_ref, merge_ref, expand_ref, shrink_ref, lateral_ref,
    features_ref, copy_ref, mixed_ref, halo_ref, order_ref, residual_ref, normed_ref, wide_ref, hidden_ref,
):
    cells_down, cells_across, _, triple = joint_out_ref.shape
    model = triple // 3
    strip = cells_across * CELL
    order_ref[...] = strip_order(cells_across * SUB)
    blocks = head_blocks(GROUP * model // HEADS)
    halo = jnp.concatenate([ref[...].reshape(-1, model) for ref in (left_ref, right_ref)], axis=0)
    halo = halo_pairs(halo, first_ref[...].reshape(1, model), joint_ref)
    halo_ref[...] = halo.reshape(2, cells_down + 2, CELL, 2 * model)
    mixed_ref[1:-1, 1:-1] = inner_ref[1:-1, 1:-1]
    mixed_ref[0, 1:-1] = ends_ref[0, 1:-1]
    mixed_ref[cells_down - 1, 1:-1] = ends_ref[1, 1:-1]

    for across in range(2):
        col = across * (cells_across - 1)
        bias = window_bias(bias_ref, [1 - across, 3 - across])
        key_mask = hidden_keys(None, None, across, at_end("col", across))

        def keys(pieces):
            rows = []
            for own, other in pieces:
                rows += [own, other] if across else [other, own]
            return jnp.concatenate(rows, axis=0)

        for i in range(1, cells_down // 2):
            cells = [2 * i - 1, 2 * i]
            both = keys(
                [(joint_out_ref[c, col, :, model:], halo_ref[across, c + 1]) for c in cells]
            )
            queries = jnp.concatenate([joint_out_ref[c, col, :, :model] for c in cells], axis=0)
            mixed = attend(queries, both[:, :model], both[:, model:], bias, blocks, key_mask)
            for place, c in enumerate(cells):
                mixed_ref[c, col] = mixed[place * CELL : (place + 1) * CELL]
        for down in range(2):
            row = down * (cells_down - 1)
            near = (joint_out_ref[row, col, :, model:], halo_ref[across, row + 1])
            far = (pairs_ref[down, col], halo_ref[across, down * (cells_down + 1)])
            both = keys([near, far] if down else [far, near])
            mixed_ref[row, col] = attend(
                joint_out_ref[row, col, :, :model], both[:, :model], both[:, model:],
                window_bias(bias_ref, [3 - 2 * down - across]), blocks,
                hidden_keys(down, at_end("row", down), across, at_end("col", across)),
            )

    second = second_ref[...].reshape(1, model)
    rows = hidden_ref.shape[1]
    group = rows // strip
    steps = cells_down // group

    def merge(step):
        residual = residual_ref.at[step % 2]
        cells = slice(step * group, (step + 1) * group)
        residual[...] = jnp.dot(
            mixed_ref[cells].reshape(rows, model), merge_ref[...], preferred_element_type=jnp.float32
        )
        for part in range(0, rows, PART):
            cut = slice(part, part + PART)
            c, a = divmod(part // CELL, cells_across)
            own = ordered_ref[step * group + c, a : a + PART // CELL].reshape(PART, model)
            total = residual[cut] + own.astype(jnp.float32)
            residual[cut] = total
            normed_ref[step % 2, cut] = norm_rows(total, second)

    def expand(step):
        wide_ref[step % 2] = jnp.dot(
            normed_ref[step % 2], expand_ref[...], preferred_element_type=jnp.float32
        )

    def activate(step):
        for part in range(0, rows, CELL):
            cut = slice(part, part + CELL)
            for lane in range(0, wide_ref.shape[2], 512):
                hidden_ref[step % 2, cut, lane : lane + 512] = gelu_value(
                    wide_ref[step % 2, cut, lane : lane + 512]
                ).astype(jnp.bfloat16)

    def shrink(step):
        block_out = residual_ref[step % 2] + jnp.dot(
            hidden_ref[step % 2], shrink_ref[...], preferred_element_type=jnp.float32
        )
        features = jnp.dot(
            block_out.astype(jnp.bfloat16), lateral_ref[...], preferred_element_type=jnp.float32
        ).astype(jnp.bfloat16)
        for part in range(group):
            natural = lax.dot_general(
                order_ref[...], features[part * strip : (part + 1) * strip], TN,
                preferred_element_type=jnp.float32,
            ).astype(jnp.bfloat16)
            first = (step * group + part) * SUB
            natural = natural.reshape((SUB,) + features_ref.shape[1:])
            features_ref[first : first + SUB] = natural
            copy_ref[first : first + SUB] = natural

    merge(0)
    expand(0)
    for step in range(steps):
        if step + 1 < steps:
            merge(step + 1)
        activate(step)
        if step + 1 < steps:
            expand(step + 1)
        shrink(step)


PART = 64


def params(mebibytes):
    return pltpu.CompilerParams(vmem_limit_bytes=mebibytes * 2**20)


def cells_of(count_down, count_across, channels, dtype=jnp.bfloat16):
    return jax.ShapeDtypeStruct((count_down, count_across, CELL, channels), dtype)


def joint_rows(tokens, gain, weight, relative):
    tile_rows, tile_cols, model = tokens.shape
    down, across = tile_rows // SUB, tile_cols // SUB
    lone = lambda n: jax.ShapeDtypeStruct((n, CELL, model), jnp.bfloat16)
    return pl.pallas_call(
        joint_kernel,
        out_shape=(
            cells_of(down, across, weight.shape[1]),
            jax.ShapeDtypeStruct((HEADS // GROUP, AREA, GROUP * AREA), jnp.float32),
            cells_of(down, across, model),
            lone(across), lone(across), lone(down), lone(down),
        ),
        in_specs=[VMEM] * 4,
        out_specs=(VMEM,) * 7,
        scratch_shapes=[pltpu.VMEM((SUB * tile_cols, SUB * tile_cols), jnp.bfloat16)],
        compiler_params=params(20),
        cost_estimate=cost(tokens.shape[0] * tile_cols, model * weight.shape[1]),
        name="joint_rows",
    )(tokens, gain, weight, relative)


def cost(rows, weights):
    return pl.CostEstimate(flops=4 * rows * weights, bytes_accessed=4 * 2**20, transcendentals=0)


def inner_windows(joint, bias):
    return pl.pallas_call(
        inner_kernel,
        out_shape=jax.ShapeDtypeStruct(joint.shape[:3] + (joint.shape[3] // 3,), jnp.bfloat16),
        in_specs=[VMEM] * 2,
        out_specs=VMEM,
        compiler_params=params(20),
        cost_estimate=cost(joint.shape[0] * joint.shape[1] * CELL, 2**19),
        name="inner_windows",
    )(joint, bias)


def end_windows(joint, up, down, bias, gain, weight):
    _, across, _, triple = joint.shape
    return pl.pallas_call(
        ends_kernel,
        out_shape=(cells_of(2, across, triple * 2 // 3), cells_of(2, across, triple // 3)),
        in_specs=[VMEM] * 6,
        out_specs=(VMEM, VMEM),
        compiler_params=params(20),
        cost_estimate=cost(joint.shape[0] * joint.shape[1] * CELL, 2**19),
        name="end_windows",
    )(joint, up, down, bias, gain, weight)


def side_windows(ordered, joint, inner, pairs, ends, left, right, bias, gains, weights):
    down, across, _, triple = joint.shape
    model = triple // 3
    strip = CELL * across
    rows = 2 * strip
    wide = weights[2].shape[1]
    tile = jax.ShapeDtypeStruct((down * SUB, across * SUB, weights[-1].shape[1]), jnp.bfloat16)
    return pl.pallas_call(
        sides_kernel,
        out_shape=(tile, tile),
        in_specs=[VMEM] * 15,
        out_specs=(VMEM, VMEM),
        scratch_shapes=[
            pltpu.VMEM((down, across, CELL, model), jnp.bfloat16),
            pltpu.VMEM((2, down + 2, CELL, 2 * model), jnp.bfloat16),
            pltpu.VMEM((strip, strip), jnp.bfloat16),
            pltpu.VMEM((2, rows, model), jnp.float32),
            pltpu.VMEM((2, rows, model), jnp.bfloat16),
            pltpu.VMEM((2, rows, wide), jnp.float32),
            pltpu.VMEM((2, rows, wide), jnp.bfloat16),
        ],
        compiler_params=params(28),
        name="side_windows",
    )(ordered, joint, inner, pairs, ends, left, right, bias, *gains, *weights)


BOX_OWN = 8


def shift(x, axis, step):
    size = lax.axis_size(axis)
    pairs = [(i, i + step) for i in range(size) if 0 <= i + step < size]
    return lax.ppermute(x, axis, pairs)


def shards(
    tokens, first_gain, second_gain, joint_weight, merge_weight, expand_weight, shrink_weight,
    relative_bias, lateral_weight, conv_weight, mask_weight, box_geometry, box_counts, box_owner,
    soft_target,
):
    tile_rows, tile_cols, model = tokens.shape
    joint, bias, ordered, north, south, west, east = joint_rows(
        tokens, first_gain, joint_weight, relative_bias
    )
    up = shift(south, "row", 1)
    down = shift(north, "row", -1)
    inner = inner_windows(joint, bias)
    left = shift(jnp.concatenate([up[-1:], east, down[-1:]], axis=0), "col", 1)
    right = shift(jnp.concatenate([up[:1], west, down[:1]], axis=0), "col", -1)
    pairs, ends = end_windows(joint, up, down, bias, first_gain, joint_weight)
    features, features_here = side_windows(
        ordered, joint, inner, pairs, ends, left, right, bias, (first_gain, second_gain),
        (joint_weight, merge_weight, expand_weight, shrink_weight, lateral_weight),
    )
    send, slope = mask_forward(
        features_here, box_geometry, box_counts, box_owner, conv_weight, mask_weight
    )
    sent = lax.all_gather(send, "row", axis=0, tiled=True)
    feature_grad = mask_backward(
        send, soft_target, slope, box_geometry, box_counts, conv_weight, mask_weight,
        (tile_rows, tile_cols),
    )
    return features, feature_grad, collect(sent, BOX_OWN, CROP * CROP)


def solution(mesh):
    tile = P("row", "col", None)
    placed = (tile,) + (P(),) * 10 + (
        P("row", "col", None, None), P("row", "col"), tile, P("row", "col", None, None),
    )
    return jax.shard_map(
        shards,
        mesh=mesh,
        in_specs=placed,
        out_specs=(tile, tile, P("row", "col", None, None)),
        check_vma=False,
    )
```

```python
import functools
import jax
import jax.numpy as jnp
from jax import lax
from jax.experimental import pallas as pl
from jax.experimental.pallas import tpu as pltpu
from jax.sharding import PartitionSpec as P

CROP = 14
ROWS = 2
FORWARD_MIB = 16
BACKWARD_MIB = 20
PAD = CROP + 2
GELU_A = 0.7978845608028654
GELU_B = 0.044715
loss_scale = 128.0
NT = (((1,), (1,)), ((), ()))
HIGHEST = lax.Precision.HIGHEST
TN = (((0,), (0,)), ((), ()))
VMEM = pl.BlockSpec(memory_space=pltpu.VMEM)
SMEM = pl.BlockSpec(memory_space=pltpu.SMEM)


def gelu_value(x):
    inner = x * (GELU_A + (GELU_A * GELU_B) * (x * x))
    return x * (0.5 + 0.5 * jnp.tanh(inner))


def gelu_parts(x):
    square = x * x
    inner = x * (GELU_A + (GELU_A * GELU_B) * square)
    half = 0.5 + 0.5 * jnp.tanh(inner)
    value = x * half
    slope = half + value * (1.0 - half) * (2.0 * GELU_A + (6.0 * GELU_A * GELU_B) * square)
    return value, slope


def clear_border(ref):
    blank = jnp.zeros((PAD,) + ref.shape[2:], ref.dtype)
    ref[0] = blank
    ref[PAD - 1] = blank
    for row in range(1, PAD - 1):
        ref[row, 0] = blank[0]
        ref[row, PAD - 1] = blank[0]


def taps_of(ref, begin, end, flip):
    boxes, channels = ref.shape[2:]
    pieces = []
    for s in range(3):
        for t in range(3):
            s0, t0 = (2 - s, 2 - t) if flip else (s, t)
            part = ref[begin + s0 : end + s0, t0 : t0 + CROP]
            pieces.append(part.reshape((end - begin) * CROP * boxes, channels))
    return pieces


def box_columns(values, shape, axis):
    index = lax.broadcasted_iota(jnp.int32, shape, axis)
    spread = jnp.zeros(shape, jnp.int32)
    for n, value in enumerate(values):
        spread = jnp.where(index == n, value, spread)
    return spread


def chain(product, finish, before_ref, stages):
    late = None
    count = 0
    for layer, source, target in stages:
        for begin in range(0, CROP, ROWS):
            end = min(begin + ROWS, CROP)
            before = before_ref.at[count % before_ref.shape[0]]
            count += 1
            before[: end - begin] = product(layer, source, begin, end).reshape(
                (end - begin,) + before.shape[1:]
            )
            if late is not None:
                late()
            late = functools.partial(finish, layer, before, target, begin, end)
    late()


def forward_kernel(
    geom_ref, count_ref, owner_ref, features_ref, weight_ref, mask_ref,
    send_ref, slope_ref,
    a_ref, b_ref, strip_ref, pick_ref, before_ref,
):
    _, boxes, tile_cols, channels = strip_ref.shape
    layers = weight_ref.shape[0]
    lanes = CROP * boxes
    count = count_ref[0, 0]
    clear_border(a_ref)
    clear_border(b_ref)
    shape = (boxes, boxes * tile_cols)
    lane = lax.broadcasted_iota(jnp.int32, shape, 1)
    start = box_columns([geom_ref[0, 0, 1, n] for n in range(boxes)], shape, 0)
    width = box_columns([geom_ref[0, 0, 3, n] for n in range(boxes)], shape, 0)
    mine = lane // tile_cols == lax.broadcasted_iota(jnp.int32, shape, 0)
    away = jnp.where(mine, lane % tile_cols - start, -1)
    away = jnp.where(away < width, away, -1)
    for v in range(CROP):
        pick_ref[v * boxes : (v + 1) * boxes, :] = (away == v).astype(jnp.bfloat16)
    for n in range(boxes):
        rows = features_ref[pl.ds(geom_ref[0, 0, 0, n], CROP)]
        tall = jnp.where(n < count, geom_ref[0, 0, 2, n], 0)
        for u in range(CROP):
            strip_ref[u, n] = jnp.where(u < tall, rows[u], jnp.zeros_like(rows[u]))
    for u in range(CROP):
        crop = jnp.dot(
            pick_ref[...], strip_ref[u].reshape(-1, channels), preferred_element_type=jnp.float32
        )
        a_ref[u + 1, 1 : 1 + CROP] = crop.astype(jnp.bfloat16).reshape(CROP, boxes, channels)

    def forward(layer, source, begin, end):
        return jnp.dot(
            jnp.concatenate(taps_of(source, begin, end, False), axis=1),
            weight_ref[layer],
            preferred_element_type=jnp.float32,
        )

    def activate(layer, before, target, begin, end):
        for u in range(begin, end):
            for v in range(CROP):
                piece = slice(v * boxes, (v + 1) * boxes)
                value, slope = gelu_parts(before[u - begin, piece])
                slope_ref[layer, u, piece] = slope.astype(jnp.bfloat16)
                target[u + 1, 1 + v] = value.astype(jnp.bfloat16)

    def up(pair, carry):
        stages = [(2 * pair, a_ref, b_ref), (2 * pair + 1, b_ref, a_ref)]
        chain(forward, activate, before_ref, stages)
        return carry

    lax.fori_loop(0, layers // 2, up, 0)
    vector = mask_ref[...].astype(jnp.float32).reshape(1, channels)
    place = lax.broadcasted_iota(jnp.int32, send_ref.shape, 1)
    sums = [jnp.zeros(send_ref.shape, jnp.float32) for _ in range(2)]
    for cell in range(CROP * CROP):
        u, v = divmod(cell, CROP)
        line = jnp.sum(a_ref[u + 1, v + 1].astype(jnp.float32) * vector, axis=-1, keepdims=True)
        sums[cell % 2] = jnp.where(place == cell, line, sums[cell % 2])
    owner = box_columns(
        [jnp.where(n < count, owner_ref[0, 0, n], -1) for n in range(boxes)], send_ref.shape, 0
    )
    send_ref[...] = jnp.where(
        place == CROP * CROP, owner.astype(jnp.float32), sums[0] + sums[1]
    )


def backward_kernel(
    geom_ref, count_ref, send_ref, soft_ref, slope_ref, weight_ref, mask_ref,
    grad_ref,
    a_ref, b_ref, spread_ref, place_ref, before_ref,
):
    boxes, channels = a_ref.shape[2:]
    tile_cols = grad_ref.shape[1]
    layers = weight_ref.shape[0]
    lanes = CROP * boxes
    cells = CROP * CROP
    count = count_ref[0, 0]
    clear_border(a_ref)
    clear_border(b_ref)
    broad = [geom_ref[0, 0, 3, n] for n in range(boxes)]
    tall = [jnp.where(n < count, geom_ref[0, 0, 2, n], 0) for n in range(boxes)]
    lane = lax.broadcasted_iota(jnp.int32, (tile_cols, lanes), 1)
    cell = lax.broadcasted_iota(jnp.int32, (tile_cols, lanes), 0)
    box, col = lane % boxes, lane // boxes
    for n in range(boxes):
        place_ref[n * tile_cols : (n + 1) * tile_cols, :] = (
            (cell == col + geom_ref[0, 0, 1, n]) & (box == n) & (col < broad[n])
        ).astype(jnp.bfloat16)
    shape = (boxes, cells)
    where = lax.broadcasted_iota(jnp.int32, shape, 1)
    inside = (where // CROP < box_columns(tall, shape, 0)) & (
        where % CROP < box_columns(broad, shape, 0)
    )
    soft = soft_ref[0, 0].astype(jnp.float32)
    lead = loss_scale * (jax.nn.sigmoid(send_ref[:, :cells]) - soft)
    lead = jnp.where(inside, lead, 0.0)
    vector = mask_ref[...].astype(jnp.float32).reshape(1, channels)
    for u in range(CROP):
        for v in range(CROP):
            piece = slice(v * boxes, (v + 1) * boxes)
            grad = lead[:, u * CROP + v : u * CROP + v + 1] * vector
            slope = slope_ref[layers - 1, u, piece].astype(jnp.float32)
            b_ref[u + 1, 1 + v] = (grad * slope).astype(jnp.bfloat16)

    def backward(layer, source, begin, end):
        total = None
        for tap, piece in enumerate(taps_of(source, begin, end, True)):
            part = lax.dot_general(
                piece,
                weight_ref[layer, tap * channels : (tap + 1) * channels, :],
                NT,
                preferred_element_type=jnp.float32,
            )
            total = part if total is None else total + part
        return total

    def descend(layer, before, target, begin, end):
        first = layer == 0
        for u in range(begin, end):
            for v in range(CROP):
                piece = slice(v * boxes, (v + 1) * boxes)
                slope = slope_ref[jnp.maximum(layer - 1, 0), u, piece].astype(jnp.float32)
                slope = jnp.where(first, 1.0, slope)
                target[u + 1, 1 + v] = (before[u - begin, piece] * slope).astype(jnp.bfloat16)

    def down(pair, carry):
        layer = layers - 1 - 2 * pair
        stages = [(layer, b_ref, a_ref), (layer - 1, a_ref, b_ref)]
        chain(backward, descend, before_ref, stages)
        return carry

    lax.fori_loop(0, layers // 2, down, 0)
    for u in range(CROP):
        spread_ref[u] = jnp.dot(
            place_ref[...],
            b_ref[u + 1, 1 : 1 + CROP].reshape(lanes, channels),
            preferred_element_type=jnp.float32,
        ).reshape(boxes, tile_cols, channels)
    grad_ref[...] = jnp.zeros_like(grad_ref)
    for n in range(boxes):
        kept = lax.broadcasted_iota(jnp.int32, (CROP, 1, 1), 0) < tall[n]
        rows = pl.ds(geom_ref[0, 0, 0, n], CROP)
        grad_ref[rows] = grad_ref[rows] + jnp.where(kept, spread_ref[:, n], 0.0)


def pair_kernel(own_ref, other_ref, out_ref):
    boxes = own_ref.shape[0]
    second = lax.axis_index("row") % 2
    out_ref[pl.ds(pl.multiple_of(second * boxes, boxes), boxes)] = own_ref[...]
    out_ref[pl.ds(pl.multiple_of((1 - second) * boxes, boxes), boxes)] = other_ref[...]


def join_pair(own, other):
    return pl.pallas_call(
        pair_kernel,
        out_shape=jax.ShapeDtypeStruct((2 * own.shape[0], own.shape[1]), own.dtype),
        in_specs=[VMEM, VMEM],
        out_specs=VMEM,
        compiler_params=pltpu.CompilerParams(vmem_limit_bytes=4 * 2**20),
        name="join_pair",
    )(own, other)


def collect_kernel(*refs):
    blocks, out_ref = refs[:-2], refs[-1]
    keep, cells = out_ref.shape[2:]
    pairs, rows = len(blocks), blocks[0].shape[0]
    sent = jnp.concatenate([ref[...] for ref in blocks], axis=0)
    me = lax.axis_index("row")
    mine = (sent[:, cells : cells + 1] == me.astype(jnp.float32)).astype(jnp.float32)

    def order(axis):
        index = lax.broadcasted_iota(jnp.int32, (pairs * rows, pairs * rows), axis)
        source = me // 2 - index // rows
        source = jnp.where(source < 0, source + pairs, source)
        return source * rows + index % rows

    earlier = (order(1) < order(0)).astype(jnp.float32).astype(jnp.bfloat16)
    many = jnp.broadcast_to(mine, (pairs * rows, 128)).astype(jnp.bfloat16)
    position = jnp.dot(earlier, many, preferred_element_type=jnp.float32)[:, :keep]
    slot = lax.broadcasted_iota(jnp.int32, (pairs * rows, keep), 1).astype(jnp.float32)
    picker = jnp.where(position == slot, mine, 0.0)
    out_ref[0, 0] = lax.dot_general(
        picker, sent[:, :cells], TN, precision=HIGHEST, preferred_element_type=jnp.float32
    )


def mask_cost(weight):
    return pl.CostEstimate(flops=25 * 10**9, bytes_accessed=2 * weight.size, transcendentals=0)


def mask_forward(features, geometry, count, owner, weight, mask):
    tile_rows, tile_cols, channels = features.shape
    boxes = geometry.shape[3]
    layers = weight.shape[0]
    lanes = CROP * boxes
    padded = pltpu.VMEM((PAD, PAD, boxes, channels), jnp.bfloat16)
    return pl.pallas_call(
        forward_kernel,
        out_shape=(
            jax.ShapeDtypeStruct((boxes, 256), jnp.float32),
            jax.ShapeDtypeStruct((layers, CROP, lanes, channels), jnp.bfloat16),
        ),
        in_specs=[SMEM, SMEM, SMEM, VMEM, VMEM, VMEM],
        out_specs=(VMEM, VMEM),
        scratch_shapes=[
            padded,
            padded,
            pltpu.VMEM((CROP, boxes, tile_cols, channels), jnp.bfloat16),
            pltpu.VMEM((lanes, boxes * tile_cols), jnp.bfloat16),
            pltpu.VMEM((3, ROWS, lanes, channels), jnp.float32),
        ],
        compiler_params=pltpu.CompilerParams(vmem_limit_bytes=FORWARD_MIB * 2**20),
        cost_estimate=mask_cost(weight),
        name="mask_forward",
    )(geometry, count, owner, features, weight, mask)


def mask_backward(send, soft, slope, geometry, count, weight, mask, tile):
    layers, _, lanes, channels = slope.shape
    boxes = geometry.shape[3]
    padded = pltpu.VMEM((PAD, PAD, boxes, channels), jnp.bfloat16)
    return pl.pallas_call(
        backward_kernel,
        out_shape=jax.ShapeDtypeStruct(tile + (channels,), jnp.float32),
        in_specs=[SMEM, SMEM, VMEM, VMEM, VMEM, VMEM, VMEM],
        out_specs=VMEM,
        scratch_shapes=[
            padded,
            padded,
            pltpu.VMEM((CROP, boxes, tile[1], channels), jnp.float32),
            pltpu.VMEM((boxes * tile[1], lanes), jnp.bfloat16),
            pltpu.VMEM((3, ROWS, lanes, channels), jnp.float32),
        ],
        compiler_params=pltpu.CompilerParams(vmem_limit_bytes=BACKWARD_MIB * 2**20),
        cost_estimate=mask_cost(weight),
        name="mask_backward",
    )(geometry, count, send, soft, slope, weight, mask)


def collect(blocks, after, keep, cells):
    return pl.pallas_call(
        collect_kernel,
        out_shape=jax.ShapeDtypeStruct((1, 1, keep, cells), jnp.float32),
        in_specs=[VMEM] * len(blocks) + [pl.BlockSpec(memory_space=pl.ANY)],
        out_specs=VMEM,
        compiler_params=pltpu.CompilerParams(vmem_limit_bytes=8 * 2**20),
        name="collect",
    )(*blocks, after)


HEADS = 12
WIN = 8
SUB = WIN // 2
CELL = SUB * SUB
AREA = WIN * WIN
GROUP = 4
EPSILON = 1e-05
BLOCKED = -1000000000.0


def norm_rows(values, gain):
    centered = values - jnp.mean(values, axis=-1, keepdims=True)
    variance = jnp.mean(centered * centered, axis=-1, keepdims=True)
    return (centered * lax.rsqrt(variance + EPSILON) * gain).astype(jnp.bfloat16)


def one_hot(equal, dtype=jnp.bfloat16):
    return equal.astype(jnp.float32).astype(dtype)


def strip_order(width):
    size = SUB * width
    cell_pos = lax.broadcasted_iota(jnp.int32, (size, size), 0)
    token = lax.broadcasted_iota(jnp.int32, (size, size), 1)
    cell, row, col = cell_pos // CELL, cell_pos // SUB % SUB, cell_pos % SUB
    return one_hot(token == row * width + cell * SUB + col)


def window_order():
    place = lax.broadcasted_iota(jnp.int32, (AREA, AREA), 0)
    token = lax.broadcasted_iota(jnp.int32, (AREA, AREA), 1)
    cell, row, col = place // CELL, place // SUB % SUB, place % SUB
    return one_hot(token == (cell // 2 * SUB + row) * WIN + cell % 2 * SUB + col, jnp.float32)


def head_blocks(lanes):
    row = lax.broadcasted_iota(jnp.int32, (GROUP * AREA, lanes), 0)
    col = lax.broadcasted_iota(jnp.int32, (GROUP * AREA, lanes), 1)
    return one_hot(row // AREA == col // (lanes // GROUP))


def attend(queries, key_rows, value_rows, bias, blocks, key_mask):
    lanes = blocks.shape[1]
    scale = (lanes // GROUP) ** (-0.5)
    first = lax.broadcasted_iota(jnp.int32, (1, 2 * AREA), 1) < AREA
    mixed = []
    for group in range(len(bias)):
        cut = slice(group * lanes, (group + 1) * lanes)
        keys = jnp.concatenate([key_rows[:, cut]] * GROUP, axis=0) * blocks
        values = jnp.concatenate([value_rows[:, cut]] * GROUP, axis=0) * blocks
        scores = lax.dot_general(queries[:, cut], keys, NT, preferred_element_type=jnp.float32)
        scores = scores * scale + bias[group]
        if key_mask is not None:
            scores = scores + key_mask
        weights = []
        for pair in range(GROUP // 2):
            part = scores[:, pair * 2 * AREA : (pair + 1) * 2 * AREA]
            low = jnp.max(jnp.where(first, part, -jnp.inf), axis=-1, keepdims=True)
            high = jnp.max(jnp.where(first, -jnp.inf, part), axis=-1, keepdims=True)
            weights.append(jnp.exp(part - jnp.where(first, low, high)))
        weights = jnp.concatenate(weights, axis=1).astype(jnp.bfloat16)
        both = jnp.dot(
            weights, jnp.concatenate([values, blocks], axis=1), preferred_element_type=jnp.float32
        )
        mixed.append((both[:, :lanes] / both[:, lanes:]).astype(jnp.bfloat16))
    return jnp.concatenate(mixed, axis=1)


def joint_kernel(
    tokens_ref, gain_ref, joint_ref,
    out_ref, ordered_ref, west_ref, east_ref, order_ref,
):
    cells_down, cells_across, _, model = ordered_ref.shape
    strip = order_ref.shape[0]
    order_ref[...] = strip_order(strip // SUB)
    gain = gain_ref[...].reshape(1, model)

    def body(step, carry):
        normed = []
        for part in range(2):
            down = 2 * step + part
            ordered = jnp.dot(
                order_ref[...],
                tokens_ref[pl.ds(down * SUB, SUB)].reshape(strip, model),
                preferred_element_type=jnp.float32,
            )
            ordered_ref[down] = ordered.astype(jnp.bfloat16).reshape(cells_across, CELL, model)
            normed.append(norm_rows(ordered, gain))
        out_ref[pl.ds(2 * step, 2)] = (
            jnp.dot(
                jnp.concatenate(normed, axis=0), joint_ref[...], preferred_element_type=jnp.float32
            )
            .astype(jnp.bfloat16)
            .reshape(2, cells_across, CELL, 3 * model)
        )
        return carry

    lax.fori_loop(0, cells_down // 2, body, 0)
    west_ref[...] = ordered_ref[:, 0]
    east_ref[...] = ordered_ref[:, cells_across - 1]


def inner_kernel(joint_ref, relative_ref, after_ref, out_ref, bias_ref):
    place = window_order()
    turned = lax.dot_general(
        relative_ref[...].reshape(-1, AREA), place, NT,
        precision=HIGHEST, preferred_element_type=jnp.float32,
    )
    for group in range(HEADS // GROUP):
        rows = [
            turned[(group * GROUP + h) * AREA : (group * GROUP + h + 1) * AREA]
            for h in range(GROUP)
        ]
        bias_ref[group] = jnp.dot(
            place,
            jnp.concatenate(rows, axis=1),
            precision=HIGHEST,
            preferred_element_type=jnp.float32,
        )
    cells_down, cells_across, _, triple = joint_ref.shape
    model = triple // 3
    blocks = head_blocks(GROUP * model // HEADS)
    bias = [bias_ref[group] for group in range(bias_ref.shape[0])]

    def body(i, carry):
        for j in range(cells_across // 2 - 1):
            rows = joint_ref[pl.ds(2 * i + 1, 2), 2 * j + 1 : 2 * j + 3].reshape(AREA, triple)
            mixed = attend(
                rows[:, :model], rows[:, model : 2 * model], rows[:, 2 * model :], bias, blocks, None
            )
            out_ref[pl.ds(2 * i + 1, 2), 2 * j + 1 : 2 * j + 3] = mixed.reshape(2, 2, CELL, model)
        return carry

    lax.fori_loop(0, cells_down // 2 - 1, body, 0)


def lengthen_kernel(
    up_ref, down_ref, west_ref, east_ref, up_out_ref, down_out_ref, west_out_ref, east_out_ref
):
    width = up_ref.shape[1]
    order = strip_order(width)
    for source, target in ((up_ref, up_out_ref), (down_ref, down_out_ref)):
        ordered = jnp.dot(
            order, source[...].reshape(SUB * width, -1), preferred_element_type=jnp.float32
        )
        target[...] = ordered.astype(jnp.bfloat16).reshape(target.shape)
    last = up_out_ref.shape[0] - 1
    for cell, own, out in ((0, west_ref, west_out_ref), (last, east_ref, east_out_ref)):
        out[0] = up_out_ref[cell]
        out[1:-1] = own[...]
        out[out.shape[0] - 1] = down_out_ref[cell]


def lengthen(up, down, west, east):
    across = jax.ShapeDtypeStruct((up.shape[1] // SUB, CELL, up.shape[2]), up.dtype)
    out = jax.ShapeDtypeStruct((west.shape[0] + 2,) + west.shape[1:], west.dtype)
    return pl.pallas_call(
        lengthen_kernel,
        out_shape=(across, across, out, out),
        in_specs=[VMEM] * 4,
        out_specs=(VMEM,) * 4,
        compiler_params=params(8),
        name="lengthen",
    )(up, down, west, east)


def hidden_keys(down_side, down_edge, across_side, across_edge):
    cell = lax.broadcasted_iota(jnp.int32, (1, GROUP * AREA), 1) // CELL % 4
    hidden = jnp.zeros((1, GROUP * AREA), jnp.bool_)
    if down_side is not None:
        hidden = hidden | ((cell // 2 == down_side) & down_edge)
    if across_side is not None:
        hidden = hidden | ((cell % 2 == across_side) & across_edge)
    return jnp.where(hidden, BLOCKED, 0.0)


def at_end(axis, side):
    return lax.axis_index(axis) == (lax.axis_size(axis) - 1 if side else 0)


def window_bias(bias_ref, cells):
    return [
        jnp.concatenate([bias_ref[g, c * CELL : (c + 1) * CELL] for c in cells], axis=0)
        for g in range(bias_ref.shape[0])
    ]


def halo_pairs(halo, gain, joint_ref):
    model = halo.shape[-1]
    normed = norm_rows(halo.astype(jnp.float32), gain)
    return jnp.dot(normed, joint_ref[:, model:], preferred_element_type=jnp.float32).astype(
        jnp.bfloat16
    )


def ends_kernel(joint_out_ref, up_ref, down_ref, bias_ref, gain_ref, joint_ref, pairs_ref, out_ref):
    cells_down, cells_across, _, triple = joint_out_ref.shape
    model = triple // 3
    blocks = head_blocks(GROUP * model // HEADS)
    gain = gain_ref[...].reshape(1, model)
    halo = jnp.concatenate([ref[...].reshape(-1, model) for ref in (up_ref, down_ref)], axis=0)
    pairs_ref[...] = halo_pairs(halo, gain, joint_ref).reshape(2, cells_across, CELL, 2 * model)
    for side in range(2):
        row = side * (cells_down - 1)
        bias = window_bias(bias_ref, [2 - 2 * side, 3 - 2 * side])
        key_mask = hidden_keys(side, at_end("row", side), None, None)
        for j in range(1, cells_across // 2):
            cut = slice(2 * j - 1, 2 * j + 1)
            own = joint_out_ref[row, cut].reshape(2 * CELL, triple)
            other = pairs_ref[side, cut].reshape(2 * CELL, 2 * model)
            both = [own[:, model:], other] if side else [other, own[:, model:]]
            both = jnp.concatenate(both, axis=0)
            mixed = attend(own[:, :model], both[:, :model], both[:, model:], bias, blocks, key_mask)
            out_ref[side, cut] = mixed.reshape(2, CELL, model)


def sides_kernel(
    ordered_ref, joint_out_ref, inner_ref, pairs_ref, ends_ref, left_ref, right_ref,
    bias_ref, first_ref, second_ref, joint_ref, merge_ref, expand_ref, shrink_ref, lateral_ref,
    features_ref, copy_ref, mixed_ref, halo_ref, order_ref, residual_ref, normed_ref, wide_ref, hidden_ref,
):
    cells_down, cells_across, _, triple = joint_out_ref.shape
    model = triple // 3
    strip = cells_across * CELL
    order_ref[...] = strip_order(cells_across * SUB)
    blocks = head_blocks(GROUP * model // HEADS)
    halo = jnp.concatenate([ref[...].reshape(-1, model) for ref in (left_ref, right_ref)], axis=0)
    halo = halo_pairs(halo, first_ref[...].reshape(1, model), joint_ref)
    halo_ref[...] = halo.reshape(2, cells_down + 2, CELL, 2 * model)
    mixed_ref[1:-1, 1:-1] = inner_ref[1:-1, 1:-1]
    mixed_ref[0, 1:-1] = ends_ref[0, 1:-1]
    mixed_ref[cells_down - 1, 1:-1] = ends_ref[1, 1:-1]

    for across in range(2):
        col = across * (cells_across - 1)
        bias = window_bias(bias_ref, [1 - across, 3 - across])
        key_mask = hidden_keys(None, None, across, at_end("col", across))

        def keys(pieces):
            rows = []
            for own, other in pieces:
                rows += [own, other] if across else [other, own]
            return jnp.concatenate(rows, axis=0)

        for i in range(1, cells_down // 2):
            cells = [2 * i - 1, 2 * i]
            both = keys(
                [(joint_out_ref[c, col, :, model:], halo_ref[across, c + 1]) for c in cells]
            )
            queries = jnp.concatenate([joint_out_ref[c, col, :, :model] for c in cells], axis=0)
            mixed = attend(queries, both[:, :model], both[:, model:], bias, blocks, key_mask)
            for place, c in enumerate(cells):
                mixed_ref[c, col] = mixed[place * CELL : (place + 1) * CELL]
        for down in range(2):
            row = down * (cells_down - 1)
            near = (joint_out_ref[row, col, :, model:], halo_ref[across, row + 1])
            far = (pairs_ref[down, col], halo_ref[across, down * (cells_down + 1)])
            both = keys([near, far] if down else [far, near])
            mixed_ref[row, col] = attend(
                joint_out_ref[row, col, :, :model], both[:, :model], both[:, model:],
                window_bias(bias_ref, [3 - 2 * down - across]), blocks,
                hidden_keys(down, at_end("row", down), across, at_end("col", across)),
            )

    second = second_ref[...].reshape(1, model)
    rows = hidden_ref.shape[1]
    group = rows // strip
    steps = cells_down // group

    def merge(step):
        residual = residual_ref.at[step % 2]
        cells = slice(step * group, (step + 1) * group)
        residual[...] = jnp.dot(
            mixed_ref[cells].reshape(rows, model), merge_ref[...], preferred_element_type=jnp.float32
        )
        for part in range(0, rows, PART):
            cut = slice(part, part + PART)
            c, a = divmod(part // CELL, cells_across)
            own = ordered_ref[step * group + c, a : a + PART // CELL].reshape(PART, model)
            total = residual[cut] + own.astype(jnp.float32)
            residual[cut] = total
            normed_ref[step % 2, cut] = norm_rows(total, second)

    def expand(step):
        wide_ref[step % 2] = jnp.dot(
            normed_ref[step % 2], expand_ref[...], preferred_element_type=jnp.float32
        )

    def activate(step):
        for part in range(0, rows, CELL):
            cut = slice(part, part + CELL)
            for lane in range(0, wide_ref.shape[2], 512):
                hidden_ref[step % 2, cut, lane : lane + 512] = gelu_value(
                    wide_ref[step % 2, cut, lane : lane + 512]
                ).astype(jnp.bfloat16)

    def shrink(step):
        block_out = residual_ref[step % 2] + jnp.dot(
            hidden_ref[step % 2], shrink_ref[...], preferred_element_type=jnp.float32
        )
        features = jnp.dot(
            block_out.astype(jnp.bfloat16), lateral_ref[...], preferred_element_type=jnp.float32
        ).astype(jnp.bfloat16)
        for part in range(group):
            natural = lax.dot_general(
                order_ref[...], features[part * strip : (part + 1) * strip], TN,
                preferred_element_type=jnp.float32,
            ).astype(jnp.bfloat16)
            first = (step * group + part) * SUB
            natural = natural.reshape((SUB,) + features_ref.shape[1:])
            features_ref[first : first + SUB] = natural
            copy_ref[first : first + SUB] = natural

    merge(0)
    expand(0)
    for step in range(steps):
        if step + 1 < steps:
            merge(step + 1)
        activate(step)
        if step + 1 < steps:
            expand(step + 1)
        shrink(step)


PART = 64


def params(mebibytes):
    return pltpu.CompilerParams(vmem_limit_bytes=mebibytes * 2**20)


def cells_of(count_down, count_across, channels, dtype=jnp.bfloat16):
    return jax.ShapeDtypeStruct((count_down, count_across, CELL, channels), dtype)


def joint_rows(tokens, gain, weight):
    tile_rows, tile_cols, model = tokens.shape
    down, across = tile_rows // SUB, tile_cols // SUB
    lone = lambda n: jax.ShapeDtypeStruct((n, CELL, model), jnp.bfloat16)
    return pl.pallas_call(
        joint_kernel,
        out_shape=(
            cells_of(down, across, weight.shape[1]),
            cells_of(down, across, model),
            lone(down), lone(down),
        ),
        in_specs=[VMEM] * 3,
        out_specs=(VMEM,) * 4,
        scratch_shapes=[
            pltpu.VMEM((SUB * tile_cols, SUB * tile_cols), jnp.bfloat16),
        ],
        compiler_params=params(20),
        cost_estimate=cost(tokens.shape[0] * tile_cols, model * weight.shape[1]),
        name="joint_rows",
    )(tokens, gain, weight)


def cost(rows, weights):
    return pl.CostEstimate(flops=4 * rows * weights, bytes_accessed=4 * 2**20, transcendentals=0)


def inner_windows(joint, relative, after):
    return pl.pallas_call(
        inner_kernel,
        out_shape=(
            jax.ShapeDtypeStruct(joint.shape[:3] + (joint.shape[3] // 3,), jnp.bfloat16),
            jax.ShapeDtypeStruct((HEADS // GROUP, AREA, GROUP * AREA), jnp.float32),
        ),
        in_specs=[VMEM, VMEM, pl.BlockSpec(memory_space=pl.ANY)],
        out_specs=(VMEM, VMEM),
        compiler_params=params(20),
        cost_estimate=cost(joint.shape[0] * joint.shape[1] * CELL, 2**19),
        name="inner_windows",
    )(joint, relative, after)


def end_windows(joint, up, down, bias, gain, weight):
    _, across, _, triple = joint.shape
    return pl.pallas_call(
        ends_kernel,
        out_shape=(cells_of(2, across, triple * 2 // 3), cells_of(2, across, triple // 3)),
        in_specs=[VMEM] * 6,
        out_specs=(VMEM, VMEM),
        compiler_params=params(20),
        cost_estimate=cost(joint.shape[0] * joint.shape[1] * CELL, 2**19),
        name="end_windows",
    )(joint, up, down, bias, gain, weight)


def side_windows(ordered, joint, inner, pairs, ends, left, right, bias, gains, weights):
    down, across, _, triple = joint.shape
    model = triple // 3
    strip = CELL * across
    rows = 2 * strip
    wide = weights[2].shape[1]
    tile = jax.ShapeDtypeStruct((down * SUB, across * SUB, weights[-1].shape[1]), jnp.bfloat16)
    return pl.pallas_call(
        sides_kernel,
        out_shape=(tile, tile),
        in_specs=[VMEM] * 15,
        out_specs=(VMEM, VMEM),
        scratch_shapes=[
            pltpu.VMEM((down, across, CELL, model), jnp.bfloat16),
            pltpu.VMEM((2, down + 2, CELL, 2 * model), jnp.bfloat16),
            pltpu.VMEM((strip, strip), jnp.bfloat16),
            pltpu.VMEM((2, rows, model), jnp.float32),
            pltpu.VMEM((2, rows, model), jnp.bfloat16),
            pltpu.VMEM((2, rows, wide), jnp.float32),
            pltpu.VMEM((2, rows, wide), jnp.bfloat16),
        ],
        compiler_params=params(28),
        name="side_windows",
    )(ordered, joint, inner, pairs, ends, left, right, bias, *gains, *weights)


BOX_OWN = 8


def shift(x, axis, step):
    size = lax.axis_size(axis)
    pairs = [(i, i + step) for i in range(size) if 0 <= i + step < size]
    return lax.ppermute(x, axis, pairs)


def shards(
    tokens, first_gain, second_gain, joint_weight, merge_weight, expand_weight, shrink_weight,
    relative_bias, lateral_weight, conv_weight, mask_weight, box_geometry, box_counts, box_owner,
    soft_target,
):
    tile_rows, tile_cols, model = tokens.shape
    up = shift(tokens[-SUB:], "row", 1)
    down = shift(tokens[:SUB], "row", -1)
    joint, ordered, west, east = joint_rows(tokens, first_gain, joint_weight)
    up, down, west, east = lengthen(up, down, west, east)
    left = shift(east, "col", 1)
    right = shift(west, "col", -1)
    inner, bias = inner_windows(joint, relative_bias, west)
    pairs, ends = end_windows(joint, up, down, bias, first_gain, joint_weight)
    features, features_here = side_windows(
        ordered, joint, inner, pairs, ends, left, right, bias, (first_gain, second_gain),
        (joint_weight, merge_weight, expand_weight, shrink_weight, lateral_weight),
    )
    rows_size = lax.axis_size("row")
    geometry = box_geometry.transpose(0, 1, 3, 2)
    send, slope = mask_forward(
        features_here, geometry, box_counts, box_owner, conv_weight, mask_weight
    )
    both = join_pair(send, lax.ppermute(send, "row", [(i, i ^ 1) for i in range(rows_size)]))
    blocks = [both]
    for back in range(2, rows_size, 2):
        blocks.append(
            lax.ppermute(both, "row", [(i, (i + back) % rows_size) for i in range(rows_size)])
        )
    feature_grad = mask_backward(
        send, soft_target, slope, geometry, box_counts, conv_weight, mask_weight,
        (tile_rows, tile_cols),
    )
    return features, feature_grad, collect(blocks, feature_grad, BOX_OWN, CROP * CROP)


def solution(mesh):
    tile = P("row", "col", None)
    placed = (tile,) + (P(),) * 10 + (
        P("row", "col", None, None), P("row", "col"), tile, P("row", "col", None, None),
    )
    return jax.shard_map(
        shards,
        mesh=mesh,
        in_specs=placed,
        out_specs=(tile, tile, P("row", "col", None, None)),
        check_vma=False,
    )
```

```python
import functools
import jax
import jax.numpy as jnp
from jax import lax
from jax.experimental import pallas as pl
from jax.experimental.pallas import tpu as pltpu
from jax.sharding import PartitionSpec as P

CROP = 14
ROWS = 2
FORWARD_MIB = 16
BACKWARD_MIB = 20
PAD = CROP + 2
GELU_A = 0.7978845608028654
GELU_B = 0.044715
loss_scale = 128.0
NT = (((1,), (1,)), ((), ()))
HIGHEST = lax.Precision.HIGHEST
TN = (((0,), (0,)), ((), ()))
VMEM = pl.BlockSpec(memory_space=pltpu.VMEM)
SMEM = pl.BlockSpec(memory_space=pltpu.SMEM)


def gelu_parts(x):
    square = x * x
    tanh = jnp.tanh(x * (GELU_A + (GELU_A * GELU_B) * square))
    above = 1.0 + tanh
    value = x * above
    rate = GELU_A + (3.0 * GELU_A * GELU_B) * square
    return 0.5 * value, above + value * (1.0 - tanh) * rate


def gelu_twice(x):
    return x * (1.0 + jnp.tanh(x * (GELU_A + (GELU_A * GELU_B) * (x * x))))


def clear_border(ref):
    blank = jnp.zeros((PAD,) + ref.shape[2:], ref.dtype)
    ref[0] = blank
    ref[PAD - 1] = blank
    for row in range(1, PAD - 1):
        ref[row, 0] = blank[0]
        ref[row, PAD - 1] = blank[0]


def tap_of(ref, begin, end, tap, flip):
    boxes, channels = ref.shape[2:]
    s, t = divmod(tap, 3)
    if flip:
        s, t = 2 - s, 2 - t
    part = ref[begin + s : end + s, t : t + CROP]
    return part.reshape((end - begin) * CROP * boxes, channels)


def box_columns(values, shape, axis):
    index = lax.broadcasted_iota(jnp.int32, shape, axis)
    spread = jnp.zeros(shape, jnp.int32)
    for n, value in enumerate(values):
        spread = jnp.where(index == n, value, spread)
    return spread


def chain(product, finish, before_ref, stages):
    late = []
    count = 0
    for layer, source, target in stages:
        for begin in range(0, CROP, ROWS):
            end = min(begin + ROWS, CROP)
            before = before_ref.at[count % before_ref.shape[0]]
            count += 1
            total = product(layer, source, begin, end)
            before[: end - begin] = total.reshape((end - begin,) + before.shape[1:])
            for piece in late:
                piece()
            late = [
                functools.partial(finish, layer, before.at[u - begin], target, u, v)
                for u in range(begin, end)
                for v in range(CROP)
            ]
    for piece in late:
        piece()


def forward_kernel(
    geom_ref, count_ref, owner_ref, features_ref, weight_ref, mask_ref,
    send_ref, slope_ref,
    a_ref, b_ref, strip_ref, pick_ref, before_ref,
):
    _, boxes, tile_cols, channels = strip_ref.shape
    layers = weight_ref.shape[0]
    lanes = CROP * boxes
    count = count_ref[0, 0]
    clear_border(a_ref)
    clear_border(b_ref)
    shape = (boxes, boxes * tile_cols)
    lane = lax.broadcasted_iota(jnp.int32, shape, 1)
    start = box_columns([geom_ref[0, 0, 1, n] for n in range(boxes)], shape, 0)
    width = box_columns([geom_ref[0, 0, 3, n] for n in range(boxes)], shape, 0)
    mine = lane // tile_cols == lax.broadcasted_iota(jnp.int32, shape, 0)
    away = jnp.where(mine, lane % tile_cols - start, -1)
    away = jnp.where(away < width, away, -1)
    for v in range(CROP):
        pick_ref[v * boxes : (v + 1) * boxes, :] = (away == v).astype(jnp.bfloat16)
    for n in range(boxes):
        rows = features_ref[pl.ds(geom_ref[0, 0, 0, n], CROP)]
        tall = jnp.where(n < count, geom_ref[0, 0, 2, n], 0)
        for u in range(CROP):
            strip_ref[u, n] = jnp.where(u < tall, rows[u], jnp.zeros_like(rows[u]))
    for u in range(CROP):
        crop = jnp.dot(
            pick_ref[...], strip_ref[u].reshape(-1, channels), preferred_element_type=jnp.float32
        )
        a_ref[u + 1, 1 : 1 + CROP] = crop.astype(jnp.bfloat16).reshape(CROP, boxes, channels)

    def forward(layer, source, begin, end):
        return jnp.dot(
            jnp.concatenate([tap_of(source, begin, end, tap, False) for tap in range(9)], axis=1),
            weight_ref[layer],
            preferred_element_type=jnp.float32,
        )

    def activate(layer, before, target, u, v):
        piece = slice(v * boxes, (v + 1) * boxes)
        value, slope = gelu_parts(before[piece])
        slope_ref[layer, u, piece] = slope.astype(jnp.bfloat16)
        target[u + 1, 1 + v] = value.astype(jnp.bfloat16)

    def up(pair, carry):
        stages = [(2 * pair, a_ref, b_ref), (2 * pair + 1, b_ref, a_ref)]
        chain(forward, activate, before_ref, stages)
        return carry

    lax.fori_loop(0, layers // 2, up, 0)
    vector = jnp.broadcast_to(
        mask_ref[...].astype(jnp.float32).reshape(1, channels), (128, channels)
    ).astype(jnp.bfloat16)
    place = lax.broadcasted_iota(jnp.int32, send_ref.shape, 1)
    lane = lax.broadcasted_iota(jnp.int32, (boxes, 128), 1)
    halves = [jnp.zeros((boxes, 128), jnp.float32) for _ in range(2)]
    for u in range(CROP):
        lines = lax.dot_general(
            a_ref[u + 1, 1 : 1 + CROP].reshape(lanes, channels), vector, NT,
            preferred_element_type=jnp.float32,
        )
        for v in range(CROP):
            half, cell = divmod(u * CROP + v, 128)
            halves[half] = jnp.where(
                lane == cell, lines[v * boxes : (v + 1) * boxes], halves[half]
            )
    owner = box_columns(
        [jnp.where(n < count, owner_ref[0, 0, n], -1) for n in range(boxes)], send_ref.shape, 0
    )
    send_ref[...] = jnp.where(
        place == CROP * CROP, owner.astype(jnp.float32), jnp.concatenate(halves, axis=1)
    )


def backward_kernel(
    geom_ref, count_ref, send_ref, soft_ref, slope_ref, weight_ref, mask_ref,
    grad_ref, done_ref,
    a_ref, b_ref, spread_ref, place_ref, before_ref,
):
    done_ref[...] = jnp.zeros_like(done_ref)
    boxes, channels = a_ref.shape[2:]
    tile_cols = grad_ref.shape[1]
    layers = weight_ref.shape[0]
    lanes = CROP * boxes
    cells = CROP * CROP
    count = count_ref[0, 0]
    clear_border(a_ref)
    clear_border(b_ref)
    broad = [geom_ref[0, 0, 3, n] for n in range(boxes)]
    tall = [jnp.where(n < count, geom_ref[0, 0, 2, n], 0) for n in range(boxes)]
    lane = lax.broadcasted_iota(jnp.int32, (tile_cols, lanes), 1)
    cell = lax.broadcasted_iota(jnp.int32, (tile_cols, lanes), 0)
    box, col = lane % boxes, lane // boxes
    for n in range(boxes):
        place_ref[n * tile_cols : (n + 1) * tile_cols, :] = (
            (cell == col + geom_ref[0, 0, 1, n]) & (box == n) & (col < broad[n])
        ).astype(jnp.bfloat16)
    shape = (boxes, cells)
    where = lax.broadcasted_iota(jnp.int32, shape, 1)
    inside = (where // CROP < box_columns(tall, shape, 0)) & (
        where % CROP < box_columns(broad, shape, 0)
    )
    soft = soft_ref[0, 0].astype(jnp.float32)
    lead = loss_scale * 0.5**layers * (jax.nn.sigmoid(send_ref[:, :cells]) - soft)
    lead = jnp.where(inside, lead, 0.0)
    vector = mask_ref[...].astype(jnp.float32).reshape(1, channels)
    for u in range(CROP):
        for v in range(CROP):
            piece = slice(v * boxes, (v + 1) * boxes)
            grad = lead[:, u * CROP + v : u * CROP + v + 1] * vector
            slope = slope_ref[layers - 1, u, piece].astype(jnp.float32)
            b_ref[u + 1, 1 + v] = (grad * slope).astype(jnp.bfloat16)

    def backward(layer, source, begin, end):
        total = None
        for tap in range(9):
            part = lax.dot_general(
                tap_of(source, begin, end, tap, True),
                weight_ref[layer, tap * channels : (tap + 1) * channels, :],
                NT,
                preferred_element_type=jnp.float32,
            )
            total = part if total is None else total + part
        return total

    def descend(layer, before, target, u, v):
        piece = slice(v * boxes, (v + 1) * boxes)
        slope = slope_ref[jnp.maximum(layer - 1, 0), u, piece].astype(jnp.float32)
        slope = jnp.where(layer == 0, 1.0, slope)
        target[u + 1, 1 + v] = (before[piece] * slope).astype(jnp.bfloat16)

    def down(pair, carry):
        layer = layers - 1 - 2 * pair
        stages = [(layer, b_ref, a_ref), (layer - 1, a_ref, b_ref)]
        chain(backward, descend, before_ref, stages)
        return carry

    lax.fori_loop(0, layers // 2, down, 0)
    for u in range(CROP):
        spread_ref[u] = jnp.dot(
            place_ref[...],
            b_ref[u + 1, 1 : 1 + CROP].reshape(lanes, channels),
            preferred_element_type=jnp.float32,
        ).astype(jnp.bfloat16).reshape(boxes, tile_cols, channels)
    grad_ref[...] = jnp.zeros_like(grad_ref)
    for n in range(boxes):
        kept = lax.broadcasted_iota(jnp.int32, (CROP, 1, 1), 0) < tall[n]
        rows = pl.ds(geom_ref[0, 0, 0, n], CROP)
        grad_ref[rows] = grad_ref[rows] + jnp.where(kept, spread_ref[:, n].astype(jnp.float32), 0.0)


def pair_kernel(own_ref, other_ref, out_ref):
    boxes = own_ref.shape[0]
    second = lax.axis_index("row") % 2
    out_ref[pl.ds(pl.multiple_of(second * boxes, boxes), boxes)] = own_ref[...]
    out_ref[pl.ds(pl.multiple_of((1 - second) * boxes, boxes), boxes)] = other_ref[...]


def join_pair(own, other):
    return pl.pallas_call(
        pair_kernel,
        out_shape=jax.ShapeDtypeStruct((2 * own.shape[0], own.shape[1]), own.dtype),
        in_specs=[VMEM, VMEM],
        out_specs=VMEM,
        compiler_params=pltpu.CompilerParams(vmem_limit_bytes=4 * 2**20),
        name="join_pair",
    )(own, other)


def collect_kernel(*refs):
    blocks, out_ref = refs[:-2], refs[-1]
    keep, cells = out_ref.shape[2:]
    pairs, rows = len(blocks), blocks[0].shape[0]
    sent = jnp.concatenate([ref[...] for ref in blocks], axis=0)
    me = lax.axis_index("row")
    mine = (sent[:, cells : cells + 1] == me.astype(jnp.float32)).astype(jnp.float32)

    def order(axis):
        index = lax.broadcasted_iota(jnp.int32, (pairs * rows, pairs * rows), axis)
        source = me // 2 - index // rows
        source = jnp.where(source < 0, source + pairs, source)
        return source * rows + index % rows

    earlier = (order(1) < order(0)).astype(jnp.float32).astype(jnp.bfloat16)
    many = jnp.broadcast_to(mine, (pairs * rows, 128)).astype(jnp.bfloat16)
    position = jnp.dot(earlier, many, preferred_element_type=jnp.float32)[:, :keep]
    slot = lax.broadcasted_iota(jnp.int32, (pairs * rows, keep), 1).astype(jnp.float32)
    picker = jnp.where(position == slot, mine, 0.0)
    out_ref[0, 0] = lax.dot_general(
        picker, sent[:, :cells], TN, precision=HIGHEST, preferred_element_type=jnp.float32
    )


def mask_cost(weight):
    return pl.CostEstimate(flops=25 * 10**9, bytes_accessed=2 * weight.size, transcendentals=0)


def mask_forward(features, geometry, count, owner, weight, mask):
    tile_rows, tile_cols, channels = features.shape
    boxes = geometry.shape[3]
    layers = weight.shape[0]
    lanes = CROP * boxes
    padded = pltpu.VMEM((PAD, PAD, boxes, channels), jnp.bfloat16)
    return pl.pallas_call(
        forward_kernel,
        out_shape=(
            jax.ShapeDtypeStruct((boxes, 256), jnp.float32),
            jax.ShapeDtypeStruct((layers, CROP, lanes, channels), jnp.bfloat16),
        ),
        in_specs=[SMEM, SMEM, SMEM, VMEM, VMEM, VMEM],
        out_specs=(VMEM, VMEM),
        scratch_shapes=[
            padded,
            padded,
            pltpu.VMEM((CROP, boxes, tile_cols, channels), jnp.bfloat16),
            pltpu.VMEM((lanes, boxes * tile_cols), jnp.bfloat16),
            pltpu.VMEM((3, ROWS, lanes, channels), jnp.float32),
        ],
        compiler_params=pltpu.CompilerParams(vmem_limit_bytes=FORWARD_MIB * 2**20),
        cost_estimate=mask_cost(weight),
        name="mask_forward",
    )(geometry, count, owner, features, weight, mask)


def mask_backward(send, soft, slope, geometry, count, weight, mask, tile):
    layers, _, lanes, channels = slope.shape
    boxes = geometry.shape[3]
    padded = pltpu.VMEM((PAD, PAD, boxes, channels), jnp.bfloat16)
    return pl.pallas_call(
        backward_kernel,
        out_shape=(
            jax.ShapeDtypeStruct(tile + (channels,), jnp.float32),
            jax.ShapeDtypeStruct((8, 128), jnp.float32),
        ),
        in_specs=[SMEM, SMEM, VMEM, VMEM, VMEM, VMEM, VMEM],
        out_specs=(VMEM, VMEM),
        scratch_shapes=[
            padded,
            padded,
            pltpu.VMEM((CROP, boxes, tile[1], channels), jnp.bfloat16),
            pltpu.VMEM((boxes * tile[1], lanes), jnp.bfloat16),
            pltpu.VMEM((3, ROWS, lanes, channels), jnp.float32),
        ],
        compiler_params=pltpu.CompilerParams(vmem_limit_bytes=BACKWARD_MIB * 2**20),
        cost_estimate=mask_cost(weight),
        name="mask_backward",
    )(geometry, count, send, soft, slope, weight, mask)


def collect(blocks, after, keep, cells):
    return pl.pallas_call(
        collect_kernel,
        out_shape=jax.ShapeDtypeStruct((1, 1, keep, cells), jnp.float32),
        in_specs=[VMEM] * len(blocks) + [pl.BlockSpec(memory_space=pl.ANY)],
        out_specs=VMEM,
        compiler_params=pltpu.CompilerParams(vmem_limit_bytes=8 * 2**20),
        name="collect",
    )(*blocks, after)


HEADS = 12
WIN = 8
SUB = WIN // 2
CELL = SUB * SUB
AREA = WIN * WIN
GROUP = 4
EPSILON = 1e-05
BLOCKED = -1000000000.0


def norm_rows(values, gain):
    centered = values - jnp.mean(values, axis=-1, keepdims=True)
    variance = jnp.mean(centered * centered, axis=-1, keepdims=True)
    return (centered * lax.rsqrt(variance + EPSILON) * gain).astype(jnp.bfloat16)


def one_hot(equal, dtype=jnp.bfloat16):
    return equal.astype(jnp.float32).astype(dtype)


def strip_order(width):
    size = SUB * width
    cell_pos = lax.broadcasted_iota(jnp.int32, (size, size), 0)
    token = lax.broadcasted_iota(jnp.int32, (size, size), 1)
    cell, row, col = cell_pos // CELL, cell_pos // SUB % SUB, cell_pos % SUB
    return one_hot(token == row * width + cell * SUB + col)


def window_order():
    place = lax.broadcasted_iota(jnp.int32, (AREA, AREA), 0)
    token = lax.broadcasted_iota(jnp.int32, (AREA, AREA), 1)
    cell, row, col = place // CELL, place // SUB % SUB, place % SUB
    return one_hot(token == (cell // 2 * SUB + row) * WIN + cell % 2 * SUB + col, jnp.float32)


def head_blocks(lanes):
    row = lax.broadcasted_iota(jnp.int32, (GROUP * AREA, lanes), 0)
    col = lax.broadcasted_iota(jnp.int32, (GROUP * AREA, lanes), 1)
    return one_hot(row // AREA == col // (lanes // GROUP))


def attend(queries, key_rows, value_rows, bias, blocks, key_mask):
    lanes = blocks.shape[1]
    scale = (lanes // GROUP) ** (-0.5)
    first = lax.broadcasted_iota(jnp.int32, (1, 2 * AREA), 1) < AREA
    mixed = []
    for group in range(len(bias)):
        cut = slice(group * lanes, (group + 1) * lanes)
        keys = jnp.concatenate([key_rows[:, cut]] * GROUP, axis=0) * blocks
        values = jnp.concatenate([value_rows[:, cut]] * GROUP, axis=0) * blocks
        scores = lax.dot_general(queries[:, cut], keys, NT, preferred_element_type=jnp.float32)
        scores = scores * scale + bias[group]
        if key_mask is not None:
            scores = scores + key_mask
        weights = []
        for pair in range(GROUP // 2):
            part = scores[:, pair * 2 * AREA : (pair + 1) * 2 * AREA]
            low = jnp.max(jnp.where(first, part, -jnp.inf), axis=-1, keepdims=True)
            high = jnp.max(jnp.where(first, -jnp.inf, part), axis=-1, keepdims=True)
            weights.append(jnp.exp(part - jnp.where(first, low, high)))
        weights = jnp.concatenate(weights, axis=1).astype(jnp.bfloat16)
        both = jnp.dot(
            weights, jnp.concatenate([values, blocks], axis=1), preferred_element_type=jnp.float32
        )
        mixed.append((both[:, :lanes] / both[:, lanes:]).astype(jnp.bfloat16))
    return jnp.concatenate(mixed, axis=1)


def joint_kernel(
    tokens_ref, gain_ref, joint_ref,
    out_ref, ordered_ref, west_ref, east_ref, order_ref,
):
    cells_down, cells_across, _, model = ordered_ref.shape
    strip = order_ref.shape[0]
    order_ref[...] = strip_order(strip // SUB)
    gain = gain_ref[...].reshape(1, model)

    def body(step, carry):
        normed = []
        for part in range(2):
            down = 2 * step + part
            ordered = jnp.dot(
                order_ref[...],
                tokens_ref[pl.ds(down * SUB, SUB)].reshape(strip, model),
                preferred_element_type=jnp.float32,
            )
            ordered_ref[down] = ordered.astype(jnp.bfloat16).reshape(cells_across, CELL, model)
            normed.append(norm_rows(ordered, gain))
        out_ref[pl.ds(2 * step, 2)] = (
            jnp.dot(
                jnp.concatenate(normed, axis=0), joint_ref[...], preferred_element_type=jnp.float32
            )
            .astype(jnp.bfloat16)
            .reshape(2, cells_across, CELL, 3 * model)
        )
        return carry

    lax.fori_loop(0, cells_down // 2, body, 0)
    west_ref[...] = ordered_ref[:, 0]
    east_ref[...] = ordered_ref[:, cells_across - 1]


def inner_kernel(joint_ref, relative_ref, after_ref, out_ref, bias_ref):
    place = window_order()
    turned = lax.dot_general(
        relative_ref[...].reshape(-1, AREA), place, NT,
        precision=HIGHEST, preferred_element_type=jnp.float32,
    )
    for group in range(HEADS // GROUP):
        rows = [
            turned[(group * GROUP + h) * AREA : (group * GROUP + h + 1) * AREA]
            for h in range(GROUP)
        ]
        bias_ref[group] = jnp.dot(
            place,
            jnp.concatenate(rows, axis=1),
            precision=HIGHEST,
            preferred_element_type=jnp.float32,
        )
    cells_down, cells_across, _, triple = joint_ref.shape
    model = triple // 3
    blocks = head_blocks(GROUP * model // HEADS)
    bias = [bias_ref[group] for group in range(bias_ref.shape[0])]

    def body(i, carry):
        for j in range(cells_across // 2 - 1):
            rows = joint_ref[pl.ds(2 * i + 1, 2), 2 * j + 1 : 2 * j + 3].reshape(AREA, triple)
            mixed = attend(
                rows[:, :model], rows[:, model : 2 * model], rows[:, 2 * model :], bias, blocks, None
            )
            out_ref[pl.ds(2 * i + 1, 2), 2 * j + 1 : 2 * j + 3] = mixed.reshape(2, 2, CELL, model)
        return carry

    lax.fori_loop(0, cells_down // 2 - 1, body, 0)


def lengthen_kernel(
    up_ref, down_ref, west_ref, east_ref, up_out_ref, down_out_ref, west_out_ref, east_out_ref
):
    width = up_ref.shape[1]
    order = strip_order(width)
    for source, target in ((up_ref, up_out_ref), (down_ref, down_out_ref)):
        ordered = jnp.dot(
            order, source[...].reshape(SUB * width, -1), preferred_element_type=jnp.float32
        )
        target[...] = ordered.astype(jnp.bfloat16).reshape(target.shape)
    last = up_out_ref.shape[0] - 1
    for cell, own, out in ((0, west_ref, west_out_ref), (last, east_ref, east_out_ref)):
        out[0] = up_out_ref[cell]
        out[1:-1] = own[...]
        out[out.shape[0] - 1] = down_out_ref[cell]


def lengthen(up, down, west, east):
    across = jax.ShapeDtypeStruct((up.shape[1] // SUB, CELL, up.shape[2]), up.dtype)
    out = jax.ShapeDtypeStruct((west.shape[0] + 2,) + west.shape[1:], west.dtype)
    return pl.pallas_call(
        lengthen_kernel,
        out_shape=(across, across, out, out),
        in_specs=[VMEM] * 4,
        out_specs=(VMEM,) * 4,
        compiler_params=params(8),
        name="lengthen",
    )(up, down, west, east)


def hidden_keys(down_side, down_edge, across_side, across_edge):
    cell = lax.broadcasted_iota(jnp.int32, (1, GROUP * AREA), 1) // CELL % 4
    hidden = jnp.zeros((1, GROUP * AREA), jnp.bool_)
    if down_side is not None:
        hidden = hidden | ((cell // 2 == down_side) & down_edge)
    if across_side is not None:
        hidden = hidden | ((cell % 2 == across_side) & across_edge)
    return jnp.where(hidden, BLOCKED, 0.0)


def at_end(axis, side):
    return lax.axis_index(axis) == (lax.axis_size(axis) - 1 if side else 0)


def window_bias(bias_ref, cells):
    return [
        jnp.concatenate([bias_ref[g, c * CELL : (c + 1) * CELL] for c in cells], axis=0)
        for g in range(bias_ref.shape[0])
    ]


def halo_pairs(halo, gain, joint_ref):
    model = halo.shape[-1]
    normed = norm_rows(halo.astype(jnp.float32), gain)
    return jnp.dot(normed, joint_ref[:, model:], preferred_element_type=jnp.float32).astype(
        jnp.bfloat16
    )


def ends_kernel(joint_out_ref, up_ref, down_ref, bias_ref, gain_ref, joint_ref, pairs_ref, out_ref):
    cells_down, cells_across, _, triple = joint_out_ref.shape
    model = triple // 3
    blocks = head_blocks(GROUP * model // HEADS)
    gain = gain_ref[...].reshape(1, model)
    halo = jnp.concatenate([ref[...].reshape(-1, model) for ref in (up_ref, down_ref)], axis=0)
    pairs_ref[...] = halo_pairs(halo, gain, joint_ref).reshape(2, cells_across, CELL, 2 * model)
    for side in range(2):
        row = side * (cells_down - 1)
        bias = window_bias(bias_ref, [2 - 2 * side, 3 - 2 * side])
        key_mask = hidden_keys(side, at_end("row", side), None, None)
        for j in range(1, cells_across // 2):
            cut = slice(2 * j - 1, 2 * j + 1)
            own = joint_out_ref[row, cut].reshape(2 * CELL, triple)
            other = pairs_ref[side, cut].reshape(2 * CELL, 2 * model)
            both = [own[:, model:], other] if side else [other, own[:, model:]]
            both = jnp.concatenate(both, axis=0)
            mixed = attend(own[:, :model], both[:, :model], both[:, model:], bias, blocks, key_mask)
            out_ref[side, cut] = mixed.reshape(2, CELL, model)


def sides_kernel(
    ordered_ref, joint_out_ref, inner_ref, pairs_ref, ends_ref, left_ref, right_ref,
    bias_ref, first_ref, second_ref, joint_ref, merge_ref, expand_ref, shrink_ref, lateral_ref,
    features_ref, copy_ref, mixed_ref, halo_ref, order_ref, residual_ref, normed_ref, wide_ref, hidden_ref,
):
    cells_down, cells_across, _, triple = joint_out_ref.shape
    model = triple // 3
    strip = cells_across * CELL
    order_ref[...] = strip_order(cells_across * SUB)
    blocks = head_blocks(GROUP * model // HEADS)
    halo = jnp.concatenate([ref[...].reshape(-1, model) for ref in (left_ref, right_ref)], axis=0)
    halo = halo_pairs(halo, first_ref[...].reshape(1, model), joint_ref)
    halo_ref[...] = halo.reshape(2, cells_down + 2, CELL, 2 * model)
    mixed_ref[1:-1, 1:-1] = inner_ref[1:-1, 1:-1]
    mixed_ref[0, 1:-1] = ends_ref[0, 1:-1]
    mixed_ref[cells_down - 1, 1:-1] = ends_ref[1, 1:-1]

    for across in range(2):
        col = across * (cells_across - 1)
        bias = window_bias(bias_ref, [1 - across, 3 - across])
        key_mask = hidden_keys(None, None, across, at_end("col", across))

        def keys(pieces):
            rows = []
            for own, other in pieces:
                rows += [own, other] if across else [other, own]
            return jnp.concatenate(rows, axis=0)

        for i in range(1, cells_down // 2):
            cells = [2 * i - 1, 2 * i]
            both = keys(
                [(joint_out_ref[c, col, :, model:], halo_ref[across, c + 1]) for c in cells]
            )
            queries = jnp.concatenate([joint_out_ref[c, col, :, :model] for c in cells], axis=0)
            mixed = attend(queries, both[:, :model], both[:, model:], bias, blocks, key_mask)
            for place, c in enumerate(cells):
                mixed_ref[c, col] = mixed[place * CELL : (place + 1) * CELL]
        for down in range(2):
            row = down * (cells_down - 1)
            near = (joint_out_ref[row, col, :, model:], halo_ref[across, row + 1])
            far = (pairs_ref[down, col], halo_ref[across, down * (cells_down + 1)])
            both = keys([near, far] if down else [far, near])
            mixed_ref[row, col] = attend(
                joint_out_ref[row, col, :, :model], both[:, :model], both[:, model:],
                window_bias(bias_ref, [3 - 2 * down - across]), blocks,
                hidden_keys(down, at_end("row", down), across, at_end("col", across)),
            )

    second = second_ref[...].reshape(1, model)
    rows = hidden_ref.shape[1]
    group = rows // strip
    steps = cells_down // group

    def merge(step):
        residual = residual_ref.at[step % 3]
        cells = slice(step * group, (step + 1) * group)
        residual[...] = jnp.dot(
            mixed_ref[cells].reshape(rows, model), merge_ref[...], preferred_element_type=jnp.float32
        )

    def normalise(step, part):
        residual = residual_ref.at[step % 3]
        cut = slice(part, part + PART)
        c, a = divmod(part // CELL, cells_across)
        own = ordered_ref[step * group + c, a : a + PART // CELL].reshape(PART, model)
        total = residual[cut] + own.astype(jnp.float32)
        residual[cut] = total
        normed_ref[step % 2, cut] = norm_rows(total, second)

    def expand(step, lane):
        cut = slice(lane, lane + LANES)
        wide_ref[step % 2, :, cut] = jnp.dot(
            normed_ref[step % 2], expand_ref[:, cut], preferred_element_type=jnp.float32
        )

    def activate(step, lane):
        cut = slice(lane, lane + LANES)
        for part in range(0, rows, CELL):
            here = slice(part, part + CELL)
            hidden_ref[step % 2, here, cut] = gelu_twice(wide_ref[step % 2, here, cut]).astype(
                jnp.bfloat16
            )

    def shrink(step):
        block_out = residual_ref[step % 3] + 0.5 * jnp.dot(
            hidden_ref[step % 2], shrink_ref[...], preferred_element_type=jnp.float32
        )
        features = jnp.dot(
            block_out.astype(jnp.bfloat16), lateral_ref[...], preferred_element_type=jnp.float32
        ).astype(jnp.bfloat16)
        for part in range(group):
            natural = lax.dot_general(
                order_ref[...], features[part * strip : (part + 1) * strip], TN,
                preferred_element_type=jnp.float32,
            ).astype(jnp.bfloat16)
            first = (step * group + part) * SUB
            natural = natural.reshape((SUB,) + features_ref.shape[1:])
            features_ref[first : first + SUB] = natural
            copy_ref[first : first + SUB] = natural

    lanes = range(0, wide_ref.shape[2], LANES)
    for step in range(min(2, steps)):
        merge(step)
        for part in range(0, rows, PART):
            normalise(step, part)
        if step == 0:
            for lane in lanes:
                expand(0, lane)
    for step in range(steps):
        for lane in lanes:
            if step + 1 < steps:
                expand(step + 1, lane)
            activate(step, lane)
        if step + 2 < steps:
            merge(step + 2)
        shrink(step)
        if step + 2 < steps:
            for part in range(0, rows, PART):
                normalise(step + 2, part)


LANES = 256
PART = 64


def params(mebibytes):
    return pltpu.CompilerParams(vmem_limit_bytes=mebibytes * 2**20)


def cells_of(count_down, count_across, channels, dtype=jnp.bfloat16):
    return jax.ShapeDtypeStruct((count_down, count_across, CELL, channels), dtype)


def end_kernel(tokens_ref, first_ref, last_ref):
    first_ref[...] = tokens_ref[:SUB]
    last_ref[...] = tokens_ref[tokens_ref.shape[0] - SUB :]


def end_rows(tokens):
    out = jax.ShapeDtypeStruct((SUB,) + tokens.shape[1:], tokens.dtype)
    return pl.pallas_call(
        end_kernel,
        out_shape=(out, out),
        in_specs=[VMEM],
        out_specs=(VMEM, VMEM),
        compiler_params=params(4),
        cost_estimate=cost(tokens.shape[0] * tokens.shape[1], 2**20),
        name="end_rows",
    )(tokens)


def joint_rows(tokens, gain, weight):
    tile_rows, tile_cols, model = tokens.shape
    down, across = tile_rows // SUB, tile_cols // SUB
    lone = lambda n: jax.ShapeDtypeStruct((n, CELL, model), jnp.bfloat16)
    return pl.pallas_call(
        joint_kernel,
        out_shape=(
            cells_of(down, across, weight.shape[1]),
            cells_of(down, across, model),
            lone(down), lone(down),
        ),
        in_specs=[VMEM] * 3,
        out_specs=(VMEM,) * 4,
        scratch_shapes=[
            pltpu.VMEM((SUB * tile_cols, SUB * tile_cols), jnp.bfloat16),
        ],
        compiler_params=params(20),
        cost_estimate=cost(tokens.shape[0] * tile_cols, model * weight.shape[1]),
        name="joint_rows",
    )(tokens, gain, weight)


def cost(rows, weights):
    return pl.CostEstimate(flops=4 * rows * weights, bytes_accessed=4 * 2**20, transcendentals=0)


def inner_windows(joint, relative, after):
    return pl.pallas_call(
        inner_kernel,
        out_shape=(
            jax.ShapeDtypeStruct(joint.shape[:3] + (joint.shape[3] // 3,), jnp.bfloat16),
            jax.ShapeDtypeStruct((HEADS // GROUP, AREA, GROUP * AREA), jnp.float32),
        ),
        in_specs=[VMEM, VMEM, pl.BlockSpec(memory_space=pl.ANY)],
        out_specs=(VMEM, VMEM),
        compiler_params=params(20),
        cost_estimate=cost(joint.shape[0] * joint.shape[1] * CELL, 2**19),
        name="inner_windows",
    )(joint, relative, after)


def end_windows(joint, up, down, bias, gain, weight):
    _, across, _, triple = joint.shape
    return pl.pallas_call(
        ends_kernel,
        out_shape=(cells_of(2, across, triple * 2 // 3), cells_of(2, across, triple // 3)),
        in_specs=[VMEM] * 6,
        out_specs=(VMEM, VMEM),
        compiler_params=params(20),
        cost_estimate=cost(joint.shape[0] * joint.shape[1] * CELL, 2**19),
        name="end_windows",
    )(joint, up, down, bias, gain, weight)


def side_windows(ordered, joint, inner, pairs, ends, left, right, bias, gains, weights):
    down, across, _, triple = joint.shape
    model = triple // 3
    strip = CELL * across
    rows = 2 * strip
    wide = weights[2].shape[1]
    tile = jax.ShapeDtypeStruct((down * SUB, across * SUB, weights[-1].shape[1]), jnp.bfloat16)
    return pl.pallas_call(
        sides_kernel,
        out_shape=(tile, tile),
        in_specs=[VMEM] * 15,
        out_specs=(VMEM, VMEM),
        scratch_shapes=[
            pltpu.VMEM((down, across, CELL, model), jnp.bfloat16),
            pltpu.VMEM((2, down + 2, CELL, 2 * model), jnp.bfloat16),
            pltpu.VMEM((strip, strip), jnp.bfloat16),
            pltpu.VMEM((3, rows, model), jnp.float32),
            pltpu.VMEM((2, rows, model), jnp.bfloat16),
            pltpu.VMEM((2, rows, wide), jnp.float32),
            pltpu.VMEM((2, rows, wide), jnp.bfloat16),
        ],
        compiler_params=params(28),
        name="side_windows",
    )(ordered, joint, inner, pairs, ends, left, right, bias, *gains, *weights)


BOX_OWN = 8


def shift(x, axis, step):
    size = lax.axis_size(axis)
    pairs = [(i, i + step) for i in range(size) if 0 <= i + step < size]
    return lax.ppermute(x, axis, pairs)


def shards(
    tokens, first_gain, second_gain, joint_weight, merge_weight, expand_weight, shrink_weight,
    relative_bias, lateral_weight, conv_weight, mask_weight, box_geometry, box_counts, box_owner,
    soft_target,
):
    tile_rows, tile_cols, model = tokens.shape
    first, last = end_rows(tokens)
    up = shift(last, "row", 1)
    down = shift(first, "row", -1)
    joint, ordered, west, east = joint_rows(tokens, first_gain, joint_weight)
    up, down, west, east = lengthen(up, down, west, east)
    left = shift(east, "col", 1)
    right = shift(west, "col", -1)
    inner, bias = inner_windows(joint, relative_bias, west)
    pairs, ends = end_windows(joint, up, down, bias, first_gain, joint_weight)
    features, features_here = side_windows(
        ordered, joint, inner, pairs, ends, left, right, bias, (first_gain, second_gain),
        (joint_weight, merge_weight, expand_weight, shrink_weight, lateral_weight),
    )
    rows_size = lax.axis_size("row")
    geometry = box_geometry.transpose(0, 1, 3, 2)
    send, slope = mask_forward(
        features_here, geometry, box_counts, box_owner, conv_weight, mask_weight
    )
    both = join_pair(send, lax.ppermute(send, "row", [(i, i ^ 1) for i in range(rows_size)]))
    blocks = [both]
    for back in range(2, rows_size, 2):
        blocks.append(
            lax.ppermute(both, "row", [(i, (i + back) % rows_size) for i in range(rows_size)])
        )
    feature_grad, done = mask_backward(
        send, soft_target, slope, geometry, box_counts, conv_weight, mask_weight,
        (tile_rows, tile_cols),
    )
    return features, feature_grad, collect(blocks, done, BOX_OWN, CROP * CROP)


def solution(mesh):
    tile = P("row", "col", None)
    placed = (tile,) + (P(),) * 10 + (
        P("row", "col", None, None), P("row", "col"), tile, P("row", "col", None, None),
    )
    return jax.shard_map(
        shards,
        mesh=mesh,
        in_specs=placed,
        out_specs=(tile, tile, P("row", "col", None, None)),
        check_vma=False,
    )
```

```python
import functools
import jax
import jax.numpy as jnp
from jax import lax
from jax.experimental import pallas as pl
from jax.experimental.pallas import tpu as pltpu
from jax.sharding import PartitionSpec as P

CROP = 14
ROWS = 2
FORWARD_MIB = 16
BACKWARD_MIB = 20
PAD = CROP + 2
GELU_A = 0.7978845608028654
GELU_B = 0.044715
loss_scale = 128.0
NT = (((1,), (1,)), ((), ()))
HIGHEST = lax.Precision.HIGHEST
TN = (((0,), (0,)), ((), ()))
VMEM = pl.BlockSpec(memory_space=pltpu.VMEM)
SMEM = pl.BlockSpec(memory_space=pltpu.SMEM)


def gelu_parts(x):
    square = x * x
    inner = x * (GELU_A + (GELU_A * GELU_B) * square)
    half = 0.5 + 0.5 * jnp.tanh(inner)
    value = x * half
    slope = half + value * (1.0 - half) * (2.0 * GELU_A + (6.0 * GELU_A * GELU_B) * square)
    return value, slope


def gelu_twice(x):
    return x * (1.0 + jnp.tanh(x * (GELU_A + (GELU_A * GELU_B) * (x * x))))


def clear_border(ref):
    blank = jnp.zeros((PAD,) + ref.shape[2:], ref.dtype)
    ref[0] = blank
    ref[PAD - 1] = blank
    for row in range(1, PAD - 1):
        ref[row, 0] = blank[0]
        ref[row, PAD - 1] = blank[0]


def tap_of(ref, begin, end, tap, flip):
    boxes, channels = ref.shape[2:]
    s, t = divmod(tap, 3)
    if flip:
        s, t = 2 - s, 2 - t
    part = ref[begin + s : end + s, t : t + CROP]
    return part.reshape((end - begin) * CROP * boxes, channels)


def box_columns(values, shape, axis):
    index = lax.broadcasted_iota(jnp.int32, shape, axis)
    spread = jnp.zeros(shape, jnp.int32)
    for n, value in enumerate(values):
        spread = jnp.where(index == n, value, spread)
    return spread


def chain(product, finish, before_ref, stages):
    late = []
    count = 0
    for layer, source, target in stages:
        for begin in range(0, CROP, ROWS):
            end = min(begin + ROWS, CROP)
            before = before_ref.at[count % before_ref.shape[0]]
            count += 1
            total = product(layer, source, begin, end)
            before[: end - begin] = total.reshape((end - begin,) + before.shape[1:])
            for piece in late:
                piece()
            late = [
                functools.partial(finish, layer, before.at[u - begin], target, u, v)
                for u in range(begin, end)
                for v in range(CROP)
            ]
    for piece in late:
        piece()


def forward_kernel(
    geom_ref, count_ref, owner_ref, features_ref, weight_ref, mask_ref,
    send_ref, slope_ref,
    a_ref, b_ref, strip_ref, pick_ref, before_ref,
):
    _, boxes, tile_cols, channels = strip_ref.shape
    layers = weight_ref.shape[0]
    lanes = CROP * boxes
    count = count_ref[0, 0]
    clear_border(a_ref)
    clear_border(b_ref)
    shape = (boxes, boxes * tile_cols)
    lane = lax.broadcasted_iota(jnp.int32, shape, 1)
    start = box_columns([geom_ref[0, 0, 1, n] for n in range(boxes)], shape, 0)
    width = box_columns([geom_ref[0, 0, 3, n] for n in range(boxes)], shape, 0)
    mine = lane // tile_cols == lax.broadcasted_iota(jnp.int32, shape, 0)
    away = jnp.where(mine, lane % tile_cols - start, -1)
    away = jnp.where(away < width, away, -1)
    for v in range(CROP):
        pick_ref[v * boxes : (v + 1) * boxes, :] = (away == v).astype(jnp.bfloat16)
    for n in range(boxes):
        rows = features_ref[pl.ds(geom_ref[0, 0, 0, n], CROP)]
        tall = jnp.where(n < count, geom_ref[0, 0, 2, n], 0)
        for u in range(CROP):
            strip_ref[u, n] = jnp.where(u < tall, rows[u], jnp.zeros_like(rows[u]))
    for u in range(CROP):
        crop = jnp.dot(
            pick_ref[...], strip_ref[u].reshape(-1, channels), preferred_element_type=jnp.float32
        )
        a_ref[u + 1, 1 : 1 + CROP] = crop.astype(jnp.bfloat16).reshape(CROP, boxes, channels)

    def forward(layer, source, begin, end):
        return jnp.dot(
            jnp.concatenate([tap_of(source, begin, end, tap, False) for tap in range(9)], axis=1),
            weight_ref[layer],
            preferred_element_type=jnp.float32,
        )

    def activate(layer, before, target, u, v):
        piece = slice(v * boxes, (v + 1) * boxes)
        value, slope = gelu_parts(before[piece])
        slope_ref[layer, u, piece] = slope.astype(jnp.bfloat16)
        target[u + 1, 1 + v] = value.astype(jnp.bfloat16)

    def up(pair, carry):
        stages = [(2 * pair, a_ref, b_ref), (2 * pair + 1, b_ref, a_ref)]
        chain(forward, activate, before_ref, stages)
        return carry

    lax.fori_loop(0, layers // 2, up, 0)
    vector = jnp.broadcast_to(
        mask_ref[...].astype(jnp.float32).reshape(1, channels), (128, channels)
    ).astype(jnp.bfloat16)
    place = lax.broadcasted_iota(jnp.int32, send_ref.shape, 1)
    lane = lax.broadcasted_iota(jnp.int32, (boxes, 128), 1)
    halves = [jnp.zeros((boxes, 128), jnp.float32) for _ in range(2)]
    for u in range(CROP):
        lines = lax.dot_general(
            a_ref[u + 1, 1 : 1 + CROP].reshape(lanes, channels), vector, NT,
            preferred_element_type=jnp.float32,
        )
        for v in range(CROP):
            half, cell = divmod(u * CROP + v, 128)
            halves[half] = jnp.where(
                lane == cell, lines[v * boxes : (v + 1) * boxes], halves[half]
            )
    owner = box_columns(
        [jnp.where(n < count, owner_ref[0, 0, n], -1) for n in range(boxes)], send_ref.shape, 0
    )
    send_ref[...] = jnp.where(
        place == CROP * CROP, owner.astype(jnp.float32), jnp.concatenate(halves, axis=1)
    )


def backward_kernel(
    geom_ref, count_ref, send_ref, soft_ref, slope_ref, weight_ref, mask_ref,
    grad_ref, done_ref,
    a_ref, b_ref, spread_ref, place_ref, before_ref,
):
    done_ref[...] = jnp.zeros_like(done_ref)
    boxes, channels = a_ref.shape[2:]
    tile_cols = grad_ref.shape[1]
    layers = weight_ref.shape[0]
    lanes = CROP * boxes
    cells = CROP * CROP
    count = count_ref[0, 0]
    clear_border(a_ref)
    clear_border(b_ref)
    broad = [geom_ref[0, 0, 3, n] for n in range(boxes)]
    tall = [jnp.where(n < count, geom_ref[0, 0, 2, n], 0) for n in range(boxes)]
    lane = lax.broadcasted_iota(jnp.int32, (tile_cols, lanes), 1)
    cell = lax.broadcasted_iota(jnp.int32, (tile_cols, lanes), 0)
    box, col = lane % boxes, lane // boxes
    for n in range(boxes):
        place_ref[n * tile_cols : (n + 1) * tile_cols, :] = (
            (cell == col + geom_ref[0, 0, 1, n]) & (box == n) & (col < broad[n])
        ).astype(jnp.bfloat16)
    shape = (boxes, cells)
    where = lax.broadcasted_iota(jnp.int32, shape, 1)
    inside = (where // CROP < box_columns(tall, shape, 0)) & (
        where % CROP < box_columns(broad, shape, 0)
    )
    soft = soft_ref[0, 0].astype(jnp.float32)
    lead = loss_scale * (jax.nn.sigmoid(send_ref[:, :cells]) - soft)
    lead = jnp.where(inside, lead, 0.0)
    vector = mask_ref[...].astype(jnp.float32).reshape(1, channels)
    for u in range(CROP):
        for v in range(CROP):
            piece = slice(v * boxes, (v + 1) * boxes)
            grad = lead[:, u * CROP + v : u * CROP + v + 1] * vector
            slope = slope_ref[layers - 1, u, piece].astype(jnp.float32)
            b_ref[u + 1, 1 + v] = (grad * slope).astype(jnp.bfloat16)

    def backward(layer, source, begin, end):
        total = None
        for tap in range(9):
            part = lax.dot_general(
                tap_of(source, begin, end, tap, True),
                weight_ref[layer, tap * channels : (tap + 1) * channels, :],
                NT,
                preferred_element_type=jnp.float32,
            )
            total = part if total is None else total + part
        return total

    def descend(layer, before, target, u, v):
        piece = slice(v * boxes, (v + 1) * boxes)
        slope = slope_ref[jnp.maximum(layer - 1, 0), u, piece].astype(jnp.float32)
        slope = jnp.where(layer == 0, 1.0, slope)
        target[u + 1, 1 + v] = (before[piece] * slope).astype(jnp.bfloat16)

    def down(pair, carry):
        layer = layers - 1 - 2 * pair
        stages = [(layer, b_ref, a_ref), (layer - 1, a_ref, b_ref)]
        chain(backward, descend, before_ref, stages)
        return carry

    lax.fori_loop(0, layers // 2, down, 0)
    for u in range(CROP):
        spread_ref[u] = jnp.dot(
            place_ref[...],
            b_ref[u + 1, 1 : 1 + CROP].reshape(lanes, channels),
            preferred_element_type=jnp.float32,
        ).astype(jnp.bfloat16).reshape(boxes, tile_cols, channels)
    grad_ref[...] = jnp.zeros_like(grad_ref)
    for n in range(boxes):
        kept = lax.broadcasted_iota(jnp.int32, (CROP, 1, 1), 0) < tall[n]
        rows = pl.ds(geom_ref[0, 0, 0, n], CROP)
        grad_ref[rows] = grad_ref[rows] + jnp.where(kept, spread_ref[:, n].astype(jnp.float32), 0.0)


def pair_kernel(own_ref, other_ref, out_ref):
    boxes = own_ref.shape[0]
    second = lax.axis_index("row") % 2
    out_ref[pl.ds(pl.multiple_of(second * boxes, boxes), boxes)] = own_ref[...]
    out_ref[pl.ds(pl.multiple_of((1 - second) * boxes, boxes), boxes)] = other_ref[...]


def join_pair(own, other):
    return pl.pallas_call(
        pair_kernel,
        out_shape=jax.ShapeDtypeStruct((2 * own.shape[0], own.shape[1]), own.dtype),
        in_specs=[VMEM, VMEM],
        out_specs=VMEM,
        compiler_params=pltpu.CompilerParams(vmem_limit_bytes=4 * 2**20),
        name="join_pair",
    )(own, other)


def collect_kernel(*refs):
    blocks, out_ref = refs[:-2], refs[-1]
    keep, cells = out_ref.shape[2:]
    pairs, rows = len(blocks), blocks[0].shape[0]
    sent = jnp.concatenate([ref[...] for ref in blocks], axis=0)
    me = lax.axis_index("row")
    mine = (sent[:, cells : cells + 1] == me.astype(jnp.float32)).astype(jnp.float32)

    def order(axis):
        index = lax.broadcasted_iota(jnp.int32, (pairs * rows, pairs * rows), axis)
        source = me // 2 - index // rows
        source = jnp.where(source < 0, source + pairs, source)
        return source * rows + index % rows

    earlier = (order(1) < order(0)).astype(jnp.float32).astype(jnp.bfloat16)
    many = jnp.broadcast_to(mine, (pairs * rows, 128)).astype(jnp.bfloat16)
    position = jnp.dot(earlier, many, preferred_element_type=jnp.float32)[:, :keep]
    slot = lax.broadcasted_iota(jnp.int32, (pairs * rows, keep), 1).astype(jnp.float32)
    picker = jnp.where(position == slot, mine, 0.0)
    out_ref[0, 0] = lax.dot_general(
        picker, sent[:, :cells], TN, precision=HIGHEST, preferred_element_type=jnp.float32
    )


def mask_cost(weight):
    return pl.CostEstimate(flops=25 * 10**9, bytes_accessed=2 * weight.size, transcendentals=0)


def mask_forward(features, geometry, count, owner, weight, mask):
    tile_rows, tile_cols, channels = features.shape
    boxes = geometry.shape[3]
    layers = weight.shape[0]
    lanes = CROP * boxes
    padded = pltpu.VMEM((PAD, PAD, boxes, channels), jnp.bfloat16)
    return pl.pallas_call(
        forward_kernel,
        out_shape=(
            jax.ShapeDtypeStruct((boxes, 256), jnp.float32),
            jax.ShapeDtypeStruct((layers, CROP, lanes, channels), jnp.bfloat16),
        ),
        in_specs=[SMEM, SMEM, SMEM, VMEM, VMEM, VMEM],
        out_specs=(VMEM, VMEM),
        scratch_shapes=[
            padded,
            padded,
            pltpu.VMEM((CROP, boxes, tile_cols, channels), jnp.bfloat16),
            pltpu.VMEM((lanes, boxes * tile_cols), jnp.bfloat16),
            pltpu.VMEM((3, ROWS, lanes, channels), jnp.float32),
        ],
        compiler_params=pltpu.CompilerParams(vmem_limit_bytes=FORWARD_MIB * 2**20),
        cost_estimate=mask_cost(weight),
        name="mask_forward",
    )(geometry, count, owner, features, weight, mask)


def mask_backward(send, soft, slope, geometry, count, weight, mask, tile):
    layers, _, lanes, channels = slope.shape
    boxes = geometry.shape[3]
    padded = pltpu.VMEM((PAD, PAD, boxes, channels), jnp.bfloat16)
    return pl.pallas_call(
        backward_kernel,
        out_shape=(
            jax.ShapeDtypeStruct(tile + (channels,), jnp.float32),
            jax.ShapeDtypeStruct((8, 128), jnp.float32),
        ),
        in_specs=[SMEM, SMEM, VMEM, VMEM, VMEM, VMEM, VMEM],
        out_specs=(VMEM, VMEM),
        scratch_shapes=[
            padded,
            padded,
            pltpu.VMEM((CROP, boxes, tile[1], channels), jnp.bfloat16),
            pltpu.VMEM((boxes * tile[1], lanes), jnp.bfloat16),
            pltpu.VMEM((3, ROWS, lanes, channels), jnp.float32),
        ],
        compiler_params=pltpu.CompilerParams(vmem_limit_bytes=BACKWARD_MIB * 2**20),
        cost_estimate=mask_cost(weight),
        name="mask_backward",
    )(geometry, count, send, soft, slope, weight, mask)


def collect(blocks, after, keep, cells):
    return pl.pallas_call(
        collect_kernel,
        out_shape=jax.ShapeDtypeStruct((1, 1, keep, cells), jnp.float32),
        in_specs=[VMEM] * len(blocks) + [pl.BlockSpec(memory_space=pl.ANY)],
        out_specs=VMEM,
        compiler_params=pltpu.CompilerParams(vmem_limit_bytes=8 * 2**20),
        name="collect",
    )(*blocks, after)


HEADS = 12
WIN = 8
SUB = WIN // 2
CELL = SUB * SUB
AREA = WIN * WIN
GROUP = 4
EPSILON = 1e-05
BLOCKED = -1000000000.0


def norm_rows(values, gain):
    centered = values - jnp.mean(values, axis=-1, keepdims=True)
    variance = jnp.mean(centered * centered, axis=-1, keepdims=True)
    return (centered * lax.rsqrt(variance + EPSILON) * gain).astype(jnp.bfloat16)


def one_hot(equal, dtype=jnp.bfloat16):
    return equal.astype(jnp.float32).astype(dtype)


def strip_order(width):
    size = SUB * width
    cell_pos = lax.broadcasted_iota(jnp.int32, (size, size), 0)
    token = lax.broadcasted_iota(jnp.int32, (size, size), 1)
    cell, row, col = cell_pos // CELL, cell_pos // SUB % SUB, cell_pos % SUB
    return one_hot(token == row * width + cell * SUB + col)


def window_order():
    place = lax.broadcasted_iota(jnp.int32, (AREA, AREA), 0)
    token = lax.broadcasted_iota(jnp.int32, (AREA, AREA), 1)
    cell, row, col = place // CELL, place // SUB % SUB, place % SUB
    return one_hot(token == (cell // 2 * SUB + row) * WIN + cell % 2 * SUB + col)


def exact(permute, values):
    total = None
    for _ in range(3):
        part = values.astype(jnp.bfloat16)
        values = values - part.astype(jnp.float32)
        moved = permute(part)
        total = moved if total is None else total + moved
    return total


def head_blocks(lanes):
    row = lax.broadcasted_iota(jnp.int32, (GROUP * AREA, lanes), 0)
    col = lax.broadcasted_iota(jnp.int32, (GROUP * AREA, lanes), 1)
    return one_hot(row // AREA == col // (lanes // GROUP))


def attend(queries, key_rows, value_rows, bias, blocks, key_mask):
    lanes = blocks.shape[1]
    scale = (lanes // GROUP) ** (-0.5)
    first = lax.broadcasted_iota(jnp.int32, (1, 2 * AREA), 1) < AREA
    mixed = []
    for group in range(len(bias)):
        cut = slice(group * lanes, (group + 1) * lanes)
        keys = jnp.concatenate([key_rows[:, cut]] * GROUP, axis=0) * blocks
        values = jnp.concatenate([value_rows[:, cut]] * GROUP, axis=0) * blocks
        scores = lax.dot_general(queries[:, cut], keys, NT, preferred_element_type=jnp.float32)
        scores = scores * scale + bias[group]
        if key_mask is not None:
            scores = scores + key_mask
        weights = []
        for pair in range(GROUP // 2):
            part = scores[:, pair * 2 * AREA : (pair + 1) * 2 * AREA]
            low = jnp.max(jnp.where(first, part, -jnp.inf), axis=-1, keepdims=True)
            high = jnp.max(jnp.where(first, -jnp.inf, part), axis=-1, keepdims=True)
            weights.append(jnp.exp(part - jnp.where(first, low, high)))
        weights = jnp.concatenate(weights, axis=1).astype(jnp.bfloat16)
        both = jnp.dot(
            weights, jnp.concatenate([values, blocks], axis=1), preferred_element_type=jnp.float32
        )
        mixed.append((both[:, :lanes] / both[:, lanes:]).astype(jnp.bfloat16))
    return jnp.concatenate(mixed, axis=1)


def joint_kernel(
    tokens_ref, gain_ref, joint_ref, relative_ref,
    out_ref, bias_ref, ordered_ref, west_ref, east_ref, order_ref,
):
    cells_down, cells_across, _, model = ordered_ref.shape
    strip = order_ref.shape[0]
    order_ref[...] = strip_order(strip // SUB)
    gain = gain_ref[...].reshape(1, model)

    for step in range(cells_down // 2):
        normed = []
        for down in (2 * step, 2 * step + 1):
            ordered = jnp.dot(
                order_ref[...],
                tokens_ref[down * SUB : (down + 1) * SUB].reshape(strip, model),
                preferred_element_type=jnp.float32,
            )
            ordered_ref[down] = ordered.astype(jnp.bfloat16).reshape(cells_across, CELL, model)
            normed.append(norm_rows(ordered, gain))
        out_ref[2 * step : 2 * step + 2] = (
            jnp.dot(
                jnp.concatenate(normed, axis=0), joint_ref[...], preferred_element_type=jnp.float32
            )
            .astype(jnp.bfloat16)
            .reshape(2, cells_across, CELL, 3 * model)
        )
    place = window_order()
    turned = exact(lambda part: lax.dot_general(part, place, NT, preferred_element_type=jnp.float32),
                   relative_ref[...].reshape(-1, AREA))
    for group in range(HEADS // GROUP):
        rows = [
            turned[(group * GROUP + h) * AREA : (group * GROUP + h + 1) * AREA]
            for h in range(GROUP)
        ]
        bias_ref[group] = exact(
            lambda part: jnp.dot(place, part, preferred_element_type=jnp.float32),
            jnp.concatenate(rows, axis=1),
        )
    west_ref[...] = ordered_ref[:, 0]
    east_ref[...] = ordered_ref[:, cells_across - 1]


def inner_kernel(joint_ref, bias_ref, after_ref, out_ref):
    cells_down, cells_across, _, triple = joint_ref.shape
    model = triple // 3
    blocks = head_blocks(GROUP * model // HEADS)
    bias = [bias_ref[group] for group in range(bias_ref.shape[0])]

    for i in range(1, cells_down - 1, 2):
        for j in range(1, cells_across - 1, 2):
            rows = joint_ref[i : i + 2, j : j + 2].reshape(AREA, triple)
            mixed = attend(
                rows[:, :model], rows[:, model : 2 * model], rows[:, 2 * model :], bias, blocks, None
            )
            out_ref[i : i + 2, j : j + 2] = mixed.reshape(2, 2, CELL, model)


def lengthen_kernel(
    up_ref, down_ref, west_ref, east_ref, up_out_ref, down_out_ref, west_out_ref, east_out_ref
):
    width = up_ref.shape[1]
    order = strip_order(width)
    for source, target in ((up_ref, up_out_ref), (down_ref, down_out_ref)):
        ordered = jnp.dot(
            order, source[...].reshape(SUB * width, -1), preferred_element_type=jnp.float32
        )
        target[...] = ordered.astype(jnp.bfloat16).reshape(target.shape)
    last = up_out_ref.shape[0] - 1
    for cell, own, out in ((0, west_ref, west_out_ref), (last, east_ref, east_out_ref)):
        out[0] = up_out_ref[cell]
        out[1:-1] = own[...]
        out[out.shape[0] - 1] = down_out_ref[cell]


def lengthen(up, down, west, east):
    across = jax.ShapeDtypeStruct((up.shape[1] // SUB, CELL, up.shape[2]), up.dtype)
    out = jax.ShapeDtypeStruct((west.shape[0] + 2,) + west.shape[1:], west.dtype)
    return pl.pallas_call(
        lengthen_kernel,
        out_shape=(across, across, out, out),
        in_specs=[VMEM] * 4,
        out_specs=(VMEM,) * 4,
        compiler_params=params(8),
        name="lengthen",
    )(up, down, west, east)


def hidden_keys(down_side, down_edge, across_side, across_edge):
    cell = lax.broadcasted_iota(jnp.int32, (1, GROUP * AREA), 1) // CELL % 4
    hidden = jnp.zeros((1, GROUP * AREA), jnp.bool_)
    if down_side is not None:
        hidden = hidden | ((cell // 2 == down_side) & down_edge)
    if across_side is not None:
        hidden = hidden | ((cell % 2 == across_side) & across_edge)
    return jnp.where(hidden, BLOCKED, 0.0)


def at_end(axis, side):
    return lax.axis_index(axis) == (lax.axis_size(axis) - 1 if side else 0)


def window_bias(bias_ref, cells):
    return [
        jnp.concatenate([bias_ref[g, c * CELL : (c + 1) * CELL] for c in cells], axis=0)
        for g in range(bias_ref.shape[0])
    ]


def halo_pairs(halo, gain, joint_ref):
    model = halo.shape[-1]
    normed = norm_rows(halo.astype(jnp.float32), gain)
    return jnp.dot(normed, joint_ref[:, model:], preferred_element_type=jnp.float32).astype(
        jnp.bfloat16
    )


def ends_kernel(joint_out_ref, up_ref, down_ref, bias_ref, gain_ref, joint_ref, pairs_ref, out_ref):
    cells_down, cells_across, _, triple = joint_out_ref.shape
    model = triple // 3
    blocks = head_blocks(GROUP * model // HEADS)
    gain = gain_ref[...].reshape(1, model)
    halo = jnp.concatenate([ref[...].reshape(-1, model) for ref in (up_ref, down_ref)], axis=0)
    pairs_ref[...] = halo_pairs(halo, gain, joint_ref).reshape(2, cells_across, CELL, 2 * model)
    for side in range(2):
        row = side * (cells_down - 1)
        bias = window_bias(bias_ref, [2 - 2 * side, 3 - 2 * side])
        key_mask = hidden_keys(side, at_end("row", side), None, None)
        for j in range(1, cells_across // 2):
            cut = slice(2 * j - 1, 2 * j + 1)
            own = joint_out_ref[row, cut].reshape(2 * CELL, triple)
            other = pairs_ref[side, cut].reshape(2 * CELL, 2 * model)
            both = [own[:, model:], other] if side else [other, own[:, model:]]
            both = jnp.concatenate(both, axis=0)
            mixed = attend(own[:, :model], both[:, :model], both[:, model:], bias, blocks, key_mask)
            out_ref[side, cut] = mixed.reshape(2, CELL, model)


def sides_kernel(
    ordered_ref, joint_out_ref, inner_ref, pairs_ref, ends_ref, left_ref, right_ref,
    bias_ref, first_ref, second_ref, joint_ref, merge_ref, expand_ref, shrink_ref, lateral_ref,
    features_ref, copy_ref, mixed_ref, halo_ref, order_ref, residual_ref, normed_ref, wide_ref, hidden_ref,
):
    cells_down, cells_across, _, triple = joint_out_ref.shape
    model = triple // 3
    strip = cells_across * CELL
    order_ref[...] = strip_order(cells_across * SUB)
    blocks = head_blocks(GROUP * model // HEADS)
    halo = jnp.concatenate([ref[...].reshape(-1, model) for ref in (left_ref, right_ref)], axis=0)
    halo = halo_pairs(halo, first_ref[...].reshape(1, model), joint_ref)
    halo_ref[...] = halo.reshape(2, cells_down + 2, CELL, 2 * model)
    mixed_ref[1:-1, 1:-1] = inner_ref[1:-1, 1:-1]
    mixed_ref[0, 1:-1] = ends_ref[0, 1:-1]
    mixed_ref[cells_down - 1, 1:-1] = ends_ref[1, 1:-1]

    for across in range(2):
        col = across * (cells_across - 1)
        bias = window_bias(bias_ref, [1 - across, 3 - across])
        key_mask = hidden_keys(None, None, across, at_end("col", across))

        def keys(pieces):
            rows = []
            for own, other in pieces:
                rows += [own, other] if across else [other, own]
            return jnp.concatenate(rows, axis=0)

        for i in range(1, cells_down // 2):
            cells = [2 * i - 1, 2 * i]
            both = keys(
                [(joint_out_ref[c, col, :, model:], halo_ref[across, c + 1]) for c in cells]
            )
            queries = jnp.concatenate([joint_out_ref[c, col, :, :model] for c in cells], axis=0)
            mixed = attend(queries, both[:, :model], both[:, model:], bias, blocks, key_mask)
            for place, c in enumerate(cells):
                mixed_ref[c, col] = mixed[place * CELL : (place + 1) * CELL]
        for down in range(2):
            row = down * (cells_down - 1)
            near = (joint_out_ref[row, col, :, model:], halo_ref[across, row + 1])
            far = (pairs_ref[down, col], halo_ref[across, down * (cells_down + 1)])
            both = keys([near, far] if down else [far, near])
            mixed_ref[row, col] = attend(
                joint_out_ref[row, col, :, :model], both[:, :model], both[:, model:],
                window_bias(bias_ref, [3 - 2 * down - across]), blocks,
                hidden_keys(down, at_end("row", down), across, at_end("col", across)),
            )

    second = second_ref[...].reshape(1, model)
    rows = hidden_ref.shape[1]
    group = rows // strip
    steps = cells_down // group

    def merge(step):
        residual = residual_ref.at[step % 3]
        cells = slice(step * group, (step + 1) * group)
        residual[...] = jnp.dot(
            mixed_ref[cells].reshape(rows, model), merge_ref[...], preferred_element_type=jnp.float32
        )

    def normalise(step, part):
        residual = residual_ref.at[step % 3]
        cut = slice(part, part + PART)
        c, a = divmod(part // CELL, cells_across)
        own = ordered_ref[step * group + c, a : a + PART // CELL].reshape(PART, model)
        total = residual[cut] + own.astype(jnp.float32)
        residual[cut] = total
        normed_ref[step % 2, cut] = norm_rows(total, second)

    def expand(step, lane):
        cut = slice(lane, lane + LANES)
        wide_ref[step % 2, :, cut] = jnp.dot(
            normed_ref[step % 2], expand_ref[:, cut], preferred_element_type=jnp.float32
        )

    def activate(step, lane):
        cut = slice(lane, lane + LANES)
        for part in range(0, rows, CELL):
            here = slice(part, part + CELL)
            hidden_ref[step % 2, here, cut] = gelu_twice(wide_ref[step % 2, here, cut]).astype(
                jnp.bfloat16
            )

    def shrink(step):
        block_out = residual_ref[step % 3] + 0.5 * jnp.dot(
            hidden_ref[step % 2], shrink_ref[...], preferred_element_type=jnp.float32
        )
        features = jnp.dot(
            block_out.astype(jnp.bfloat16), lateral_ref[...], preferred_element_type=jnp.float32
        ).astype(jnp.bfloat16)
        for part in range(group):
            natural = lax.dot_general(
                order_ref[...], features[part * strip : (part + 1) * strip], TN,
                preferred_element_type=jnp.float32,
            ).astype(jnp.bfloat16)
            first = (step * group + part) * SUB
            natural = natural.reshape((SUB,) + features_ref.shape[1:])
            features_ref[first : first + SUB] = natural
            copy_ref[first : first + SUB] = natural

    lanes = range(0, wide_ref.shape[2], LANES)
    for step in range(min(2, steps)):
        merge(step)
        for part in range(0, rows, PART):
            normalise(step, part)
        if step == 0:
            for lane in lanes:
                expand(0, lane)
    for step in range(steps):
        for lane in lanes:
            if step + 1 < steps:
                expand(step + 1, lane)
            activate(step, lane)
        if step + 2 < steps:
            merge(step + 2)
        shrink(step)
        if step + 2 < steps:
            for part in range(0, rows, PART):
                normalise(step + 2, part)


LANES = 256
PART = 64


def params(mebibytes):
    return pltpu.CompilerParams(vmem_limit_bytes=mebibytes * 2**20)


def cells_of(count_down, count_across, channels, dtype=jnp.bfloat16):
    return jax.ShapeDtypeStruct((count_down, count_across, CELL, channels), dtype)


def end_kernel(tokens_ref, first_ref, last_ref):
    first_ref[...] = tokens_ref[:SUB]
    last_ref[...] = tokens_ref[tokens_ref.shape[0] - SUB :]


def end_rows(tokens):
    out = jax.ShapeDtypeStruct((SUB,) + tokens.shape[1:], tokens.dtype)
    return pl.pallas_call(
        end_kernel,
        out_shape=(out, out),
        in_specs=[VMEM],
        out_specs=(VMEM, VMEM),
        compiler_params=params(4),
        cost_estimate=cost(tokens.shape[0] * tokens.shape[1], 2**20),
        name="end_rows",
    )(tokens)


def joint_rows(tokens, gain, weight, relative):
    tile_rows, tile_cols, model = tokens.shape
    down, across = tile_rows // SUB, tile_cols // SUB
    lone = lambda n: jax.ShapeDtypeStruct((n, CELL, model), jnp.bfloat16)
    return pl.pallas_call(
        joint_kernel,
        out_shape=(
            cells_of(down, across, weight.shape[1]),
            jax.ShapeDtypeStruct((HEADS // GROUP, AREA, GROUP * AREA), jnp.float32),
            cells_of(down, across, model),
            lone(down), lone(down),
        ),
        in_specs=[VMEM] * 4,
        out_specs=(VMEM,) * 5,
        scratch_shapes=[
            pltpu.VMEM((SUB * tile_cols, SUB * tile_cols), jnp.bfloat16),
        ],
        compiler_params=params(20),
        cost_estimate=cost(tokens.shape[0] * tile_cols, model * weight.shape[1]),
        name="joint_rows",
    )(tokens, gain, weight, relative)


def cost(rows, weights):
    return pl.CostEstimate(flops=4 * rows * weights, bytes_accessed=4 * 2**20, transcendentals=0)


def inner_windows(joint, bias, after):
    return pl.pallas_call(
        inner_kernel,
        out_shape=jax.ShapeDtypeStruct(joint.shape[:3] + (joint.shape[3] // 3,), jnp.bfloat16),
        in_specs=[VMEM, VMEM, pl.BlockSpec(memory_space=pl.ANY)],
        out_specs=VMEM,
        compiler_params=params(20),
        cost_estimate=cost(joint.shape[0] * joint.shape[1] * CELL, 2**19),
        name="inner_windows",
    )(joint, bias, after)


def end_windows(joint, up, down, bias, gain, weight):
    _, across, _, triple = joint.shape
    return pl.pallas_call(
        ends_kernel,
        out_shape=(cells_of(2, across, triple * 2 // 3), cells_of(2, across, triple // 3)),
        in_specs=[VMEM] * 6,
        out_specs=(VMEM, VMEM),
        compiler_params=params(20),
        cost_estimate=cost(joint.shape[0] * joint.shape[1] * CELL, 2**19),
        name="end_windows",
    )(joint, up, down, bias, gain, weight)


def side_windows(ordered, joint, inner, pairs, ends, left, right, bias, gains, weights):
    down, across, _, triple = joint.shape
    model = triple // 3
    strip = CELL * across
    rows = 4 * strip
    wide = weights[2].shape[1]
    tile = jax.ShapeDtypeStruct((down * SUB, across * SUB, weights[-1].shape[1]), jnp.bfloat16)
    return pl.pallas_call(
        sides_kernel,
        out_shape=(tile, tile),
        in_specs=[VMEM] * 15,
        out_specs=(VMEM, VMEM),
        scratch_shapes=[
            pltpu.VMEM((down, across, CELL, model), jnp.bfloat16),
            pltpu.VMEM((2, down + 2, CELL, 2 * model), jnp.bfloat16),
            pltpu.VMEM((strip, strip), jnp.bfloat16),
            pltpu.VMEM((3, rows, model), jnp.float32),
            pltpu.VMEM((2, rows, model), jnp.bfloat16),
            pltpu.VMEM((2, rows, wide), jnp.float32),
            pltpu.VMEM((2, rows, wide), jnp.bfloat16),
        ],
        compiler_params=params(34),
        name="side_windows",
    )(ordered, joint, inner, pairs, ends, left, right, bias, *gains, *weights)


BOX_OWN = 8


def shift(x, axis, step):
    size = lax.axis_size(axis)
    pairs = [(i, i + step) for i in range(size) if 0 <= i + step < size]
    return lax.ppermute(x, axis, pairs)


def shards(
    tokens, first_gain, second_gain, joint_weight, merge_weight, expand_weight, shrink_weight,
    relative_bias, lateral_weight, conv_weight, mask_weight, box_geometry, box_counts, box_owner,
    soft_target,
):
    tile_rows, tile_cols, model = tokens.shape
    first, last = end_rows(tokens)
    up = shift(last, "row", 1)
    down = shift(first, "row", -1)
    joint, bias, ordered, west, east = joint_rows(
        tokens, first_gain, joint_weight, relative_bias
    )
    up, down, west, east = lengthen(up, down, west, east)
    left = shift(east, "col", 1)
    right = shift(west, "col", -1)
    inner = inner_windows(joint, bias, west)
    pairs, ends = end_windows(joint, up, down, bias, first_gain, joint_weight)
    features, features_here = side_windows(
        ordered, joint, inner, pairs, ends, left, right, bias, (first_gain, second_gain),
        (joint_weight, merge_weight, expand_weight, shrink_weight, lateral_weight),
    )
    rows_size = lax.axis_size("row")
    geometry = box_geometry.transpose(0, 1, 3, 2)
    send, slope = mask_forward(
        features_here, geometry, box_counts, box_owner, conv_weight, mask_weight
    )
    both = join_pair(send, lax.ppermute(send, "row", [(i, i ^ 1) for i in range(rows_size)]))
    blocks = [both]
    for back in range(2, rows_size, 2):
        blocks.append(
            lax.ppermute(both, "row", [(i, (i + back) % rows_size) for i in range(rows_size)])
        )
    feature_grad, done = mask_backward(
        send, soft_target, slope, geometry, box_counts, conv_weight, mask_weight,
        (tile_rows, tile_cols),
    )
    return features, feature_grad, collect(blocks, done, BOX_OWN, CROP * CROP)


def solution(mesh):
    tile = P("row", "col", None)
    placed = (tile,) + (P(),) * 10 + (
        P("row", "col", None, None), P("row", "col"), tile, P("row", "col", None, None),
    )
    return jax.shard_map(
        shards,
        mesh=mesh,
        in_specs=placed,
        out_specs=(tile, tile, P("row", "col", None, None)),
        check_vma=False,
    )
```

```python
import functools
import jax
import jax.numpy as jnp
from jax import lax
from jax.experimental import pallas as pl
from jax.experimental.pallas import tpu as pltpu
from jax.sharding import PartitionSpec as P

CROP = 14
ROWS = 2
FORWARD_MIB = 16
BACKWARD_MIB = 20
PAD = CROP + 2
GELU_A = 0.7978845608028654
GELU_B = 0.044715
loss_scale = 128.0
NT = (((1,), (1,)), ((), ()))
HIGHEST = lax.Precision.HIGHEST
TN = (((0,), (0,)), ((), ()))
VMEM = pl.BlockSpec(memory_space=pltpu.VMEM)
SMEM = pl.BlockSpec(memory_space=pltpu.SMEM)


def gelu_parts(x):
    square = x * x
    inner = x * (GELU_A + (GELU_A * GELU_B) * square)
    half = 0.5 + 0.5 * jnp.tanh(inner)
    value = x * half
    slope = half + value * (1.0 - half) * (2.0 * GELU_A + (6.0 * GELU_A * GELU_B) * square)
    return value, slope


def gelu_twice(x):
    return x * (1.0 + jnp.tanh(x * (GELU_A + (GELU_A * GELU_B) * (x * x))))


def clear_border(ref):
    blank = jnp.zeros((PAD,) + ref.shape[2:], ref.dtype)
    ref[0] = blank
    ref[PAD - 1] = blank
    for row in range(1, PAD - 1):
        ref[row, 0] = blank[0]
        ref[row, PAD - 1] = blank[0]


def tap_of(ref, begin, end, tap, flip):
    boxes, channels = ref.shape[2:]
    s, t = divmod(tap, 3)
    if flip:
        s, t = 2 - s, 2 - t
    part = ref[begin + s : end + s, t : t + CROP]
    return part.reshape((end - begin) * CROP * boxes, channels)


def box_columns(values, shape, axis):
    index = lax.broadcasted_iota(jnp.int32, shape, axis)
    spread = jnp.zeros(shape, jnp.int32)
    for n, value in enumerate(values):
        spread = jnp.where(index == n, value, spread)
    return spread


def chain(product, finish, before_ref, stages):
    late = []
    count = 0
    for layer, source, target in stages:
        for begin in range(0, CROP, ROWS):
            end = min(begin + ROWS, CROP)
            before = before_ref.at[count % before_ref.shape[0]]
            count += 1
            total = product(layer, source, begin, end)
            before[: end - begin] = total.reshape((end - begin,) + before.shape[1:])
            for piece in late:
                piece()
            late = [
                functools.partial(finish, layer, before.at[u - begin], target, u, v)
                for u in range(begin, end)
                for v in range(CROP)
            ]
    for piece in late:
        piece()


def forward_kernel(
    geom_ref, count_ref, owner_ref, features_ref, weight_ref, mask_ref,
    send_ref, slope_ref,
    a_ref, b_ref, strip_ref, pick_ref, before_ref,
):
    _, boxes, tile_cols, channels = strip_ref.shape
    layers = weight_ref.shape[0]
    lanes = CROP * boxes
    count = count_ref[0, 0]
    clear_border(a_ref)
    clear_border(b_ref)
    shape = (boxes, boxes * tile_cols)
    lane = lax.broadcasted_iota(jnp.int32, shape, 1)
    start = box_columns([geom_ref[0, 0, 1, n] for n in range(boxes)], shape, 0)
    width = box_columns([geom_ref[0, 0, 3, n] for n in range(boxes)], shape, 0)
    mine = lane // tile_cols == lax.broadcasted_iota(jnp.int32, shape, 0)
    away = jnp.where(mine, lane % tile_cols - start, -1)
    away = jnp.where(away < width, away, -1)
    for v in range(CROP):
        pick_ref[v * boxes : (v + 1) * boxes, :] = (away == v).astype(jnp.bfloat16)
    for n in range(boxes):
        rows = features_ref[pl.ds(geom_ref[0, 0, 0, n], CROP)]
        tall = jnp.where(n < count, geom_ref[0, 0, 2, n], 0)
        for u in range(CROP):
            strip_ref[u, n] = jnp.where(u < tall, rows[u], jnp.zeros_like(rows[u]))
    for u in range(CROP):
        crop = jnp.dot(
            pick_ref[...], strip_ref[u].reshape(-1, channels), preferred_element_type=jnp.float32
        )
        a_ref[u + 1, 1 : 1 + CROP] = crop.astype(jnp.bfloat16).reshape(CROP, boxes, channels)

    def forward(layer, source, begin, end):
        return jnp.dot(
            jnp.concatenate([tap_of(source, begin, end, tap, False) for tap in range(9)], axis=1),
            weight_ref[layer],
            preferred_element_type=jnp.float32,
        )

    def activate(layer, before, target, u, v):
        piece = slice(v * boxes, (v + 1) * boxes)
        value, slope = gelu_parts(before[piece])
        slope_ref[layer, u, piece] = slope.astype(jnp.bfloat16)
        target[u + 1, 1 + v] = value.astype(jnp.bfloat16)

    def up(pair, carry):
        stages = [(2 * pair, a_ref, b_ref), (2 * pair + 1, b_ref, a_ref)]
        chain(forward, activate, before_ref, stages)
        return carry

    lax.fori_loop(0, layers // 2, up, 0)
    vector = jnp.broadcast_to(
        mask_ref[...].astype(jnp.float32).reshape(1, channels), (128, channels)
    ).astype(jnp.bfloat16)
    place = lax.broadcasted_iota(jnp.int32, send_ref.shape, 1)
    lane = lax.broadcasted_iota(jnp.int32, (boxes, 128), 1)
    halves = [jnp.zeros((boxes, 128), jnp.float32) for _ in range(2)]
    for u in range(CROP):
        lines = lax.dot_general(
            a_ref[u + 1, 1 : 1 + CROP].reshape(lanes, channels), vector, NT,
            preferred_element_type=jnp.float32,
        )
        for v in range(CROP):
            half, cell = divmod(u * CROP + v, 128)
            halves[half] = jnp.where(
                lane == cell, lines[v * boxes : (v + 1) * boxes], halves[half]
            )
    owner = box_columns(
        [jnp.where(n < count, owner_ref[0, 0, n], -1) for n in range(boxes)], send_ref.shape, 0
    )
    send_ref[...] = jnp.where(
        place == CROP * CROP, owner.astype(jnp.float32), jnp.concatenate(halves, axis=1)
    )


def backward_kernel(
    geom_ref, count_ref, send_ref, soft_ref, slope_ref, weight_ref, mask_ref,
    grad_ref, done_ref,
    a_ref, b_ref, spread_ref, place_ref, before_ref,
):
    done_ref[...] = jnp.zeros_like(done_ref)
    boxes, channels = a_ref.shape[2:]
    tile_cols = grad_ref.shape[1]
    layers = weight_ref.shape[0]
    lanes = CROP * boxes
    cells = CROP * CROP
    count = count_ref[0, 0]
    clear_border(a_ref)
    clear_border(b_ref)
    broad = [geom_ref[0, 0, 3, n] for n in range(boxes)]
    tall = [jnp.where(n < count, geom_ref[0, 0, 2, n], 0) for n in range(boxes)]
    lane = lax.broadcasted_iota(jnp.int32, (tile_cols, lanes), 1)
    cell = lax.broadcasted_iota(jnp.int32, (tile_cols, lanes), 0)
    box, col = lane % boxes, lane // boxes
    for n in range(boxes):
        place_ref[n * tile_cols : (n + 1) * tile_cols, :] = (
            (cell == col + geom_ref[0, 0, 1, n]) & (box == n) & (col < broad[n])
        ).astype(jnp.bfloat16)
    shape = (boxes, cells)
    where = lax.broadcasted_iota(jnp.int32, shape, 1)
    inside = (where // CROP < box_columns(tall, shape, 0)) & (
        where % CROP < box_columns(broad, shape, 0)
    )
    soft = soft_ref[0, 0].astype(jnp.float32)
    lead = loss_scale * (jax.nn.sigmoid(send_ref[:, :cells]) - soft)
    lead = jnp.where(inside, lead, 0.0)
    vector = mask_ref[...].astype(jnp.float32).reshape(1, channels)
    for u in range(CROP):
        for v in range(CROP):
            piece = slice(v * boxes, (v + 1) * boxes)
            grad = lead[:, u * CROP + v : u * CROP + v + 1] * vector
            slope = slope_ref[layers - 1, u, piece].astype(jnp.float32)
            b_ref[u + 1, 1 + v] = (grad * slope).astype(jnp.bfloat16)

    def backward(layer, source, begin, end):
        total = None
        for tap in range(9):
            part = lax.dot_general(
                tap_of(source, begin, end, tap, True),
                weight_ref[layer, tap * channels : (tap + 1) * channels, :],
                NT,
                preferred_element_type=jnp.float32,
            )
            total = part if total is None else total + part
        return total

    def descend(layer, before, target, u, v):
        piece = slice(v * boxes, (v + 1) * boxes)
        grad = before[piece]
        if layer > 0:
            grad = grad * slope_ref[layer - 1, u, piece].astype(jnp.float32)
        target[u + 1, 1 + v] = grad.astype(jnp.bfloat16)

    stages = []
    for layer in reversed(range(layers)):
        refs = (b_ref, a_ref) if (layers - layer) % 2 else (a_ref, b_ref)
        stages.append((layer,) + refs)
    chain(backward, descend, before_ref, stages)
    for u in range(CROP):
        spread_ref[u] = jnp.dot(
            place_ref[...],
            b_ref[u + 1, 1 : 1 + CROP].reshape(lanes, channels),
            preferred_element_type=jnp.float32,
        ).astype(jnp.bfloat16).reshape(boxes, tile_cols, channels)
    grad_ref[...] = jnp.zeros_like(grad_ref)
    for n in range(boxes):
        kept = lax.broadcasted_iota(jnp.int32, (CROP, 1, 1), 0) < tall[n]
        rows = pl.ds(geom_ref[0, 0, 0, n], CROP)
        grad_ref[rows] = grad_ref[rows] + jnp.where(kept, spread_ref[:, n].astype(jnp.float32), 0.0)


def pair_kernel(own_ref, other_ref, out_ref):
    boxes = own_ref.shape[0]
    second = lax.axis_index("row") % 2
    out_ref[pl.ds(pl.multiple_of(second * boxes, boxes), boxes)] = own_ref[...]
    out_ref[pl.ds(pl.multiple_of((1 - second) * boxes, boxes), boxes)] = other_ref[...]


def join_pair(own, other):
    return pl.pallas_call(
        pair_kernel,
        out_shape=jax.ShapeDtypeStruct((2 * own.shape[0], own.shape[1]), own.dtype),
        in_specs=[VMEM, VMEM],
        out_specs=VMEM,
        compiler_params=pltpu.CompilerParams(vmem_limit_bytes=4 * 2**20),
        name="join_pair",
    )(own, other)


def collect_kernel(*refs):
    blocks, out_ref = refs[:-2], refs[-1]
    keep, cells = out_ref.shape[2:]
    pairs, rows = len(blocks), blocks[0].shape[0]
    sent = jnp.concatenate([ref[...] for ref in blocks], axis=0)
    me = lax.axis_index("row")
    mine = (sent[:, cells : cells + 1] == me.astype(jnp.float32)).astype(jnp.float32)

    def order(axis):
        index = lax.broadcasted_iota(jnp.int32, (pairs * rows, pairs * rows), axis)
        source = me // 2 - index // rows
        source = jnp.where(source < 0, source + pairs, source)
        return source * rows + index % rows

    earlier = (order(1) < order(0)).astype(jnp.float32).astype(jnp.bfloat16)
    many = jnp.broadcast_to(mine, (pairs * rows, 128)).astype(jnp.bfloat16)
    position = jnp.dot(earlier, many, preferred_element_type=jnp.float32)[:, :keep]
    slot = lax.broadcasted_iota(jnp.int32, (pairs * rows, keep), 1).astype(jnp.float32)
    picker = jnp.where(position == slot, mine, 0.0)
    out_ref[0, 0] = lax.dot_general(
        picker, sent[:, :cells], TN, precision=HIGHEST, preferred_element_type=jnp.float32
    )


def mask_cost(weight):
    return pl.CostEstimate(flops=25 * 10**9, bytes_accessed=2 * weight.size, transcendentals=0)


def mask_forward(features, geometry, count, owner, weight, mask):
    tile_rows, tile_cols, channels = features.shape
    boxes = geometry.shape[3]
    layers = weight.shape[0]
    lanes = CROP * boxes
    padded = pltpu.VMEM((PAD, PAD, boxes, channels), jnp.bfloat16)
    return pl.pallas_call(
        forward_kernel,
        out_shape=(
            jax.ShapeDtypeStruct((boxes, 256), jnp.float32),
            jax.ShapeDtypeStruct((layers, CROP, lanes, channels), jnp.bfloat16),
        ),
        in_specs=[SMEM, SMEM, SMEM, VMEM, VMEM, VMEM],
        out_specs=(VMEM, VMEM),
        scratch_shapes=[
            padded,
            padded,
            pltpu.VMEM((CROP, boxes, tile_cols, channels), jnp.bfloat16),
            pltpu.VMEM((lanes, boxes * tile_cols), jnp.bfloat16),
            pltpu.VMEM((3, ROWS, lanes, channels), jnp.float32),
        ],
        compiler_params=pltpu.CompilerParams(vmem_limit_bytes=FORWARD_MIB * 2**20),
        cost_estimate=mask_cost(weight),
        name="mask_forward",
    )(geometry, count, owner, features, weight, mask)


def mask_backward(send, soft, slope, geometry, count, weight, mask, tile):
    layers, _, lanes, channels = slope.shape
    boxes = geometry.shape[3]
    padded = pltpu.VMEM((PAD, PAD, boxes, channels), jnp.bfloat16)
    return pl.pallas_call(
        backward_kernel,
        out_shape=(
            jax.ShapeDtypeStruct(tile + (channels,), jnp.float32),
            jax.ShapeDtypeStruct((8, 128), jnp.float32),
        ),
        in_specs=[SMEM, SMEM, VMEM, VMEM, VMEM, VMEM, VMEM],
        out_specs=(VMEM, VMEM),
        scratch_shapes=[
            padded,
            padded,
            pltpu.VMEM((CROP, boxes, tile[1], channels), jnp.bfloat16),
            pltpu.VMEM((boxes * tile[1], lanes), jnp.bfloat16),
            pltpu.VMEM((3, ROWS, lanes, channels), jnp.float32),
        ],
        compiler_params=pltpu.CompilerParams(vmem_limit_bytes=BACKWARD_MIB * 2**20),
        cost_estimate=mask_cost(weight),
        name="mask_backward",
    )(geometry, count, send, soft, slope, weight, mask)


def collect(blocks, after, keep, cells):
    return pl.pallas_call(
        collect_kernel,
        out_shape=jax.ShapeDtypeStruct((1, 1, keep, cells), jnp.float32),
        in_specs=[VMEM] * len(blocks) + [pl.BlockSpec(memory_space=pl.ANY)],
        out_specs=VMEM,
        compiler_params=pltpu.CompilerParams(vmem_limit_bytes=8 * 2**20),
        name="collect",
    )(*blocks, after)


HEADS = 12
WIN = 8
SUB = WIN // 2
CELL = SUB * SUB
AREA = WIN * WIN
GROUP = 4
EPSILON = 1e-05
BLOCKED = -1000000000.0


def norm_rows(values, gain):
    centered = values - jnp.mean(values, axis=-1, keepdims=True)
    variance = jnp.mean(centered * centered, axis=-1, keepdims=True)
    return (centered * lax.rsqrt(variance + EPSILON) * gain).astype(jnp.bfloat16)


def one_hot(equal, dtype=jnp.bfloat16):
    return equal.astype(jnp.float32).astype(dtype)


def strip_order(width):
    size = SUB * width
    cell_pos = lax.broadcasted_iota(jnp.int32, (size, size), 0)
    token = lax.broadcasted_iota(jnp.int32, (size, size), 1)
    cell, row, col = cell_pos // CELL, cell_pos // SUB % SUB, cell_pos % SUB
    return one_hot(token == row * width + cell * SUB + col)


def window_order():
    place = lax.broadcasted_iota(jnp.int32, (AREA, AREA), 0)
    token = lax.broadcasted_iota(jnp.int32, (AREA, AREA), 1)
    cell, row, col = place // CELL, place // SUB % SUB, place % SUB
    return one_hot(token == (cell // 2 * SUB + row) * WIN + cell % 2 * SUB + col)


def exact(permute, values):
    total = None
    for _ in range(3):
        part = values.astype(jnp.bfloat16)
        values = values - part.astype(jnp.float32)
        moved = permute(part)
        total = moved if total is None else total + moved
    return total


def head_blocks(lanes):
    row = lax.broadcasted_iota(jnp.int32, (GROUP * AREA, lanes), 0)
    col = lax.broadcasted_iota(jnp.int32, (GROUP * AREA, lanes), 1)
    return one_hot(row // AREA == col // (lanes // GROUP))


def attend(queries, key_rows, value_rows, bias, blocks, key_mask):
    lanes = blocks.shape[1]
    scale = (lanes // GROUP) ** (-0.5)
    first = lax.broadcasted_iota(jnp.int32, (1, 2 * AREA), 1) < AREA
    mixed = []
    for group in range(len(bias)):
        cut = slice(group * lanes, (group + 1) * lanes)
        keys = jnp.concatenate([key_rows[:, cut]] * GROUP, axis=0) * blocks
        values = jnp.concatenate([value_rows[:, cut]] * GROUP, axis=0) * blocks
        scores = lax.dot_general(queries[:, cut], keys, NT, preferred_element_type=jnp.float32)
        scores = scores * scale + bias[group]
        if key_mask is not None:
            scores = scores + key_mask
        weights = []
        for pair in range(GROUP // 2):
            part = scores[:, pair * 2 * AREA : (pair + 1) * 2 * AREA]
            low = jnp.max(jnp.where(first, part, -jnp.inf), axis=-1, keepdims=True)
            high = jnp.max(jnp.where(first, -jnp.inf, part), axis=-1, keepdims=True)
            weights.append(jnp.exp(part - jnp.where(first, low, high)))
        weights = jnp.concatenate(weights, axis=1).astype(jnp.bfloat16)
        both = jnp.dot(
            weights, jnp.concatenate([values, blocks], axis=1), preferred_element_type=jnp.float32
        )
        mixed.append((both[:, :lanes] / both[:, lanes:]).astype(jnp.bfloat16))
    return jnp.concatenate(mixed, axis=1)


def joint_kernel(
    tokens_ref, gain_ref, joint_ref, relative_ref,
    out_ref, bias_ref, ordered_ref, west_ref, east_ref, order_ref,
):
    cells_down, cells_across, _, model = ordered_ref.shape
    strip = order_ref.shape[0]
    order_ref[...] = strip_order(strip // SUB)
    gain = gain_ref[...].reshape(1, model)

    for step in range(cells_down // 2):
        normed = []
        for down in (2 * step, 2 * step + 1):
            ordered = jnp.dot(
                order_ref[...],
                tokens_ref[down * SUB : (down + 1) * SUB].reshape(strip, model),
                preferred_element_type=jnp.float32,
            )
            ordered_ref[down] = ordered.astype(jnp.bfloat16).reshape(cells_across, CELL, model)
            normed.append(norm_rows(ordered, gain))
        out_ref[2 * step : 2 * step + 2] = (
            jnp.dot(
                jnp.concatenate(normed, axis=0), joint_ref[...], preferred_element_type=jnp.float32
            )
            .astype(jnp.bfloat16)
            .reshape(2, cells_across, CELL, 3 * model)
        )
    place = window_order()
    turned = exact(lambda part: lax.dot_general(part, place, NT, preferred_element_type=jnp.float32),
                   relative_ref[...].reshape(-1, AREA))
    for group in range(HEADS // GROUP):
        rows = [
            turned[(group * GROUP + h) * AREA : (group * GROUP + h + 1) * AREA]
            for h in range(GROUP)
        ]
        bias_ref[group] = exact(
            lambda part: jnp.dot(place, part, preferred_element_type=jnp.float32),
            jnp.concatenate(rows, axis=1),
        )
    west_ref[...] = ordered_ref[:, 0]
    east_ref[...] = ordered_ref[:, cells_across - 1]


def inner_kernel(joint_ref, bias_ref, after_ref, out_ref):
    cells_down, cells_across, _, triple = joint_ref.shape
    model = triple // 3
    blocks = head_blocks(GROUP * model // HEADS)
    bias = [bias_ref[group] for group in range(bias_ref.shape[0])]

    for i in range(1, cells_down - 1, 2):
        for j in range(1, cells_across - 1, 2):
            rows = joint_ref[i : i + 2, j : j + 2].reshape(AREA, triple)
            mixed = attend(
                rows[:, :model], rows[:, model : 2 * model], rows[:, 2 * model :], bias, blocks, None
            )
            out_ref[i : i + 2, j : j + 2] = mixed.reshape(2, 2, CELL, model)


def lengthen_kernel(
    up_ref, down_ref, west_ref, east_ref, up_out_ref, down_out_ref, west_out_ref, east_out_ref
):
    width = up_ref.shape[1]
    order = strip_order(width)
    for source, target in ((up_ref, up_out_ref), (down_ref, down_out_ref)):
        ordered = jnp.dot(
            order, source[...].reshape(SUB * width, -1), preferred_element_type=jnp.float32
        )
        target[...] = ordered.astype(jnp.bfloat16).reshape(target.shape)
    last = up_out_ref.shape[0] - 1
    for cell, own, out in ((0, west_ref, west_out_ref), (last, east_ref, east_out_ref)):
        out[0] = up_out_ref[cell]
        out[1:-1] = own[...]
        out[out.shape[0] - 1] = down_out_ref[cell]


def lengthen(up, down, west, east):
    across = jax.ShapeDtypeStruct((up.shape[1] // SUB, CELL, up.shape[2]), up.dtype)
    out = jax.ShapeDtypeStruct((west.shape[0] + 2,) + west.shape[1:], west.dtype)
    return pl.pallas_call(
        lengthen_kernel,
        out_shape=(across, across, out, out),
        in_specs=[VMEM] * 4,
        out_specs=(VMEM,) * 4,
        compiler_params=params(8),
        name="lengthen",
    )(up, down, west, east)


def hidden_keys(down_side, down_edge, across_side, across_edge):
    cell = lax.broadcasted_iota(jnp.int32, (1, GROUP * AREA), 1) // CELL % 4
    hidden = jnp.zeros((1, GROUP * AREA), jnp.bool_)
    if down_side is not None:
        hidden = hidden | ((cell // 2 == down_side) & down_edge)
    if across_side is not None:
        hidden = hidden | ((cell % 2 == across_side) & across_edge)
    return jnp.where(hidden, BLOCKED, 0.0)


def at_end(axis, side):
    return lax.axis_index(axis) == (lax.axis_size(axis) - 1 if side else 0)


def window_bias(bias_ref, cells):
    return [
        jnp.concatenate([bias_ref[g, c * CELL : (c + 1) * CELL] for c in cells], axis=0)
        for g in range(bias_ref.shape[0])
    ]


def halo_pairs(halo, gain, joint_ref):
    model = halo.shape[-1]
    normed = norm_rows(halo.astype(jnp.float32), gain)
    return jnp.dot(normed, joint_ref[:, model:], preferred_element_type=jnp.float32).astype(
        jnp.bfloat16
    )


def ends_kernel(joint_out_ref, up_ref, down_ref, bias_ref, gain_ref, joint_ref, pairs_ref, out_ref):
    cells_down, cells_across, _, triple = joint_out_ref.shape
    model = triple // 3
    blocks = head_blocks(GROUP * model // HEADS)
    gain = gain_ref[...].reshape(1, model)
    halo = jnp.concatenate([ref[...].reshape(-1, model) for ref in (up_ref, down_ref)], axis=0)
    pairs_ref[...] = halo_pairs(halo, gain, joint_ref).reshape(2, cells_across, CELL, 2 * model)
    for side in range(2):
        row = side * (cells_down - 1)
        bias = window_bias(bias_ref, [2 - 2 * side, 3 - 2 * side])
        key_mask = hidden_keys(side, at_end("row", side), None, None)
        for j in range(1, cells_across // 2):
            cut = slice(2 * j - 1, 2 * j + 1)
            own = joint_out_ref[row, cut].reshape(2 * CELL, triple)
            other = pairs_ref[side, cut].reshape(2 * CELL, 2 * model)
            both = [own[:, model:], other] if side else [other, own[:, model:]]
            both = jnp.concatenate(both, axis=0)
            mixed = attend(own[:, :model], both[:, :model], both[:, model:], bias, blocks, key_mask)
            out_ref[side, cut] = mixed.reshape(2, CELL, model)


def sides_kernel(
    ordered_ref, joint_out_ref, inner_ref, pairs_ref, ends_ref, left_ref, right_ref,
    bias_ref, first_ref, second_ref, joint_ref, merge_ref, expand_ref, shrink_ref, lateral_ref,
    features_ref, copy_ref, mixed_ref, halo_ref, order_ref, residual_ref, normed_ref, wide_ref, hidden_ref,
):
    cells_down, cells_across, _, triple = joint_out_ref.shape
    model = triple // 3
    strip = cells_across * CELL
    order_ref[...] = strip_order(cells_across * SUB)
    blocks = head_blocks(GROUP * model // HEADS)
    halo = jnp.concatenate([ref[...].reshape(-1, model) for ref in (left_ref, right_ref)], axis=0)
    halo = halo_pairs(halo, first_ref[...].reshape(1, model), joint_ref)
    halo_ref[...] = halo.reshape(2, cells_down + 2, CELL, 2 * model)
    mixed_ref[1:-1, 1:-1] = inner_ref[1:-1, 1:-1]
    mixed_ref[0, 1:-1] = ends_ref[0, 1:-1]
    mixed_ref[cells_down - 1, 1:-1] = ends_ref[1, 1:-1]

    for across in range(2):
        col = across * (cells_across - 1)
        bias = window_bias(bias_ref, [1 - across, 3 - across])
        key_mask = hidden_keys(None, None, across, at_end("col", across))

        def keys(pieces):
            rows = []
            for own, other in pieces:
                rows += [own, other] if across else [other, own]
            return jnp.concatenate(rows, axis=0)

        for i in range(1, cells_down // 2):
            cells = [2 * i - 1, 2 * i]
            both = keys(
                [(joint_out_ref[c, col, :, model:], halo_ref[across, c + 1]) for c in cells]
            )
            queries = jnp.concatenate([joint_out_ref[c, col, :, :model] for c in cells], axis=0)
            mixed = attend(queries, both[:, :model], both[:, model:], bias, blocks, key_mask)
            for place, c in enumerate(cells):
                mixed_ref[c, col] = mixed[place * CELL : (place + 1) * CELL]
        for down in range(2):
            row = down * (cells_down - 1)
            near = (joint_out_ref[row, col, :, model:], halo_ref[across, row + 1])
            far = (pairs_ref[down, col], halo_ref[across, down * (cells_down + 1)])
            both = keys([near, far] if down else [far, near])
            mixed_ref[row, col] = attend(
                joint_out_ref[row, col, :, :model], both[:, :model], both[:, model:],
                window_bias(bias_ref, [3 - 2 * down - across]), blocks,
                hidden_keys(down, at_end("row", down), across, at_end("col", across)),
            )

    second = second_ref[...].reshape(1, model)
    rows = hidden_ref.shape[1]
    group = rows // strip
    steps = cells_down // group

    def merge(step):
        residual = residual_ref.at[step % 3]
        cells = slice(step * group, (step + 1) * group)
        residual[...] = jnp.dot(
            mixed_ref[cells].reshape(rows, model), merge_ref[...], preferred_element_type=jnp.float32
        )

    def normalise(step, part):
        residual = residual_ref.at[step % 3]
        cut = slice(part, part + PART)
        c, a = divmod(part // CELL, cells_across)
        own = ordered_ref[step * group + c, a : a + PART // CELL].reshape(PART, model)
        total = residual[cut] + own.astype(jnp.float32)
        residual[cut] = total
        normed_ref[step % 2, cut] = norm_rows(total, second)

    def expand(step, lane):
        cut = slice(lane, lane + LANES)
        wide_ref[step % 2, :, cut] = jnp.dot(
            normed_ref[step % 2], expand_ref[:, cut], preferred_element_type=jnp.float32
        )

    def activate(step, lane):
        cut = slice(lane, lane + LANES)
        for part in range(0, rows, CELL):
            here = slice(part, part + CELL)
            hidden_ref[step % 2, here, cut] = gelu_twice(wide_ref[step % 2, here, cut]).astype(
                jnp.bfloat16
            )

    def shrink(step):
        block_out = residual_ref[step % 3] + 0.5 * jnp.dot(
            hidden_ref[step % 2], shrink_ref[...], preferred_element_type=jnp.float32
        )
        features = jnp.dot(
            block_out.astype(jnp.bfloat16), lateral_ref[...], preferred_element_type=jnp.float32
        ).astype(jnp.bfloat16)
        for part in range(group):
            natural = lax.dot_general(
                order_ref[...], features[part * strip : (part + 1) * strip], TN,
                preferred_element_type=jnp.float32,
            ).astype(jnp.bfloat16)
            first = (step * group + part) * SUB
            natural = natural.reshape((SUB,) + features_ref.shape[1:])
            features_ref[first : first + SUB] = natural
            copy_ref[first : first + SUB] = natural

    lanes = range(0, wide_ref.shape[2], LANES)
    for step in range(min(2, steps)):
        merge(step)
        for part in range(0, rows, PART):
            normalise(step, part)
        if step == 0:
            for lane in lanes:
                expand(0, lane)
    for step in range(steps):
        for lane in lanes:
            if step + 1 < steps:
                expand(step + 1, lane)
            activate(step, lane)
        if step + 2 < steps:
            merge(step + 2)
        shrink(step)
        if step + 2 < steps:
            for part in range(0, rows, PART):
                normalise(step + 2, part)


LANES = 256
PART = 64


def params(mebibytes):
    return pltpu.CompilerParams(vmem_limit_bytes=mebibytes * 2**20)


def cells_of(count_down, count_across, channels, dtype=jnp.bfloat16):
    return jax.ShapeDtypeStruct((count_down, count_across, CELL, channels), dtype)


def end_kernel(tokens_ref, first_ref, last_ref):
    first_ref[...] = tokens_ref[:SUB]
    last_ref[...] = tokens_ref[tokens_ref.shape[0] - SUB :]


def end_rows(tokens):
    out = jax.ShapeDtypeStruct((SUB,) + tokens.shape[1:], tokens.dtype)
    return pl.pallas_call(
        end_kernel,
        out_shape=(out, out),
        in_specs=[VMEM],
        out_specs=(VMEM, VMEM),
        compiler_params=params(4),
        cost_estimate=cost(tokens.shape[0] * tokens.shape[1], 2**20),
        name="end_rows",
    )(tokens)


def joint_rows(tokens, gain, weight, relative):
    tile_rows, tile_cols, model = tokens.shape
    down, across = tile_rows // SUB, tile_cols // SUB
    lone = lambda n: jax.ShapeDtypeStruct((n, CELL, model), jnp.bfloat16)
    return pl.pallas_call(
        joint_kernel,
        out_shape=(
            cells_of(down, across, weight.shape[1]),
            jax.ShapeDtypeStruct((HEADS // GROUP, AREA, GROUP * AREA), jnp.float32),
            cells_of(down, across, model),
            lone(down), lone(down),
        ),
        in_specs=[VMEM] * 4,
        out_specs=(VMEM,) * 5,
        scratch_shapes=[
            pltpu.VMEM((SUB * tile_cols, SUB * tile_cols), jnp.bfloat16),
        ],
        compiler_params=params(20),
        cost_estimate=cost(tokens.shape[0] * tile_cols, model * weight.shape[1]),
        name="joint_rows",
    )(tokens, gain, weight, relative)


def cost(rows, weights):
    return pl.CostEstimate(flops=4 * rows * weights, bytes_accessed=4 * 2**20, transcendentals=0)


def inner_windows(joint, bias, after):
    return pl.pallas_call(
        inner_kernel,
        out_shape=jax.ShapeDtypeStruct(joint.shape[:3] + (joint.shape[3] // 3,), jnp.bfloat16),
        in_specs=[VMEM, VMEM, pl.BlockSpec(memory_space=pl.ANY)],
        out_specs=VMEM,
        compiler_params=params(20),
        cost_estimate=cost(joint.shape[0] * joint.shape[1] * CELL, 2**19),
        name="inner_windows",
    )(joint, bias, after)


def end_windows(joint, up, down, bias, gain, weight):
    _, across, _, triple = joint.shape
    return pl.pallas_call(
        ends_kernel,
        out_shape=(cells_of(2, across, triple * 2 // 3), cells_of(2, across, triple // 3)),
        in_specs=[VMEM] * 6,
        out_specs=(VMEM, VMEM),
        compiler_params=params(20),
        cost_estimate=cost(joint.shape[0] * joint.shape[1] * CELL, 2**19),
        name="end_windows",
    )(joint, up, down, bias, gain, weight)


def side_windows(ordered, joint, inner, pairs, ends, left, right, bias, gains, weights):
    down, across, _, triple = joint.shape
    model = triple // 3
    strip = CELL * across
    rows = 4 * strip
    wide = weights[2].shape[1]
    tile = jax.ShapeDtypeStruct((down * SUB, across * SUB, weights[-1].shape[1]), jnp.bfloat16)
    return pl.pallas_call(
        sides_kernel,
        out_shape=(tile, tile),
        in_specs=[VMEM] * 15,
        out_specs=(VMEM, VMEM),
        scratch_shapes=[
            pltpu.VMEM((down, across, CELL, model), jnp.bfloat16),
            pltpu.VMEM((2, down + 2, CELL, 2 * model), jnp.bfloat16),
            pltpu.VMEM((strip, strip), jnp.bfloat16),
            pltpu.VMEM((3, rows, model), jnp.float32),
            pltpu.VMEM((2, rows, model), jnp.bfloat16),
            pltpu.VMEM((2, rows, wide), jnp.float32),
            pltpu.VMEM((2, rows, wide), jnp.bfloat16),
        ],
        compiler_params=params(34),
        name="side_windows",
    )(ordered, joint, inner, pairs, ends, left, right, bias, *gains, *weights)


BOX_OWN = 8


def shift(x, axis, step):
    size = lax.axis_size(axis)
    pairs = [(i, i + step) for i in range(size) if 0 <= i + step < size]
    return lax.ppermute(x, axis, pairs)


def shards(
    tokens, first_gain, second_gain, joint_weight, merge_weight, expand_weight, shrink_weight,
    relative_bias, lateral_weight, conv_weight, mask_weight, box_geometry, box_counts, box_owner,
    soft_target,
):
    tile_rows, tile_cols, model = tokens.shape
    first, last = end_rows(tokens)
    up = shift(last, "row", 1)
    down = shift(first, "row", -1)
    joint, bias, ordered, west, east = joint_rows(
        tokens, first_gain, joint_weight, relative_bias
    )
    up, down, west, east = lengthen(up, down, west, east)
    left = shift(east, "col", 1)
    right = shift(west, "col", -1)
    inner = inner_windows(joint, bias, west)
    pairs, ends = end_windows(joint, up, down, bias, first_gain, joint_weight)
    features, features_here = side_windows(
        ordered, joint, inner, pairs, ends, left, right, bias, (first_gain, second_gain),
        (joint_weight, merge_weight, expand_weight, shrink_weight, lateral_weight),
    )
    rows_size = lax.axis_size("row")
    geometry = box_geometry.transpose(0, 1, 3, 2)
    send, slope = mask_forward(
        features_here, geometry, box_counts, box_owner, conv_weight, mask_weight
    )
    both = join_pair(send, lax.ppermute(send, "row", [(i, i ^ 1) for i in range(rows_size)]))
    blocks = [both]
    for back in range(2, rows_size, 2):
        blocks.append(
            lax.ppermute(both, "row", [(i, (i + back) % rows_size) for i in range(rows_size)])
        )
    feature_grad, done = mask_backward(
        send, soft_target, slope, geometry, box_counts, conv_weight, mask_weight,
        (tile_rows, tile_cols),
    )
    return features, feature_grad, collect(blocks, done, BOX_OWN, CROP * CROP)


def solution(mesh):
    tile = P("row", "col", None)
    placed = (tile,) + (P(),) * 10 + (
        P("row", "col", None, None), P("row", "col"), tile, P("row", "col", None, None),
    )
    return jax.shard_map(
        shards,
        mesh=mesh,
        in_specs=placed,
        out_specs=(tile, tile, P("row", "col", None, None)),
        check_vma=False,
    )
```
